768 devices in a mesh: slab: 64 (over y, x, core), sub: 12 (over z).
Axes of the slice: x: 4, y: 8, z: 12, core: 2. Of those that a mesh axis runs over, the one named last changes fastest.
Arguments:
- fine_old: float32 [4, 192, 98304], P(None, 'sub', 'slab'), may hold values from -1 to 1
- coarse: float32 [4, 96, 98304], P(None, 'sub', 'slab'), may hold values from -1 to 1
- box_pos: int32 [1536], replicated, may hold values from 0 to 3071, as said below
- old_owner: int32 [1536], replicated, may hold values from 0 to 63, as said below
- new_counts: int32 [64], replicated, may hold values from 1 to 48, 1536 in all
Outputs:
- fine_new: float32 [4, 192, 196608], P(None, 'sub', 'slab')
The draws below stay inside these ranges and needn't reach their ends.
Inputs may be any that keep to these rules, and one draw needn't show every extreme that they name: `box_pos`: strictly increasing; the first box sits at 0 and the last at 3071. `old_owner`: any 64 consecutive boxes of the list have different old owners, so each old owner holds exactly 24 boxes and at most 1 boxes pass from one old owner to one new owner, a bound that is reached. `new_counts`: sums to 1536; some owner receives exactly 48 boxes.
All inputs are finite; a program needn't handle non-finite values.
Results may differ from the reference program's by a relative error of at most 0.00002.
Values sent between devices are 32-bit elements; how exact they have to be, the bound alone decides.
No kernel may reach another device: no remote copies, remote signals or barrier semaphores. Data moves between devices by JAX's collectives and lax.ppermute only.
A program may use at most 128 MiB of HBM per device.

```python
import math
import jax
import jax.numpy as jnp
import numpy as np

BX = 64
BOX_DEV = 24
MOST = 48
NBOX = 1536
PPD = 48
NPOS = 3072
NY = 192
N_SLAB = 64


def draw_box_pos(key, part):
    key = jax.random.fold_in(key, 11)
    inner_ids = jax.random.permutation(key, NPOS - 2) + 1
    chosen = jnp.sort(inner_ids[:NBOX - 2]).astype(jnp.int32)
    return jnp.concatenate([jnp.zeros((1,), jnp.int32), chosen, jnp.full((1,), NPOS - 1, jnp.int32)])


def draw_old_owner(key, part):
    key = jax.random.fold_in(key, 23)
    key_order, key_shift = jax.random.split(key)
    order_ids = jax.random.permutation(key_order, N_SLAB).astype(jnp.int32)
    offset_draw = jax.random.randint(key_shift, (), 0, N_SLAB)
    return jnp.take(order_ids, (jnp.arange(NBOX) + offset_draw) % N_SLAB).astype(jnp.int32)


def levels(own_key, extent, pieces, smallest, top_value):
    def one(dim, parts):
        steps = jax.random.uniform(jax.random.fold_in(jax.random.fold_in(own_key, 6), dim), (parts,), jnp.float32, smallest / len(pieces), top_value / len(pieces))
        return jnp.repeat(jnp.exp(steps), extent[dim] // parts).reshape((-1,) + (1,) * (len(extent) - dim - 1))

    level = one(*pieces[0])
    for cut in pieces[1:]:
        level = level * one(*cut)
    return level


def length_profile(number_of, total, limit, lean):
    loads = [(1 << 20) // math.isqrt(rank ** lean) + 1 for rank in range(2, number_of + 1)]
    surplus, counts = total - limit - (number_of - 1), [1] * (number_of - 1)
    while surplus > 0:
        free = [i for i in range(number_of - 1) if counts[i] < limit]
        mass, remaining = sum([loads[i] for i in free]), surplus
        for i in free:
            addition = min(limit - counts[i], max(1, remaining * loads[i] // mass), surplus)
            counts[i] = counts[i] + addition
            surplus = surplus - addition
    return np.array([limit] + counts)


def uneven_parts(rng, count, total, limit, skew):
    if count == 2:
        one = jax.random.randint(rng, (), max(1, total - limit), min(limit, total - 1) + 1)
        return jnp.stack([one, total - one])
    sizes = jnp.asarray(length_profile(count, total, limit, skew), jnp.int32)
    pairs = (count - 1) // 2
    donor, taker = sizes[1:1 + 2 * pairs:2], sizes[2:2 + 2 * pairs:2]
    slack = jnp.minimum(donor - 1, limit - taker)
    passed = jax.random.randint(jax.random.fold_in(rng, 1), (pairs,), 0, 1 << 20) % (slack + 1)
    sizes = sizes.at[1:1 + 2 * pairs:2].set(donor - passed).at[2:2 + 2 * pairs:2].set(taker + passed)
    return sizes[jax.random.permutation(jax.random.fold_in(rng, 2), count)]


def setup_inputs(seed: int = 0) -> dict:
    keys = jax.random.split(jax.random.key(seed), 6)
    fine_old = jnp.clip(jax.random.uniform(keys[0], (4, NY, NBOX * BX), jnp.float32, -1.0, 1.0) * levels(keys[0], (4, NY, NBOX * BX), ((1, 12), (2, 64)), -0.4, 0.0), -1.0, 1.0)
    coarse = jnp.clip(jax.random.uniform(keys[1], (4, NY // 2, NPOS * BX // 2), jnp.float32, -1.0, 1.0) * levels(keys[1], (4, NY // 2, NPOS * BX // 2), ((1, 12), (2, 64)), -0.4, 0.0), -1.0, 1.0)
    box_pos = draw_box_pos(jax.random.fold_in(keys[5], 71), 0)
    old_owner = draw_old_owner(jax.random.fold_in(keys[5], 71), 0)
    new_counts = uneven_parts(keys[4], N_SLAB, NBOX, MOST, 2).astype(jnp.int32)
    return {"fine_old": fine_old, "coarse": coarse, "box_pos": box_pos, "old_owner": old_owner, "new_counts": new_counts}


ANISOTROPY = 0.3
TIME_STEP = 0.1
COUPLING = 1.5
SOLUTE_ONE = 0.6
SOLUTE_TWO = -0.4
DIFF_HEAT = 2.0
DIFF_ONE = 0.5
DIFF_TWO = 0.25
LATENT = 0.5
REJECT_ONE = 0.5
REJECT_TWO = -0.3


def advance(center, west_cells, east_cells, south_cells, north_cells):
    laplace = west_cells + east_cells + south_cells + north_cells - 4.0 * center
    phase = center[0]
    grad_x = 0.5 * (east_cells[0] - west_cells[0])
    grad_y = 0.5 * (north_cells[0] - south_cells[0])
    sq_x = grad_x * grad_x
    sq_y = grad_y * grad_y
    spread_sum = sq_x + sq_y + 1.0
    anisotropy = 1.0 + ANISOTROPY * (sq_x * sq_x - 6.0 * sq_x * sq_y + sq_y * sq_y) / (spread_sum * spread_sum)
    couple = center[1] + SOLUTE_ONE * center[2] + SOLUTE_TWO * center[3]
    wall_term = 1.0 - phase * phase
    phase_step = TIME_STEP * (anisotropy * anisotropy * laplace[0] + phase - phase * phase * phase - COUPLING * wall_term * wall_term * couple)
    heat_new = center[1] + TIME_STEP * DIFF_HEAT * laplace[1] + LATENT * phase_step
    first_solute = center[2] + TIME_STEP * DIFF_ONE * laplace[2] + REJECT_ONE * center[2] * phase_step
    second_solute = center[3] + TIME_STEP * DIFF_TWO * laplace[3] + REJECT_TWO * center[3] * phase_step
    return jnp.stack([phase + phase_step, heat_new, first_solute, second_solute])


def stored_block(position, per_device, device_count):
    total = per_device * device_count
    wrapped = (position % total).astype(jnp.int32)
    block = wrapped // per_device
    target = jnp.where(block % 2 == 1, block - 1, (block + device_count // 2 + 1) % device_count)
    return (target * per_device + wrapped % per_device).astype(jnp.int32)


def reference(fine_old, coarse, box_pos, old_owner, new_counts):
    owners = jnp.arange(N_SLAB, dtype=jnp.int32)
    onehot = (old_owner[:, None] == owners[None, :]).astype(jnp.int32)
    earlier = (jnp.cumsum(onehot, axis=0) - onehot).astype(jnp.int32)
    old_slot = jnp.sum(earlier * onehot, axis=1).astype(jnp.int32)
    cell_ids = jnp.arange(BX, dtype=jnp.int32)
    base_col = ((old_owner * BOX_DEV + old_slot) * BX).astype(jnp.int32)
    regridded = jnp.take(fine_old, (base_col[:, None] + cell_ids[None, :]).reshape(-1).astype(jnp.int32), axis=2)
    half_width = BX // 2
    first_cols = regridded[:, :, 0::BX]
    last_cols = regridded[:, :, BX - 1::BX]
    doubled = jnp.repeat(coarse, 2, axis=1)
    left_block = stored_block(box_pos - 1, PPD, N_SLAB)
    right_block = stored_block(box_pos + 1, PPD, N_SLAB)
    left_coarse = jnp.take(doubled, (left_block * half_width + half_width - 1).astype(jnp.int32), axis=2)
    right_coarse = jnp.take(doubled, (right_block * half_width).astype(jnp.int32), axis=2)
    prev_pos = jnp.concatenate([jnp.full((1,), -5, jnp.int32), box_pos[:-1]])
    next_pos = jnp.concatenate([box_pos[1:], jnp.full((1,), -5, jnp.int32)])
    fine_left = prev_pos == box_pos - 1
    fine_right = next_pos == box_pos + 1
    zero_col = jnp.zeros((4, regridded.shape[1], 1), regridded.dtype)
    prev_last = jnp.concatenate([zero_col, last_cols[:, :, :-1]], axis=2)
    next_first = jnp.concatenate([first_cols[:, :, 1:], zero_col], axis=2)
    left_val = jnp.where(fine_left, prev_last, jnp.where(box_pos > 0, left_coarse, first_cols))
    right_val = jnp.where(fine_right, next_first, jnp.where(box_pos < NPOS - 1, right_coarse, last_cols))
    col_ids = jnp.arange(NBOX * BX, dtype=jnp.int32) % BX
    shifted_west = jnp.concatenate([zero_col, regridded[:, :, :-1]], axis=2)
    shifted_east = jnp.concatenate([regridded[:, :, 1:], zero_col], axis=2)
    west_cells = jnp.where(col_ids == 0, jnp.repeat(left_val, BX, axis=2), shifted_west)
    east_cells = jnp.where(col_ids == BX - 1, jnp.repeat(right_val, BX, axis=2), shifted_east)
    south_cells = jnp.concatenate([regridded[:, :1], regridded[:, :-1]], axis=1)
    north_cells = jnp.concatenate([regridded[:, 1:], regridded[:, -1:]], axis=1)
    stepped = advance(regridded, west_cells, east_cells, south_cells, north_cells)
    starts = (jnp.cumsum(new_counts) - new_counts).astype(jnp.int32)
    out_cols = jnp.arange(N_SLAB * MOST * BX, dtype=jnp.int32)
    owner_of = out_cols // (MOST * BX)
    slot_of = (out_cols // BX) % MOST
    live_mask = slot_of < jnp.take(new_counts, owner_of)
    source_col = jnp.where(live_mask, (jnp.take(starts, owner_of) + slot_of) * BX + out_cols % BX, 0).astype(jnp.int32)
    return jnp.where(live_mask, jnp.take(stepped, source_col, axis=2), 0.0)
```

```python
import jax
import jax.numpy as jnp
from jax import lax
from jax.experimental import pallas as pl
from jax.experimental.pallas import tpu as pltpu
from jax.sharding import PartitionSpec as P

BX = 64
BOX_DEV = 24
MOST = 48
NBOX = 1536
PPD = 48
NPOS = 3072
SLABS = 64
TILES = MOST // 2
FIELDS = 4
ROWS = 16
BOX_ROWS = FIELDS * 8
MSG_ROWS = BOX_ROWS + 8

ANISOTROPY = 0.3
TIME_STEP = 0.1
COUPLING = 1.5
SOLUTE_ONE = 0.6
SOLUTE_TWO = -0.4
DIFF_HEAT = 2.0
DIFF_ONE = 0.5
DIFF_TWO = 0.25
LATENT = 0.5
REJECT_ONE = 0.5
REJECT_TWO = -0.3

SRC, FINE_L, FINE_R, OWN_L, OWN_R, SIB_L, SIB_R, MISC = range(8)


def lanes(shape=(8, 128)):
    return lax.broadcasted_iota(jnp.int32, shape, 1)


def pick(cond, a, b):
    return lax.select(cond, jnp.int32(a), jnp.int32(b))


def pack_kernel(owner, counts, pos, fine, coarse, out, starts, packed):
    me = lax.axis_index("slab")
    lane = lanes()
    low = lane < 64

    for tile in range(BOX_DEV // 2):
        for f in range(FIELDS):
            top = fine[f, 0:8, tile * 128 : tile * 128 + 128]
            bottom = fine[f, 8:16, tile * 128 : tile * 128 + 128]
            packed[2 * tile, f * 8 : f * 8 + 8] = jnp.where(low, top, pltpu.roll(bottom, 64, 1))
            packed[2 * tile + 1, f * 8 : f * 8 + 8] = jnp.where(low, pltpu.roll(top, 64, 1), bottom)

    inner = lane & 31
    group = lane >> 5
    even = (lane & 1) == 0
    firsts = [jnp.zeros((8, 128), jnp.float32) for _ in range(2)]
    lasts = [jnp.zeros((8, 128), jnp.float32) for _ in range(2)]
    for f in range(FIELDS):
        first = jnp.zeros((8, 128), jnp.float32)
        last = jnp.zeros((8, 128), jnp.float32)
        for tile in range(12):
            x = coarse[f, :, tile * 128 : tile * 128 + 128]
            if tile:
                x = pltpu.roll(x, 2 * tile, 1)
            first = jnp.where(inner == 2 * tile, x, first)
            last = jnp.where(inner == (31 + 2 * tile) % 32, x, last)

        def moved(x, shift):
            shift = (f * 32 + shift) % 128
            return pltpu.roll(x, shift, 1) if shift else x

        here = group == f
        first_even = jnp.where(even, moved(first, 0), moved(first, -63))
        first_odd = jnp.where(even, moved(first, -32), moved(first, -95))
        last_even = jnp.where(even, moved(last, -125), moved(last, -62))
        last_odd = jnp.where(even, moved(last, -31), moved(last, -94))
        firsts = [jnp.where(here, a, b) for a, b in zip((first_even, first_odd), firsts)]
        lasts = [jnp.where(here, a, b) for a, b in zip((last_even, last_odd), lasts)]

    block = pick((me & 1) == 0, me + 1, (me + 31) & 63)
    base = block * PPD
    first_box = jnp.int32(0)
    for step in (1024, 512, 256, 128, 64, 32, 16, 8, 4, 2, 1):
        trial = first_box + step
        value = pos[jnp.minimum(trial, NBOX) - 1]
        first_box = pick((trial <= NBOX) & (value < base), trial, first_box)

    def mark(i, words):
        word0, word1 = words
        k = first_box + i
        at = pos[jnp.minimum(k, NBOX - 1)] - base
        good = (k < NBOX) & (at <= PPD)
        bit = jnp.left_shift(jnp.int32(1), at & 31)
        word0 = word0 | pick(good & (at < 32), bit, 0)
        word1 = word1 | pick(good & (at >= 32), bit, 0)
        return word0, word1

    word0, word1 = lax.fori_loop(0, PPD + 1, mark, (jnp.int32(0), jnp.int32(0)), unroll=7)
    for core in range(2):
        joint = 2 * inner + core
        words = jnp.where(joint < 32, word0, word1)
        fine_here = (lax.shift_right_logical(words, joint & 31) & 1) == 1
        edge = jnp.where(fine_here, lasts[core], firsts[core])
        for b in range(core, SLABS, 2):
            out[b, BOX_ROWS:MSG_ROWS] = edge

    def find(i, r):
        return r + pick(owner[i] == me, i, 0)

    residue = lax.fori_loop(0, SLABS, find, jnp.int32(0), unroll=16)

    def fill(b, start):
        starts[b] = start
        k = start - 1 + ((residue - (start - 1)) & 63)
        slot = jnp.clip(k >> 6, 0, BOX_DEV - 1)
        out[b, 0:BOX_ROWS] = packed[slot]
        return start + counts[b]

    lax.fori_loop(0, SLABS, fill, jnp.int32(0), unroll=8)


def plan_kernel(owner, counts, pos, starts, plan):
    me = lax.axis_index("slab")
    mine = me & 1
    start = starts[me]
    plan[MISC * 64] = start
    plan[MISC * 64 + 1] = counts[me]

    def source(i, carry):
        plan[SRC * 64 + i] = owner[(start + i - 2) & 63]
        return carry

    lax.fori_loop(0, MOST + 4, source, 0, unroll=4)

    def code(at, joint, wanted):
        block = (at * 43691) >> 21
        joint = joint + at - block * PPD
        device = pick((block & 1) == 1, block - 1, (block + 33) & 63)
        keep = wanted & ((joint & 1) == mine)
        return pick(keep, device * 32 + (joint >> 1), -1)

    def ghosts(first, left_row, right_row, flags):
        def one(s, carry):
            k = jnp.minimum(first + s, NBOX - 1)
            at = pos[k]
            before = pos[jnp.maximum(k - 1, 0)]
            after = pos[jnp.minimum(k + 1, NBOX - 1)]
            fine_l = before == at - 1
            fine_r = after == at + 1
            if flags:
                plan[FINE_L * 64 + s] = pick(fine_l, 1, 0)
                plan[FINE_R * 64 + s] = pick(fine_r, 1, 0)
            has_l = jnp.logical_not(fine_l) & (k > 0)
            has_r = jnp.logical_not(fine_r) & (k < NBOX - 1)
            plan[left_row * 64 + s] = code(jnp.maximum(at - 1, 0), 1, has_l)
            plan[right_row * 64 + s] = code(jnp.minimum(at + 1, NPOS - 1), 0, has_r)
            return carry

        lax.fori_loop(0, MOST, one, 0, unroll=2)

    ghosts(start, OWN_L, OWN_R, True)
    ghosts(starts[me ^ 1], SIB_L, SIB_R, False)


def gather_edges(plan, inc, rows):
    lane = lanes()
    inner = lane & 31

    def one(m, carry):
        here = inner == m
        out = []
        for n, (row, half) in enumerate((row, half) for row in rows for half in range(2)):
            code = plan[row * 64 + half * TILES + m]
            x = inc[jnp.maximum(code, 0) >> 5, BOX_ROWS:MSG_ROWS]
            x = pltpu.roll(x, (m - (code & 31)) & 127, 1)
            out.append(jnp.where(here & (code >= 0), x, carry[n]))
        return tuple(out)

    zero = jnp.zeros((8, 128), jnp.float32)
    return lax.fori_loop(0, TILES, one, (zero,) * (2 * len(rows)), unroll=4)


def edge_kernel(plan, inc, low_rows, high_rows, sibling):
    low = lanes((1, 128)) < 64

    def one(t, carry):
        a = plan[SRC * 64 + 2 + 2 * t]
        b = plan[SRC * 64 + 3 + 2 * t]
        for f in range(FIELDS):
            row = f * 8
            low_rows[t, f : f + 1] = jnp.where(
                low, inc[a, row : row + 1], pltpu.roll(inc[b, row : row + 1], 64, 1)
            )
            row = f * 8 + 7
            high_rows[t, f : f + 1] = jnp.where(
                low, pltpu.roll(inc[a, row : row + 1], 64, 1), inc[b, row : row + 1]
            )
        return carry

    lax.fori_loop(0, TILES, one, 0, unroll=4)
    for n, edges in enumerate(gather_edges(plan, inc, (SIB_L, SIB_R))):
        sibling[n] = edges


def advance(center, west_cells, east_cells, south_cells, north_cells):
    laplace = [
        w + e + s + n - 4.0 * c
        for c, w, e, s, n in zip(center, west_cells, east_cells, south_cells, north_cells)
    ]
    phase = center[0]
    grad_x = 0.5 * (east_cells[0] - west_cells[0])
    grad_y = 0.5 * (north_cells[0] - south_cells[0])
    sq_x = grad_x * grad_x
    sq_y = grad_y * grad_y
    spread_sum = sq_x + sq_y + 1.0
    anisotropy = 1.0 + ANISOTROPY * (sq_x * sq_x - 6.0 * sq_x * sq_y + sq_y * sq_y) / (
        spread_sum * spread_sum
    )
    couple = center[1] + SOLUTE_ONE * center[2] + SOLUTE_TWO * center[3]
    wall_term = 1.0 - phase * phase
    phase_step = TIME_STEP * (
        anisotropy * anisotropy * laplace[0]
        + phase
        - phase * phase * phase
        - COUPLING * wall_term * wall_term * couple
    )
    return (
        phase + phase_step,
        center[1] + TIME_STEP * DIFF_HEAT * laplace[1] + LATENT * phase_step,
        center[2] + TIME_STEP * DIFF_ONE * laplace[2] + REJECT_ONE * center[2] * phase_step,
        center[3] + TIME_STEP * DIFF_TWO * laplace[3] + REJECT_TWO * center[3] * phase_step,
    )


def step_kernel(plan, inc, from_below, from_above, sibling, out, cen, edges):
    sub = lax.axis_index("sub")
    lane = lanes()
    low = lane < 64
    row8 = lax.broadcasted_iota(jnp.int32, (8, 128), 0)
    start = plan[MISC * 64]
    count = plan[MISC * 64 + 1]

    def unpack(t, carry):
        a = plan[SRC * 64 + 2 * t]
        b = plan[SRC * 64 + 1 + 2 * t]
        for f in range(FIELDS):
            x = inc[a, f * 8 : f * 8 + 8]
            y = inc[b, f * 8 : f * 8 + 8]
            cen[t, f, 0:8] = jnp.where(low, x, pltpu.roll(y, 64, 1))
            cen[t, f, 8:16] = jnp.where(low, pltpu.roll(x, 64, 1), y)
        return carry

    lax.fori_loop(0, TILES + 2, unpack, 0, unroll=2)

    own = gather_edges(plan, inc, (OWN_L, OWN_R))
    for n in range(4):
        whole = own[n] + sibling[n]
        edges[n, 0:8] = jnp.take_along_axis(whole, row8 >> 1, axis=0)
        edges[n, 8:16] = jnp.take_along_axis(whole, 4 + (row8 >> 1), axis=0)

    lane = lanes((ROWS, 128))
    row = lax.broadcasted_iota(jnp.int32, (ROWS, 128), 0)
    at_first = (lane & 31) == 0
    outer = (lane == 0) | (lane == 127)
    at_bottom = sub == 0
    at_top = sub == lax.axis_size("sub") - 1

    def one(t, carry):
        s = 2 * t
        half = pick(s >= TILES, 1, 0)
        m = s - half * TILES
        left = edges[half]
        right = edges[2 + half]
        ends = jnp.where(at_first, pltpu.roll(left, (128 - m) & 127, 1), pltpu.roll(right, 126 - m, 1))
        middle = jnp.where(at_first, pltpu.roll(left, 127 - m, 1), pltpu.roll(right, 127 - m, 1))
        fl0, fl1 = plan[FINE_L * 64 + s] == 1, plan[FINE_L * 64 + s + 1] == 1
        fr0, fr1 = plan[FINE_R * 64 + s] == 1, plan[FINE_R * 64 + s + 1] == 1
        k = start + s
        ghost_w = ((lane == 0) & jnp.logical_not(fl0)) | ((lane == 64) & jnp.logical_not(fl1))
        ghost_e = ((lane == 63) & jnp.logical_not(fr0)) | ((lane == 127) & jnp.logical_not(fr1))
        border = (
            ((lane == 0) & (k == 0))
            | ((lane == 63) & (k == NBOX - 1))
            | ((lane == 127) & (k + 1 == NBOX - 1))
        )
        live = jnp.where(lane < 64, s, s + 1) < count
        center, west, east, south, north = [], [], [], [], []
        for f in range(FIELDS):
            c = cen[t + 1, f]
            w = jnp.where(lane == 0, pltpu.roll(cen[t, f], 1, 1), pltpu.roll(c, 1, 1))
            e = jnp.where(lane == 127, pltpu.roll(cen[t + 2, f], 127, 1), pltpu.roll(c, 127, 1))
            g = jnp.where(
                outer,
                pltpu.roll(ends, 128 - 32 * f, 1) if f else ends,
                pltpu.roll(middle, (192 - 32 * f) % 128, 1) if f != 2 else middle,
            )
            g = jnp.where(border, c, g)
            below = jnp.where(at_bottom, c[0:1], from_below[t, f : f + 1])
            above = jnp.where(at_top, c[15:16], from_above[t, f : f + 1])
            center.append(c)
            west.append(jnp.where(ghost_w, g, w))
            east.append(jnp.where(ghost_e, g, e))
            south.append(jnp.where(row == 0, below, pltpu.roll(c, 1, 0)))
            north.append(jnp.where(row == ROWS - 1, above, pltpu.roll(c, ROWS - 1, 0)))
        stepped = advance(center, west, east, south, north)
        at = pl.ds(pl.multiple_of(t * 128, 128), 128)
        for f in range(FIELDS):
            out[f, :, at] = jnp.where(live, stepped[f], 0.0)
        return carry

    lax.fori_loop(0, TILES, one, 0)


SMEM = pl.BlockSpec(memory_space=pltpu.SMEM)
VMEM = pl.BlockSpec(memory_space=pltpu.VMEM)
PARAMS = pltpu.CompilerParams(vmem_limit_bytes=32 * 1024 * 1024)


def f32(*shape):
    return jax.ShapeDtypeStruct(shape, jnp.float32)


def i32(*shape):
    return jax.ShapeDtypeStruct(shape, jnp.int32)


def body(fine_old, coarse, box_pos, old_owner, new_counts):
    outgoing, starts = pl.pallas_call(
        pack_kernel,
        name="pack",
        out_shape=(f32(SLABS, MSG_ROWS, 128), i32(SLABS)),
        in_specs=[SMEM, SMEM, SMEM, VMEM, VMEM],
        out_specs=(VMEM, SMEM),
        scratch_shapes=[pltpu.VMEM((BOX_DEV, BOX_ROWS, 128), jnp.float32)],
        compiler_params=PARAMS,
    )(old_owner, new_counts, box_pos, fine_old, coarse)
    incoming = lax.all_to_all(outgoing, "slab", 0, 0, tiled=True)
    plan = pl.pallas_call(
        plan_kernel,
        name="plan",
        out_shape=i32(8 * 64),
        in_specs=[SMEM] * 4,
        out_specs=SMEM,
        compiler_params=PARAMS,
    )(old_owner, new_counts, box_pos, starts)
    low_rows, high_rows, sibling = pl.pallas_call(
        edge_kernel,
        name="edges",
        out_shape=(f32(TILES, FIELDS, 128), f32(TILES, FIELDS, 128), f32(4, 8, 128)),
        in_specs=[SMEM, VMEM],
        out_specs=(VMEM, VMEM, VMEM),
        compiler_params=PARAMS,
    )(plan, incoming)
    count = lax.axis_size("sub")
    up = [(i, i + 1) for i in range(count - 1)]
    sibling = lax.ppermute(sibling, "slab", [(i, i ^ 1) for i in range(SLABS)])
    from_below = lax.ppermute(high_rows, "sub", up)
    from_above = lax.ppermute(low_rows, "sub", [(b, a) for a, b in up])
    return pl.pallas_call(
        step_kernel,
        name="step",
        out_shape=f32(FIELDS, ROWS, MOST * BX),
        in_specs=[SMEM] + [VMEM] * 4,
        out_specs=VMEM,
        scratch_shapes=[
            pltpu.VMEM((TILES + 2, FIELDS, ROWS, 128), jnp.float32),
            pltpu.VMEM((4, ROWS, 128), jnp.float32),
        ],
        compiler_params=PARAMS,
    )(plan, incoming, from_below, from_above, sibling)


def solution(mesh):
    placed = (P(None, "sub", "slab"), P(None, "sub", "slab"), P(), P(), P())
    return jax.shard_map(
        body, mesh=mesh, in_specs=placed, out_specs=P(None, "sub", "slab"), check_vma=False
    )
```

```python
import jax
import jax.numpy as jnp
from jax import lax
from jax.experimental import pallas as pl
from jax.experimental.pallas import tpu as pltpu
from jax.sharding import PartitionSpec as P

BX = 64
BOX_DEV = 24
MOST = 48
NBOX = 1536
PPD = 48
NPOS = 3072
SLABS = 64
TILES = MOST // 2
QUARTER = MOST // 4
GU = 12
UU = 24
FIELDS = 4
ROWS = 16
BOX_ROWS = FIELDS * 8
MSG_ROWS = BOX_ROWS + 8

ANISOTROPY = 0.3
TIME_STEP = 0.1
COUPLING = 1.5
SOLUTE_ONE = 0.6
SOLUTE_TWO = -0.4
DIFF_HEAT = 2.0
DIFF_ONE = 0.5
DIFF_TWO = 0.25
LATENT = 0.5
REJECT_ONE = 0.5
REJECT_TWO = -0.3

SRC, FINE_L, FINE_R, OWN_L, OWN_R, SIB_L, SIB_R, MISC = range(8)


def lanes(shape=(8, 128)):
    return lax.broadcasted_iota(jnp.int32, shape, 1)


def pick(cond, a, b):
    return lax.select(cond, jnp.int32(a), jnp.int32(b))


def pack_kernel(
    owner_in, counts_in, pos_in, fine_in, coarse_in, out, starts, owner, counts, pos, fine, coarse, packed, sems
):
    copies = [
        pltpu.make_async_copy(a, b, sems.at[n])
        for n, (a, b) in enumerate(
            ((pos_in, pos), (owner_in, owner), (counts_in, counts), (fine_in, fine), (coarse_in, coarse))
        )
    ]
    for copy in copies:
        copy.start()
    for copy in copies:
        copy.wait()
    me = lax.axis_index("slab")
    lane = lanes()
    low = lane < 64

    for tile in range(BOX_DEV // 2):
        for f in range(FIELDS):
            top = fine[f, 0:8, tile * 128 : tile * 128 + 128]
            bottom = fine[f, 8:16, tile * 128 : tile * 128 + 128]
            packed[2 * tile, f * 8 : f * 8 + 8] = jnp.where(low, top, pltpu.roll(bottom, 64, 1))
            packed[2 * tile + 1, f * 8 : f * 8 + 8] = jnp.where(low, pltpu.roll(top, 64, 1), bottom)

    inner = lane & 31
    group = lane >> 5
    even = (lane & 1) == 0
    firsts = [jnp.zeros((8, 128), jnp.float32) for _ in range(2)]
    lasts = [jnp.zeros((8, 128), jnp.float32) for _ in range(2)]
    for f in range(FIELDS):
        first = jnp.zeros((8, 128), jnp.float32)
        last = jnp.zeros((8, 128), jnp.float32)
        for tile in range(12):
            x = coarse[f, :, tile * 128 : tile * 128 + 128]
            if tile:
                x = pltpu.roll(x, 2 * tile, 1)
            first = jnp.where(inner == 2 * tile, x, first)
            last = jnp.where(inner == (31 + 2 * tile) % 32, x, last)

        def moved(x, shift):
            shift = (f * 32 + shift) % 128
            return pltpu.roll(x, shift, 1) if shift else x

        here = group == f
        first_even = jnp.where(even, moved(first, 0), moved(first, -63))
        first_odd = jnp.where(even, moved(first, -32), moved(first, -95))
        last_even = jnp.where(even, moved(last, -125), moved(last, -62))
        last_odd = jnp.where(even, moved(last, -31), moved(last, -94))
        firsts = [jnp.where(here, a, b) for a, b in zip((first_even, first_odd), firsts)]
        lasts = [jnp.where(here, a, b) for a, b in zip((last_even, last_odd), lasts)]

    block = pick((me & 1) == 0, me + 1, (me + 31) & 63)
    base = block * PPD
    first_box = jnp.int32(0)
    for step in (1024, 512, 256, 128, 64, 32, 16, 8, 4, 2, 1):
        trial = first_box + step
        value = pos[jnp.minimum(trial, NBOX) - 1]
        first_box = pick((trial <= NBOX) & (value < base), trial, first_box)

    def mark(i, words):
        word0, word1 = words
        k = first_box + i
        at = pos[jnp.minimum(k, NBOX - 1)] - base
        good = (k < NBOX) & (at <= PPD)
        bit = jnp.left_shift(jnp.int32(1), at & 31)
        word0 = word0 | pick(good & (at < 32), bit, 0)
        word1 = word1 | pick(good & (at >= 32), bit, 0)
        return word0, word1

    word0, word1 = lax.fori_loop(0, PPD + 1, mark, (jnp.int32(0), jnp.int32(0)), unroll=49)
    for core in range(2):
        joint = 2 * inner + core
        words = jnp.where(joint < 32, word0, word1)
        fine_here = (lax.shift_right_logical(words, joint & 31) & 1) == 1
        edge = jnp.where(fine_here, lasts[core], firsts[core])
        for b in range(core, SLABS, 2):
            out[b, BOX_ROWS:MSG_ROWS] = edge

    def find(i, r):
        return r + pick(owner[i] == me, i, 0)

    residue = lax.fori_loop(0, SLABS, find, jnp.int32(0), unroll=64)

    def fill(b, start):
        starts[b] = start
        k = start - 1 + ((residue - (start - 1)) & 63)
        slot = jnp.clip(k >> 6, 0, BOX_DEV - 1)
        out[b, 0:BOX_ROWS] = packed[slot]
        return start + counts[b]

    lax.fori_loop(0, SLABS, fill, jnp.int32(0), unroll=64)


def plan_kernel(owner, counts, pos, starts, plan):
    me = lax.axis_index("slab")
    mine = me & 1
    start = starts[me]
    plan[MISC * 64] = start
    plan[MISC * 64 + 1] = counts[me]

    def source(i, carry):
        plan[SRC * 64 + i] = owner[(start + i - 2) & 63]
        return carry

    lax.fori_loop(0, MOST + 4, source, 0, unroll=4)

    def code(at, joint, wanted):
        block = (at * 43691) >> 21
        joint = joint + at - block * PPD
        device = pick((block & 1) == 1, block - 1, (block + 33) & 63)
        keep = wanted & ((joint & 1) == mine)
        return pick(keep, device * 32 + (joint >> 1), -1)

    def ghosts(first, left_row, right_row, flags):
        def one(s, carry):
            k = jnp.minimum(first + s, NBOX - 1)
            at = pos[k]
            before = pos[jnp.maximum(k - 1, 0)]
            after = pos[jnp.minimum(k + 1, NBOX - 1)]
            fine_l = before == at - 1
            fine_r = after == at + 1
            if flags:
                plan[FINE_L * 64 + s] = pick(fine_l, 1, 0)
                plan[FINE_R * 64 + s] = pick(fine_r, 1, 0)
            has_l = jnp.logical_not(fine_l) & (k > 0)
            has_r = jnp.logical_not(fine_r) & (k < NBOX - 1)
            plan[left_row * 64 + s] = code(jnp.maximum(at - 1, 0), 1, has_l)
            plan[right_row * 64 + s] = code(jnp.minimum(at + 1, NPOS - 1), 0, has_r)
            return carry

        lax.fori_loop(0, MOST, one, 0, unroll=2)

    ghosts(start, OWN_L, OWN_R, True)
    ghosts(starts[me ^ 1], SIB_L, SIB_R, False)


def gather_edges(plan, inc, left, right):
    lane = lanes()
    inner = lane & 31

    def one(m, carry):
        out = []
        for q, edges in enumerate(carry):
            for row, to in ((left, m), (right, m + QUARTER)):
                code = plan[row * 64 + q * QUARTER + m]
                x = inc[jnp.maximum(code, 0) >> 5, BOX_ROWS:MSG_ROWS]
                x = pltpu.roll(x, (to - (code & 31)) & 127, 1)
                edges = jnp.where((inner == to) & (code >= 0), x, edges)
            out.append(edges)
        return tuple(out)

    zero = jnp.zeros((8, 128), jnp.float32)
    return lax.fori_loop(0, QUARTER, one, (zero,) * 4, unroll=GU)


def edge_kernel(plan, inc, low_rows, high_rows, sibling):
    low = lanes((1, 128)) < 64

    def one(t, carry):
        a = plan[SRC * 64 + 2 + 2 * t]
        b = plan[SRC * 64 + 3 + 2 * t]
        for f in range(FIELDS):
            row = f * 8
            low_rows[t, f : f + 1] = jnp.where(
                low, inc[a, row : row + 1], pltpu.roll(inc[b, row : row + 1], 64, 1)
            )
            row = f * 8 + 7
            high_rows[t, f : f + 1] = jnp.where(
                low, pltpu.roll(inc[a, row : row + 1], 64, 1), inc[b, row : row + 1]
            )
        return carry

    lax.fori_loop(0, TILES, one, 0, unroll=24)
    for n, edges in enumerate(gather_edges(plan, inc, SIB_L, SIB_R)):
        sibling[n] = edges


def advance(center, across, sq_x, south_cells, north_cells):
    laplace = [a + s + n - 4.0 * c for c, a, s, n in zip(center, across, south_cells, north_cells)]
    phase = center[0]
    grad_y = 0.5 * (north_cells[0] - south_cells[0])
    sq_y = grad_y * grad_y
    spread_sum = sq_x + sq_y + 1.0
    anisotropy = 1.0 + ANISOTROPY * (sq_x * sq_x - 6.0 * sq_x * sq_y + sq_y * sq_y) / (
        spread_sum * spread_sum
    )
    couple = center[1] + SOLUTE_ONE * center[2] + SOLUTE_TWO * center[3]
    wall_term = 1.0 - phase * phase
    phase_step = TIME_STEP * (
        anisotropy * anisotropy * laplace[0]
        + phase
        - phase * phase * phase
        - COUPLING * wall_term * wall_term * couple
    )
    return (
        phase + phase_step,
        center[1] + TIME_STEP * DIFF_HEAT * laplace[1] + LATENT * phase_step,
        center[2] + TIME_STEP * DIFF_ONE * laplace[2] + REJECT_ONE * center[2] * phase_step,
        center[3] + TIME_STEP * DIFF_TWO * laplace[3] + REJECT_TWO * center[3] * phase_step,
    )


def middle_kernel(plan, inc, sibling, cen, across, slope, edges, outside):
    lane = lanes()
    low = lane < 64
    row8 = lax.broadcasted_iota(jnp.int32, (8, 128), 0)
    start = plan[MISC * 64]

    def unpack(a, b, put):
        for f in range(FIELDS):
            x = inc[a, f * 8 : f * 8 + 8]
            y = inc[b, f * 8 : f * 8 + 8]
            put(f, 0, jnp.where(low, x, pltpu.roll(y, 64, 1)))
            put(f, 8, jnp.where(low, pltpu.roll(x, 64, 1), y))

    def inside(t, carry):
        def put(f, row, x):
            cen[t, f, row : row + 8] = x

        unpack(plan[SRC * 64 + 2 + 2 * t], plan[SRC * 64 + 3 + 2 * t], put)
        return carry

    lax.fori_loop(0, TILES, inside, 0, unroll=UU)
    for n, s in enumerate((0, MOST + 2)):

        def put(f, row, x):
            outside[n, f, row : row + 8] = x

        unpack(plan[SRC * 64 + s], plan[SRC * 64 + s + 1], put)

    own = gather_edges(plan, inc, OWN_L, OWN_R)
    for n in range(4):
        whole = own[n] + sibling[n]
        edges[n, 0:8] = jnp.take_along_axis(whole, row8 >> 1, axis=0)
        edges[n, 8:16] = jnp.take_along_axis(whole, 4 + (row8 >> 1), axis=0)

    lane = lanes((ROWS, 128))
    near = lanes()
    where_from = jnp.where(near >= 64, 1, 0) + jnp.where((near & 63) >= 32, QUARTER, 0)

    def one(t, before, after):
        s = 2 * t
        q = (s * 43691) >> 19
        m = s - q * QUARTER
        fl0, fl1 = plan[FINE_L * 64 + s] == 1, plan[FINE_L * 64 + s + 1] == 1
        fr0, fr1 = plan[FINE_R * 64 + s] == 1, plan[FINE_R * 64 + s + 1] == 1
        k = start + s
        ghost_w = ((lane == 0) & jnp.logical_not(fl0)) | ((lane == 64) & jnp.logical_not(fl1))
        ghost_e = ((lane == 63) & jnp.logical_not(fr0)) | ((lane == 127) & jnp.logical_not(fr1))
        border = (
            ((lane == 0) & (k == 0))
            | ((lane == 63) & (k == NBOX - 1))
            | ((lane == 127) & (k + 1 == NBOX - 1))
        )
        for f in range(FIELDS):
            c = cen[t, f]
            w = pltpu.roll(jnp.where(lane == 127, before[f], c), 1, 1)
            e = pltpu.roll(jnp.where(lane == 0, after[f], c), 127, 1)
            at = where_from + (m + 32 * f)
            g = jnp.concatenate(
                [jnp.take_along_axis(edges[q, h : h + 8], at, axis=1) for h in (0, 8)], axis=0
            )
            g = jnp.where(border, c, g)
            w = jnp.where(ghost_w, g, w)
            e = jnp.where(ghost_e, g, e)
            across[t, f] = w + e
            if f == 0:
                grad = 0.5 * (e - w)
                slope[t] = grad * grad

    def between(t, carry):
        one(t, cen.at[t - 1], cen.at[t + 1])
        return carry

    one(0, outside.at[0], cen.at[1])
    lax.fori_loop(1, TILES - 1, between, 0, unroll=22)
    one(TILES - 1, cen.at[TILES - 2], outside.at[1])


def step_kernel(plan, cen, across, slope, from_below, from_above, out, held, sems):
    sub = lax.axis_index("sub")
    count = plan[MISC * 64 + 1]
    lane = lanes((ROWS, 128))
    row = lax.broadcasted_iota(jnp.int32, (ROWS, 128), 0)
    at_bottom = sub == 0
    at_top = sub == lax.axis_size("sub") - 1

    def one(t, carry):
        live = jnp.where(lane < 64, 2 * t, 2 * t + 1) < count
        center, south, north = [], [], []
        for f in range(FIELDS):
            c = cen[t, f]
            below = jnp.where(at_bottom, c[0:1], from_below[t, f : f + 1])
            above = jnp.where(at_top, c[15:16], from_above[t, f : f + 1])
            center.append(c)
            south.append(jnp.where(row == 0, below, pltpu.roll(c, 1, 0)))
            north.append(jnp.where(row == ROWS - 1, above, pltpu.roll(c, ROWS - 1, 0)))
        stepped = advance(center, [across[t, f] for f in range(FIELDS)], slope[t], south, north)
        at = pl.ds(pl.multiple_of(t * 128, 128), 128)
        for f in range(FIELDS):
            held[f, :, at] = jnp.where(live, stepped[f], 0.0)
        return carry

    copies = []
    for part in range(PARTS):
        each = TILES // PARTS
        lax.fori_loop(part * each, (part + 1) * each, one, 0, unroll=UNROLL)
        columns = pl.ds(part * each * 128, each * 128)
        copies.append(pltpu.make_async_copy(held.at[:, :, columns], out.at[:, :, columns], sems.at[part]))
        copies[-1].start()
    for copy in copies:
        copy.wait()


PARTS = 4
UNROLL = 6
SMEM = pl.BlockSpec(memory_space=pltpu.SMEM)
VMEM = pl.BlockSpec(memory_space=pltpu.VMEM)
HBM = pl.BlockSpec(memory_space=pltpu.HBM)
PARAMS = pltpu.CompilerParams(vmem_limit_bytes=32 * 1024 * 1024)


def f32(*shape):
    return jax.ShapeDtypeStruct(shape, jnp.float32)


def i32(*shape):
    return jax.ShapeDtypeStruct(shape, jnp.int32)


def body(fine_old, coarse, box_pos, old_owner, new_counts):
    outgoing, starts = pl.pallas_call(
        pack_kernel,
        name="pack",
        out_shape=(f32(SLABS, MSG_ROWS, 128), i32(SLABS)),
        in_specs=[HBM] * 5,
        out_specs=(VMEM, SMEM),
        scratch_shapes=[
            pltpu.SMEM((NBOX,), jnp.int32),
            pltpu.SMEM((SLABS,), jnp.int32),
            pltpu.SMEM((NBOX,), jnp.int32),
            pltpu.VMEM((FIELDS, ROWS, BOX_DEV * BX), jnp.float32),
            pltpu.VMEM((FIELDS, ROWS // 2, PPD * BX // 2), jnp.float32),
            pltpu.VMEM((BOX_DEV, BOX_ROWS, 128), jnp.float32),
            pltpu.SemaphoreType.DMA((5,)),
        ],
        compiler_params=pltpu.CompilerParams(vmem_limit_bytes=62914560),
    )(old_owner, new_counts, box_pos, fine_old, coarse)
    incoming = lax.all_to_all(outgoing, "slab", 0, 0, tiled=True)
    plan = pl.pallas_call(
        plan_kernel,
        name="plan",
        out_shape=i32(8 * 64),
        in_specs=[SMEM] * 4,
        out_specs=SMEM,
        compiler_params=PARAMS,
    )(old_owner, new_counts, box_pos, starts)
    low_rows, high_rows, sibling = pl.pallas_call(
        edge_kernel,
        name="edges",
        out_shape=(f32(TILES, FIELDS, 128), f32(TILES, FIELDS, 128), f32(4, 8, 128)),
        in_specs=[SMEM, VMEM],
        out_specs=(VMEM, VMEM, VMEM),
        compiler_params=PARAMS,
    )(plan, incoming)
    count = lax.axis_size("sub")
    up = [(i, i + 1) for i in range(count - 1)]
    sibling = lax.ppermute(sibling, "slab", [(i, i ^ 1) for i in range(SLABS)])
    from_below = lax.ppermute(high_rows, "sub", up)
    from_above = lax.ppermute(low_rows, "sub", [(b, a) for a, b in up])
    cells = (TILES, FIELDS, ROWS, 128)
    cen, across, slope = pl.pallas_call(
        middle_kernel,
        name="middle",
        out_shape=(f32(*cells), f32(*cells), f32(TILES, ROWS, 128)),
        in_specs=[SMEM, VMEM, VMEM],
        out_specs=(VMEM, VMEM, VMEM),
        scratch_shapes=[
            pltpu.VMEM((4, ROWS, 128), jnp.float32),
            pltpu.VMEM((2, FIELDS, ROWS, 128), jnp.float32),
        ],
        cost_estimate=pl.CostEstimate(flops=8_000_000, bytes_accessed=8_000_000, transcendentals=0),
        compiler_params=PARAMS,
    )(plan, incoming, sibling)
    return pl.pallas_call(
        step_kernel,
        name="step",
        out_shape=f32(FIELDS, ROWS, MOST * BX),
        in_specs=[SMEM] + [VMEM] * 5,
        out_specs=HBM,
        scratch_shapes=[
            pltpu.VMEM((FIELDS, ROWS, MOST * BX), jnp.float32),
            pltpu.SemaphoreType.DMA((PARTS,)),
        ],
        compiler_params=PARAMS,
    )(plan, cen, across, slope, from_below, from_above)


def solution(mesh):
    placed = (P(None, "sub", "slab"), P(None, "sub", "slab"), P(), P(), P())
    return jax.shard_map(
        body, mesh=mesh, in_specs=placed, out_specs=P(None, "sub", "slab"), check_vma=False
    )
```

```python
import jax
import jax.numpy as jnp
from jax import lax
from jax.experimental import pallas as pl
from jax.experimental.pallas import tpu as pltpu
from jax.sharding import PartitionSpec as P

BX = 64
BOX_DEV = 24
MOST = 48
NBOX = 1536
PPD = 48
NPOS = 3072
SLABS = 64
TILES = MOST // 2
QUARTER = MOST // 4
GU = 12
UU = 24
FIELDS = 4
ROWS = 16
BOX_ROWS = FIELDS * 8
MSG_ROWS = BOX_ROWS + 8

ANISOTROPY = 0.3
TIME_STEP = 0.1
COUPLING = 1.5
SOLUTE_ONE = 0.6
SOLUTE_TWO = -0.4
DIFF_HEAT = 2.0
DIFF_ONE = 0.5
DIFF_TWO = 0.25
LATENT = 0.5
REJECT_ONE = 0.5
REJECT_TWO = -0.3

SRC, FINE_L, FINE_R, OWN_L, OWN_R, SIB_L, SIB_R, MISC = range(8)


def lanes(shape=(8, 128)):
    return lax.broadcasted_iota(jnp.int32, shape, 1)


def pick(cond, a, b):
    return lax.select(cond, jnp.int32(a), jnp.int32(b))


def pack_kernel(
    owner_in, counts_in, pos_in, fine_in, coarse_in, out, starts, owner, counts, pos, fine, coarse, packed, sems
):
    copies = [
        pltpu.make_async_copy(a, b, sems.at[n])
        for n, (a, b) in enumerate(
            ((pos_in, pos), (owner_in, owner), (counts_in, counts), (fine_in, fine), (coarse_in, coarse))
        )
    ]
    for copy in copies:
        copy.start()
    for copy in copies:
        copy.wait()
    me = lax.axis_index("slab")
    lane = lanes()
    low = lane < 64

    for tile in range(BOX_DEV // 2):
        for f in range(FIELDS):
            top = fine[f, 0:8, tile * 128 : tile * 128 + 128]
            bottom = fine[f, 8:16, tile * 128 : tile * 128 + 128]
            packed[2 * tile, f * 8 : f * 8 + 8] = jnp.where(low, top, pltpu.roll(bottom, 64, 1))
            packed[2 * tile + 1, f * 8 : f * 8 + 8] = jnp.where(low, pltpu.roll(top, 64, 1), bottom)

    inner = lane & 31
    group = lane >> 5
    even = (lane & 1) == 0
    firsts = [jnp.zeros((8, 128), jnp.float32) for _ in range(2)]
    lasts = [jnp.zeros((8, 128), jnp.float32) for _ in range(2)]
    for f in range(FIELDS):
        first = jnp.zeros((8, 128), jnp.float32)
        last = jnp.zeros((8, 128), jnp.float32)
        for tile in range(12):
            x = coarse[f, :, tile * 128 : tile * 128 + 128]
            if tile:
                x = pltpu.roll(x, 2 * tile, 1)
            first = jnp.where(inner == 2 * tile, x, first)
            last = jnp.where(inner == (31 + 2 * tile) % 32, x, last)

        def moved(x, shift):
            shift = (f * 32 + shift) % 128
            return pltpu.roll(x, shift, 1) if shift else x

        here = group == f
        first_even = jnp.where(even, moved(first, 0), moved(first, -63))
        first_odd = jnp.where(even, moved(first, -32), moved(first, -95))
        last_even = jnp.where(even, moved(last, -125), moved(last, -62))
        last_odd = jnp.where(even, moved(last, -31), moved(last, -94))
        firsts = [jnp.where(here, a, b) for a, b in zip((first_even, first_odd), firsts)]
        lasts = [jnp.where(here, a, b) for a, b in zip((last_even, last_odd), lasts)]

    block = pick((me & 1) == 0, me + 1, (me + 31) & 63)
    base = block * PPD
    first_box = jnp.int32(0)
    for step in (1024, 512, 256, 128, 64, 32, 16, 8, 4, 2, 1):
        trial = first_box + step
        value = pos[jnp.minimum(trial, NBOX) - 1]
        first_box = pick((trial <= NBOX) & (value < base), trial, first_box)

    def mark(i, words):
        word0, word1 = words
        k = first_box + i
        at = pos[jnp.minimum(k, NBOX - 1)] - base
        good = (k < NBOX) & (at <= PPD)
        bit = jnp.left_shift(jnp.int32(1), at & 31)
        word0 = word0 | pick(good & (at < 32), bit, 0)
        word1 = word1 | pick(good & (at >= 32), bit, 0)
        return word0, word1

    word0, word1 = lax.fori_loop(0, PPD + 1, mark, (jnp.int32(0), jnp.int32(0)), unroll=49)
    for core in range(2):
        joint = 2 * inner + core
        words = jnp.where(joint < 32, word0, word1)
        fine_here = (lax.shift_right_logical(words, joint & 31) & 1) == 1
        edge = jnp.where(fine_here, lasts[core], firsts[core])
        for b in range(core, SLABS, 2):
            out[b, BOX_ROWS:MSG_ROWS] = edge

    def find(i, r):
        return r + pick(owner[i] == me, i, 0)

    residue = lax.fori_loop(0, SLABS, find, jnp.int32(0), unroll=64)

    def fill(b, start):
        starts[b] = start
        k = start - 1 + ((residue - (start - 1)) & 63)
        slot = jnp.clip(k >> 6, 0, BOX_DEV - 1)
        out[b, 0:BOX_ROWS] = packed[slot]
        return start + counts[b]

    lax.fori_loop(0, SLABS, fill, jnp.int32(0), unroll=64)


def plan_kernel(owner, counts, pos, starts, plan):
    me = lax.axis_index("slab")
    mine = me & 1
    start = starts[me]
    plan[MISC * 64] = start
    plan[MISC * 64 + 1] = counts[me]

    def source(i, carry):
        plan[SRC * 64 + i] = owner[(start + i - 2) & 63]
        return carry

    lax.fori_loop(0, MOST + 4, source, 0, unroll=4)

    def code(at, joint, wanted):
        block = (at * 43691) >> 21
        joint = joint + at - block * PPD
        device = pick((block & 1) == 1, block - 1, (block + 33) & 63)
        keep = wanted & ((joint & 1) == mine)
        return pick(keep, device * 32 + (joint >> 1), -1)

    def ghosts(first, left_row, right_row, flags):
        def one(s, carry):
            k = jnp.minimum(first + s, NBOX - 1)
            at = pos[k]
            before = pos[jnp.maximum(k - 1, 0)]
            after = pos[jnp.minimum(k + 1, NBOX - 1)]
            fine_l = before == at - 1
            fine_r = after == at + 1
            if flags:
                plan[FINE_L * 64 + s] = pick(fine_l, 1, 0)
                plan[FINE_R * 64 + s] = pick(fine_r, 1, 0)
            has_l = jnp.logical_not(fine_l) & (k > 0)
            has_r = jnp.logical_not(fine_r) & (k < NBOX - 1)
            plan[left_row * 64 + s] = code(jnp.maximum(at - 1, 0), 1, has_l)
            plan[right_row * 64 + s] = code(jnp.minimum(at + 1, NPOS - 1), 0, has_r)
            return carry

        lax.fori_loop(0, MOST, one, 0, unroll=2)

    ghosts(start, OWN_L, OWN_R, True)
    ghosts(starts[me ^ 1], SIB_L, SIB_R, False)


def gather_edges(plan, inc, left, right):
    lane = lanes()
    inner = lane & 31

    def one(m, carry):
        out = []
        for q, edges in enumerate(carry):
            for row, to in ((left, m), (right, m + QUARTER)):
                code = plan[row * 64 + q * QUARTER + m]
                x = inc[jnp.maximum(code, 0) >> 5, BOX_ROWS:MSG_ROWS]
                x = pltpu.roll(x, (to - (code & 31)) & 127, 1)
                edges = jnp.where((inner == to) & (code >= 0), x, edges)
            out.append(edges)
        return tuple(out)

    zero = jnp.zeros((8, 128), jnp.float32)
    return lax.fori_loop(0, QUARTER, one, (zero,) * 4, unroll=GU)


def edge_kernel(plan, inc, low_rows, high_rows, sibling):
    low = lanes((1, 128)) < 64

    def one(t, carry):
        a = plan[SRC * 64 + 2 + 2 * t]
        b = plan[SRC * 64 + 3 + 2 * t]
        for f in range(FIELDS):
            row = f * 8
            low_rows[t, f : f + 1] = jnp.where(
                low, inc[a, row : row + 1], pltpu.roll(inc[b, row : row + 1], 64, 1)
            )
            row = f * 8 + 7
            high_rows[t, f : f + 1] = jnp.where(
                low, pltpu.roll(inc[a, row : row + 1], 64, 1), inc[b, row : row + 1]
            )
        return carry

    lax.fori_loop(0, TILES, one, 0, unroll=24)
    for n, edges in enumerate(gather_edges(plan, inc, SIB_L, SIB_R)):
        sibling[n] = edges


def advance(center, across, sq_x, south_cells, north_cells):
    laplace = [a + s + n - 4.0 * c for c, a, s, n in zip(center, across, south_cells, north_cells)]
    phase = center[0]
    grad_y = 0.5 * (north_cells[0] - south_cells[0])
    sq_y = grad_y * grad_y
    spread_sum = sq_x + sq_y + 1.0
    anisotropy = 1.0 + ANISOTROPY * (sq_x * sq_x - 6.0 * sq_x * sq_y + sq_y * sq_y) / (
        spread_sum * spread_sum
    )
    couple = center[1] + SOLUTE_ONE * center[2] + SOLUTE_TWO * center[3]
    wall_term = 1.0 - phase * phase
    phase_step = TIME_STEP * (
        anisotropy * anisotropy * laplace[0]
        + phase
        - phase * phase * phase
        - COUPLING * wall_term * wall_term * couple
    )
    return (
        phase + phase_step,
        center[1] + TIME_STEP * DIFF_HEAT * laplace[1] + LATENT * phase_step,
        center[2] + TIME_STEP * DIFF_ONE * laplace[2] + REJECT_ONE * center[2] * phase_step,
        center[3] + TIME_STEP * DIFF_TWO * laplace[3] + REJECT_TWO * center[3] * phase_step,
    )


def whole_rows(coarse_rows, edges):
    row = lax.broadcasted_iota(jnp.int32, (8, 128), 0) >> 1
    for n, x in enumerate(coarse_rows):
        edges[n, 0:8] = jnp.take_along_axis(x, row, axis=0)
        edges[n, 8:16] = jnp.take_along_axis(x, 4 + row, axis=0)


def ghost_source():
    lane = lanes()
    return jnp.where(lane >= 64, 1, 0) + jnp.where((lane & 63) >= 32, QUARTER, 0)


def ghosts_of(edges, t, f, where_from):
    q = (2 * t * 43691) >> 19
    at = where_from + (2 * t - q * QUARTER + 32 * f)
    return jnp.concatenate([jnp.take_along_axis(edges[q, h : h + 8], at, axis=1) for h in (0, 8)], axis=0)


def middle_kernel(plan, inc, cen, across, slope, edges, outside):
    lane = lanes()
    low = lane < 64
    start = plan[MISC * 64]

    def unpack(a, b, put):
        for f in range(FIELDS):
            x = inc[a, f * 8 : f * 8 + 8]
            y = inc[b, f * 8 : f * 8 + 8]
            put(f, 0, jnp.where(low, x, pltpu.roll(y, 64, 1)))
            put(f, 8, jnp.where(low, pltpu.roll(x, 64, 1), y))

    def inside(t, carry):
        def put(f, row, x):
            cen[t, f, row : row + 8] = x

        unpack(plan[SRC * 64 + 2 + 2 * t], plan[SRC * 64 + 3 + 2 * t], put)
        return carry

    lax.fori_loop(0, TILES, inside, 0, unroll=UU)
    for n, s in enumerate((0, MOST + 2)):

        def put(f, row, x):
            outside[n, f, row : row + 8] = x

        unpack(plan[SRC * 64 + s], plan[SRC * 64 + s + 1], put)

    whole_rows(gather_edges(plan, inc, OWN_L, OWN_R), edges)
    lane = lanes((ROWS, 128))
    where_from = ghost_source()

    def one(t, before, after):
        s = 2 * t
        fl0, fl1 = plan[FINE_L * 64 + s] == 1, plan[FINE_L * 64 + s + 1] == 1
        fr0, fr1 = plan[FINE_R * 64 + s] == 1, plan[FINE_R * 64 + s + 1] == 1
        k = start + s
        ghost_w = ((lane == 0) & jnp.logical_not(fl0)) | ((lane == 64) & jnp.logical_not(fl1))
        ghost_e = ((lane == 63) & jnp.logical_not(fr0)) | ((lane == 127) & jnp.logical_not(fr1))
        border = (
            ((lane == 0) & (k == 0))
            | ((lane == 63) & (k == NBOX - 1))
            | ((lane == 127) & (k + 1 == NBOX - 1))
        )
        for f in range(FIELDS):
            c = cen[t, f]
            w = pltpu.roll(jnp.where(lane == 127, before[f], c), 1, 1)
            e = pltpu.roll(jnp.where(lane == 0, after[f], c), 127, 1)
            g = ghosts_of(edges, t, f, where_from)
            g = jnp.where(border, c, g)
            w = jnp.where(ghost_w, g, w)
            e = jnp.where(ghost_e, g, e)
            across[t, f] = w + e
            if f == 0:
                slope[t] = e - w

    def between(t, carry):
        one(t, cen.at[t - 1], cen.at[t + 1])
        return carry

    one(0, outside.at[0], cen.at[1])
    lax.fori_loop(1, TILES - 1, between, 0, unroll=22)
    one(TILES - 1, cen.at[TILES - 2], outside.at[1])


def step_kernel(plan, cen, across, slope, sibling, from_below, from_above, out, held, edges, sems):
    sub = lax.axis_index("sub")
    count = plan[MISC * 64 + 1]
    lane = lanes((ROWS, 128))
    row = lax.broadcasted_iota(jnp.int32, (ROWS, 128), 0)
    at_bottom = sub == 0
    at_top = sub == lax.axis_size("sub") - 1
    right = (lane & 63) >= 32
    where_from = ghost_source()
    whole_rows([sibling[n] for n in range(4)], edges)

    def one(t, carry):
        live = jnp.where(lane < 64, 2 * t, 2 * t + 1) < count
        center, sides, south, north = [], [], [], []
        for f in range(FIELDS):
            c = cen[t, f]
            below = jnp.where(at_bottom, c[0:1], from_below[t, f : f + 1])
            above = jnp.where(at_top, c[15:16], from_above[t, f : f + 1])
            g = ghosts_of(edges, t, f, where_from)
            g = jnp.where(((lane + 1) & 63) < 2, g, 0.0)
            if f == 0:
                grad_x = 0.5 * (slope[t] + jnp.where(right, g, -g))
            center.append(c)
            sides.append(across[t, f] + g)
            south.append(jnp.where(row == 0, below, pltpu.roll(c, 1, 0)))
            north.append(jnp.where(row == ROWS - 1, above, pltpu.roll(c, ROWS - 1, 0)))
        stepped = advance(center, sides, grad_x * grad_x, south, north)
        at = pl.ds(pl.multiple_of(t * 128, 128), 128)
        for f in range(FIELDS):
            held[f, :, at] = jnp.where(live, stepped[f], 0.0)
        return carry

    copies = []
    for part in range(PARTS):
        each = TILES // PARTS
        lax.fori_loop(part * each, (part + 1) * each, one, 0, unroll=UNROLL)
        columns = pl.ds(part * each * 128, each * 128)
        copies.append(pltpu.make_async_copy(held.at[:, :, columns], out.at[:, :, columns], sems.at[part]))
        copies[-1].start()
    for copy in copies:
        copy.wait()


PARTS = 4
UNROLL = 6
SMEM = pl.BlockSpec(memory_space=pltpu.SMEM)
VMEM = pl.BlockSpec(memory_space=pltpu.VMEM)
HBM = pl.BlockSpec(memory_space=pltpu.HBM)
PARAMS = pltpu.CompilerParams(vmem_limit_bytes=32 * 1024 * 1024)


def f32(*shape):
    return jax.ShapeDtypeStruct(shape, jnp.float32)


def i32(*shape):
    return jax.ShapeDtypeStruct(shape, jnp.int32)


def body(fine_old, coarse, box_pos, old_owner, new_counts):
    outgoing, starts = pl.pallas_call(
        pack_kernel,
        name="pack",
        out_shape=(f32(SLABS, MSG_ROWS, 128), i32(SLABS)),
        in_specs=[HBM] * 5,
        out_specs=(VMEM, SMEM),
        scratch_shapes=[
            pltpu.SMEM((NBOX,), jnp.int32),
            pltpu.SMEM((SLABS,), jnp.int32),
            pltpu.SMEM((NBOX,), jnp.int32),
            pltpu.VMEM((FIELDS, ROWS, BOX_DEV * BX), jnp.float32),
            pltpu.VMEM((FIELDS, ROWS // 2, PPD * BX // 2), jnp.float32),
            pltpu.VMEM((BOX_DEV, BOX_ROWS, 128), jnp.float32),
            pltpu.SemaphoreType.DMA((5,)),
        ],
        compiler_params=pltpu.CompilerParams(vmem_limit_bytes=62914560),
    )(old_owner, new_counts, box_pos, fine_old, coarse)
    incoming = lax.all_to_all(outgoing, "slab", 0, 0, tiled=True)
    plan = pl.pallas_call(
        plan_kernel,
        name="plan",
        out_shape=i32(8 * 64),
        in_specs=[SMEM] * 4,
        out_specs=SMEM,
        compiler_params=PARAMS,
    )(old_owner, new_counts, box_pos, starts)
    low_rows, high_rows, sibling = pl.pallas_call(
        edge_kernel,
        name="edges",
        out_shape=(f32(TILES, FIELDS, 128), f32(TILES, FIELDS, 128), f32(4, 8, 128)),
        in_specs=[SMEM, VMEM],
        out_specs=(VMEM, VMEM, VMEM),
        compiler_params=PARAMS,
    )(plan, incoming)
    count = lax.axis_size("sub")
    up = [(i, i + 1) for i in range(count - 1)]
    sibling = lax.ppermute(sibling, "slab", [(i, i ^ 1) for i in range(SLABS)])
    from_below = lax.ppermute(high_rows, "sub", up)
    from_above = lax.ppermute(low_rows, "sub", [(b, a) for a, b in up])
    cells = (TILES, FIELDS, ROWS, 128)
    cen, across, slope = pl.pallas_call(
        middle_kernel,
        name="middle",
        out_shape=(f32(*cells), f32(*cells), f32(TILES, ROWS, 128)),
        in_specs=[SMEM, VMEM],
        out_specs=(VMEM, VMEM, VMEM),
        scratch_shapes=[
            pltpu.VMEM((4, ROWS, 128), jnp.float32),
            pltpu.VMEM((2, FIELDS, ROWS, 128), jnp.float32),
        ],
        cost_estimate=pl.CostEstimate(flops=8_000_000, bytes_accessed=8_000_000, transcendentals=0),
        compiler_params=PARAMS,
    )(plan, incoming)
    return pl.pallas_call(
        step_kernel,
        name="step",
        out_shape=f32(FIELDS, ROWS, MOST * BX),
        in_specs=[SMEM] + [VMEM] * 6,
        out_specs=HBM,
        scratch_shapes=[
            pltpu.VMEM((FIELDS, ROWS, MOST * BX), jnp.float32),
            pltpu.VMEM((4, ROWS, 128), jnp.float32),
            pltpu.SemaphoreType.DMA((PARTS,)),
        ],
        compiler_params=PARAMS,
    )(plan, cen, across, slope, sibling, from_below, from_above)


def solution(mesh):
    placed = (P(None, "sub", "slab"), P(None, "sub", "slab"), P(), P(), P())
    return jax.shard_map(
        body, mesh=mesh, in_specs=placed, out_specs=P(None, "sub", "slab"), check_vma=False
    )
```

```python
import jax
import jax.numpy as jnp
from jax import lax
from jax.experimental import pallas as pl
from jax.experimental.pallas import tpu as pltpu
from jax.sharding import PartitionSpec as P

BX = 64
BOX_DEV = 24
MOST = 48
NBOX = 1536
PPD = 48
NPOS = 3072
SLABS = 64
TILES = MOST // 2
QUARTER = MOST // 4
GU = 12
UU = 24
FIELDS = 4
ROWS = 16
BOX_ROWS = FIELDS * 8
MSG_ROWS = BOX_ROWS + 8

ANISOTROPY = 0.3
TIME_STEP = 0.1
COUPLING = 1.5
SOLUTE_ONE = 0.6
SOLUTE_TWO = -0.4
DIFF_HEAT = 2.0
DIFF_ONE = 0.5
DIFF_TWO = 0.25
LATENT = 0.5
REJECT_ONE = 0.5
REJECT_TWO = -0.3

SRC, FINE_L, FINE_R, OWN_L, OWN_R, SIB_L, SIB_R, MISC = range(8)


def lanes(shape=(8, 128)):
    return lax.broadcasted_iota(jnp.int32, shape, 1)


def pick(cond, a, b):
    return lax.select(cond, jnp.int32(a), jnp.int32(b))


def pack_kernel(
    owner_in, counts_in, pos_in, fine_in, coarse_in, out, starts, owner, counts, pos, fine, coarse, packed, sems
):
    copies = [
        pltpu.make_async_copy(a, b, sems.at[n])
        for n, (a, b) in enumerate(
            ((pos_in, pos), (owner_in, owner), (counts_in, counts), (fine_in, fine), (coarse_in, coarse))
        )
    ]
    for copy in copies:
        copy.start()
    for copy in copies:
        copy.wait()
    me = lax.axis_index("slab")
    lane = lanes()
    low = lane < 64

    for tile in range(BOX_DEV // 2):
        for f in range(FIELDS):
            top = fine[f, 0:8, tile * 128 : tile * 128 + 128]
            bottom = fine[f, 8:16, tile * 128 : tile * 128 + 128]
            packed[2 * tile, f * 8 : f * 8 + 8] = jnp.where(low, top, pltpu.roll(bottom, 64, 1))
            packed[2 * tile + 1, f * 8 : f * 8 + 8] = jnp.where(low, pltpu.roll(top, 64, 1), bottom)

    inner = lane & 31
    group = lane >> 5
    even = (lane & 1) == 0
    firsts = [jnp.zeros((8, 128), jnp.float32) for _ in range(2)]
    lasts = [jnp.zeros((8, 128), jnp.float32) for _ in range(2)]
    for f in range(FIELDS):
        first = jnp.zeros((8, 128), jnp.float32)
        last = jnp.zeros((8, 128), jnp.float32)
        for tile in range(12):
            x = coarse[f, :, tile * 128 : tile * 128 + 128]
            if tile:
                x = pltpu.roll(x, 2 * tile, 1)
            first = jnp.where(inner == 2 * tile, x, first)
            last = jnp.where(inner == (31 + 2 * tile) % 32, x, last)

        def moved(x, shift):
            shift = (f * 32 + shift) % 128
            return pltpu.roll(x, shift, 1) if shift else x

        here = group == f
        first_even = jnp.where(even, moved(first, 0), moved(first, -63))
        first_odd = jnp.where(even, moved(first, -32), moved(first, -95))
        last_even = jnp.where(even, moved(last, -125), moved(last, -62))
        last_odd = jnp.where(even, moved(last, -31), moved(last, -94))
        firsts = [jnp.where(here, a, b) for a, b in zip((first_even, first_odd), firsts)]
        lasts = [jnp.where(here, a, b) for a, b in zip((last_even, last_odd), lasts)]

    block = pick((me & 1) == 0, me + 1, (me + 31) & 63)
    base = block * PPD
    first_box = jnp.int32(0)
    for step in (1024, 512, 256, 128, 64, 32, 16, 8, 4, 2, 1):
        trial = first_box + step
        value = pos[jnp.minimum(trial, NBOX) - 1]
        first_box = pick((trial <= NBOX) & (value < base), trial, first_box)

    def mark(i, words):
        word0, word1 = words
        k = first_box + i
        at = pos[jnp.minimum(k, NBOX - 1)] - base
        good = (k < NBOX) & (at <= PPD)
        bit = jnp.left_shift(jnp.int32(1), at & 31)
        word0 = word0 | pick(good & (at < 32), bit, 0)
        word1 = word1 | pick(good & (at >= 32), bit, 0)
        return word0, word1

    word0, word1 = lax.fori_loop(0, PPD + 1, mark, (jnp.int32(0), jnp.int32(0)), unroll=49)
    for core in range(2):
        joint = 2 * inner + core
        words = jnp.where(joint < 32, word0, word1)
        fine_here = (lax.shift_right_logical(words, joint & 31) & 1) == 1
        edge = jnp.where(fine_here, lasts[core], firsts[core])
        for b in range(core, SLABS, 2):
            out[b, BOX_ROWS:MSG_ROWS] = edge

    def find(i, r):
        return r + pick(owner[i] == me, i, 0)

    residue = lax.fori_loop(0, SLABS, find, jnp.int32(0), unroll=64)

    def fill(b, start):
        starts[b] = start
        k = start - 1 + ((residue - (start - 1)) & 63)
        slot = jnp.clip(k >> 6, 0, BOX_DEV - 1)
        out[b, 0:BOX_ROWS] = packed[slot]
        return start + counts[b]

    lax.fori_loop(0, SLABS, fill, jnp.int32(0), unroll=64)


def plan_kernel(owner, counts, pos, starts, plan):
    me = lax.axis_index("slab")
    mine = me & 1
    start = starts[me]
    plan[MISC * 64] = start
    plan[MISC * 64 + 1] = counts[me]

    def source(i, carry):
        plan[SRC * 64 + i] = owner[(start + i - 2) & 63]
        return carry

    lax.fori_loop(0, MOST + 4, source, 0, unroll=4)

    def code(at, joint, wanted):
        block = (at * 43691) >> 21
        joint = joint + at - block * PPD
        device = pick((block & 1) == 1, block - 1, (block + 33) & 63)
        keep = wanted & ((joint & 1) == mine)
        return pick(keep, device * 32 + (joint >> 1), -1)

    def ghosts(first, left_row, right_row, flags):
        def one(s, carry):
            k = jnp.minimum(first + s, NBOX - 1)
            at = pos[k]
            before = pos[jnp.maximum(k - 1, 0)]
            after = pos[jnp.minimum(k + 1, NBOX - 1)]
            fine_l = before == at - 1
            fine_r = after == at + 1
            if flags:
                plan[FINE_L * 64 + s] = pick(fine_l, 1, 0)
                plan[FINE_R * 64 + s] = pick(fine_r, 1, 0)
            has_l = jnp.logical_not(fine_l) & (k > 0)
            has_r = jnp.logical_not(fine_r) & (k < NBOX - 1)
            plan[left_row * 64 + s] = code(jnp.maximum(at - 1, 0), 1, has_l)
            plan[right_row * 64 + s] = code(jnp.minimum(at + 1, NPOS - 1), 0, has_r)
            return carry

        lax.fori_loop(0, MOST, one, 0, unroll=2)

    ghosts(start, OWN_L, OWN_R, True)
    ghosts(starts[me ^ 1], SIB_L, SIB_R, False)


def gather_edges(plan, inc, left, right):
    lane = lanes()
    inner = lane & 31

    def one(m, carry):
        out = []
        for q, edges in enumerate(carry):
            for row, to in ((left, m), (right, m + QUARTER)):
                code = plan[row * 64 + q * QUARTER + m]
                x = inc[jnp.maximum(code, 0) >> 5, BOX_ROWS:MSG_ROWS]
                x = pltpu.roll(x, (to - (code & 31)) & 127, 1)
                edges = jnp.where((inner == to) & (code >= 0), x, edges)
            out.append(edges)
        return tuple(out)

    zero = jnp.zeros((8, 128), jnp.float32)
    return lax.fori_loop(0, QUARTER, one, (zero,) * 4, unroll=GU)


def edge_kernel(plan, inc, first_rows, second_rows, sibling):
    low = lanes((1, 128)) < 64
    odd = (lax.axis_index("sub") & 1) == 1

    def one(t, carry):
        a = plan[SRC * 64 + 2 + 2 * t]
        b = plan[SRC * 64 + 3 + 2 * t]
        for f in range(FIELDS):
            row = f * 8
            bottom = jnp.where(low, inc[a, row : row + 1], pltpu.roll(inc[b, row : row + 1], 64, 1))
            row = f * 8 + 7
            top = jnp.where(low, pltpu.roll(inc[a, row : row + 1], 64, 1), inc[b, row : row + 1])
            first_rows[t, f : f + 1] = jnp.where(odd, top, bottom)
            second_rows[t, f : f + 1] = jnp.where(odd, bottom, top)
        return carry

    lax.fori_loop(0, TILES, one, 0, unroll=24)
    for n, edges in enumerate(gather_edges(plan, inc, SIB_L, SIB_R)):
        sibling[n] = edges


def advance(center, across, sq_x, south_cells, north_cells):
    laplace = [a + s + n - 4.0 * c for c, a, s, n in zip(center, across, south_cells, north_cells)]
    phase = center[0]
    grad_y = 0.5 * (north_cells[0] - south_cells[0])
    sq_y = grad_y * grad_y
    spread_sum = sq_x + sq_y + 1.0
    anisotropy = 1.0 + ANISOTROPY * (sq_x * sq_x - 6.0 * sq_x * sq_y + sq_y * sq_y) / (
        spread_sum * spread_sum
    )
    couple = center[1] + SOLUTE_ONE * center[2] + SOLUTE_TWO * center[3]
    wall_term = 1.0 - phase * phase
    phase_step = TIME_STEP * (
        anisotropy * anisotropy * laplace[0]
        + phase
        - phase * phase * phase
        - COUPLING * wall_term * wall_term * couple
    )
    return (
        phase + phase_step,
        center[1] + TIME_STEP * DIFF_HEAT * laplace[1] + LATENT * phase_step,
        center[2] + TIME_STEP * DIFF_ONE * laplace[2] + REJECT_ONE * center[2] * phase_step,
        center[3] + TIME_STEP * DIFF_TWO * laplace[3] + REJECT_TWO * center[3] * phase_step,
    )


def whole_rows(coarse_rows, edges):
    row = lax.broadcasted_iota(jnp.int32, (8, 128), 0) >> 1
    for n, x in enumerate(coarse_rows):
        edges[n, 0:8] = jnp.take_along_axis(x, row, axis=0)
        edges[n, 8:16] = jnp.take_along_axis(x, 4 + row, axis=0)


def ghost_source():
    lane = lanes()
    return jnp.where(lane >= 64, 1, 0) + jnp.where((lane & 63) >= 32, QUARTER, 0)


def ghosts_of(edges, t, f, where_from):
    q = (2 * t * 43691) >> 19
    at = where_from + (2 * t - q * QUARTER + 32 * f)
    return jnp.concatenate([jnp.take_along_axis(edges[q, h : h + 8], at, axis=1) for h in (0, 8)], axis=0)


def middle_kernel(plan, inc, cen, across, slope, edges, outside):
    lane = lanes()
    low = lane < 64
    start = plan[MISC * 64]

    def unpack(a, b, put):
        for f in range(FIELDS):
            x = inc[a, f * 8 : f * 8 + 8]
            y = inc[b, f * 8 : f * 8 + 8]
            put(f, 0, jnp.where(low, x, pltpu.roll(y, 64, 1)))
            put(f, 8, jnp.where(low, pltpu.roll(x, 64, 1), y))

    def inside(t, carry):
        def put(f, row, x):
            cen[t, f, row : row + 8] = x

        unpack(plan[SRC * 64 + 2 + 2 * t], plan[SRC * 64 + 3 + 2 * t], put)
        return carry

    lax.fori_loop(0, TILES, inside, 0, unroll=UU)
    for n, s in enumerate((0, MOST + 2)):

        def put(f, row, x):
            outside[n, f, row : row + 8] = x

        unpack(plan[SRC * 64 + s], plan[SRC * 64 + s + 1], put)

    whole_rows(gather_edges(plan, inc, OWN_L, OWN_R), edges)
    lane = lanes((ROWS, 128))
    where_from = ghost_source()

    def one(t, before, after):
        s = 2 * t
        fl0, fl1 = plan[FINE_L * 64 + s] == 1, plan[FINE_L * 64 + s + 1] == 1
        fr0, fr1 = plan[FINE_R * 64 + s] == 1, plan[FINE_R * 64 + s + 1] == 1
        k = start + s
        ghost_w = ((lane == 0) & jnp.logical_not(fl0)) | ((lane == 64) & jnp.logical_not(fl1))
        ghost_e = ((lane == 63) & jnp.logical_not(fr0)) | ((lane == 127) & jnp.logical_not(fr1))
        border = (
            ((lane == 0) & (k == 0))
            | ((lane == 63) & (k == NBOX - 1))
            | ((lane == 127) & (k + 1 == NBOX - 1))
        )
        for f in range(FIELDS):
            c = cen[t, f]
            w = pltpu.roll(jnp.where(lane == 127, before[f], c), 1, 1)
            e = pltpu.roll(jnp.where(lane == 0, after[f], c), 127, 1)
            g = ghosts_of(edges, t, f, where_from)
            g = jnp.where(border, c, g)
            w = jnp.where(ghost_w, g, w)
            e = jnp.where(ghost_e, g, e)
            across[t, f] = w + e
            if f == 0:
                slope[t] = e - w

    def between(t, carry):
        one(t, cen.at[t - 1], cen.at[t + 1])
        return carry

    one(0, outside.at[0], cen.at[1])
    lax.fori_loop(1, TILES - 1, between, 0, unroll=22)
    one(TILES - 1, cen.at[TILES - 2], outside.at[1])


def step_kernel(plan, cen, across, slope, sibling, first_rows, second_rows, out, held, edges, sems):
    sub = lax.axis_index("sub")
    count = plan[MISC * 64 + 1]
    lane = lanes((ROWS, 128))
    row = lax.broadcasted_iota(jnp.int32, (ROWS, 128), 0)
    odd = (sub & 1) == 1
    at_bottom = sub == 0
    at_top = sub == lax.axis_size("sub") - 1
    right = (lane & 63) >= 32
    where_from = ghost_source()
    whole_rows([sibling[n] for n in range(4)], edges)

    def one(t, carry):
        live = jnp.where(lane < 64, 2 * t, 2 * t + 1) < count
        center, sides, south, north = [], [], [], []
        for f in range(FIELDS):
            c = cen[t, f]
            one_side, other_side = first_rows[t, f : f + 1], second_rows[t, f : f + 1]
            below = jnp.where(at_bottom, c[0:1], jnp.where(odd, other_side, one_side))
            above = jnp.where(at_top, c[15:16], jnp.where(odd, one_side, other_side))
            g = ghosts_of(edges, t, f, where_from)
            g = jnp.where(((lane + 1) & 63) < 2, g, 0.0)
            if f == 0:
                grad_x = 0.5 * (slope[t] + jnp.where(right, g, -g))
            center.append(c)
            sides.append(across[t, f] + g)
            south.append(jnp.where(row == 0, below, pltpu.roll(c, 1, 0)))
            north.append(jnp.where(row == ROWS - 1, above, pltpu.roll(c, ROWS - 1, 0)))
        stepped = advance(center, sides, grad_x * grad_x, south, north)
        at = pl.ds(pl.multiple_of(t * 128, 128), 128)
        for f in range(FIELDS):
            held[f, :, at] = jnp.where(live, stepped[f], 0.0)
        return carry

    copies = []
    for part in range(PARTS):
        each = TILES // PARTS
        lax.fori_loop(part * each, (part + 1) * each, one, 0, unroll=UNROLL)
        columns = pl.ds(part * each * 128, each * 128)
        copies.append(pltpu.make_async_copy(held.at[:, :, columns], out.at[:, :, columns], sems.at[part]))
        copies[-1].start()
    for copy in copies:
        copy.wait()


PARTS = 4
UNROLL = 6
SMEM = pl.BlockSpec(memory_space=pltpu.SMEM)
VMEM = pl.BlockSpec(memory_space=pltpu.VMEM)
HBM = pl.BlockSpec(memory_space=pltpu.HBM)
PARAMS = pltpu.CompilerParams(vmem_limit_bytes=32 * 1024 * 1024)


def f32(*shape):
    return jax.ShapeDtypeStruct(shape, jnp.float32)


def i32(*shape):
    return jax.ShapeDtypeStruct(shape, jnp.int32)


def body(fine_old, coarse, box_pos, old_owner, new_counts):
    outgoing, starts = pl.pallas_call(
        pack_kernel,
        name="pack",
        out_shape=(f32(SLABS, MSG_ROWS, 128), i32(SLABS)),
        in_specs=[HBM] * 5,
        out_specs=(VMEM, SMEM),
        scratch_shapes=[
            pltpu.SMEM((NBOX,), jnp.int32),
            pltpu.SMEM((SLABS,), jnp.int32),
            pltpu.SMEM((NBOX,), jnp.int32),
            pltpu.VMEM((FIELDS, ROWS, BOX_DEV * BX), jnp.float32),
            pltpu.VMEM((FIELDS, ROWS // 2, PPD * BX // 2), jnp.float32),
            pltpu.VMEM((BOX_DEV, BOX_ROWS, 128), jnp.float32),
            pltpu.SemaphoreType.DMA((5,)),
        ],
        compiler_params=pltpu.CompilerParams(vmem_limit_bytes=62914560),
    )(old_owner, new_counts, box_pos, fine_old, coarse)
    incoming = lax.all_to_all(outgoing, "slab", 0, 0, tiled=True)
    plan = pl.pallas_call(
        plan_kernel,
        name="plan",
        out_shape=i32(8 * 64),
        in_specs=[SMEM] * 4,
        out_specs=SMEM,
        compiler_params=PARAMS,
    )(old_owner, new_counts, box_pos, starts)
    first_rows, second_rows, sibling = pl.pallas_call(
        edge_kernel,
        name="edges",
        out_shape=(f32(TILES, FIELDS, 128), f32(TILES, FIELDS, 128), f32(4, 8, 128)),
        in_specs=[SMEM, VMEM],
        out_specs=(VMEM, VMEM, VMEM),
        compiler_params=PARAMS,
    )(plan, incoming)
    count = lax.axis_size("sub")
    pairs = [(i, i + 1) for i in range(count - 1)]
    pairs = [pairs[start::2] + [(b, a) for a, b in pairs[start::2]] for start in (1, 0)]
    first_rows = lax.ppermute(first_rows, "sub", pairs[0])
    second_rows = lax.ppermute(second_rows, "sub", pairs[1])
    sibling = lax.ppermute(sibling, "slab", [(i, i ^ 1) for i in range(SLABS)])
    cells = (TILES, FIELDS, ROWS, 128)
    cen, across, slope = pl.pallas_call(
        middle_kernel,
        name="middle",
        out_shape=(f32(*cells), f32(*cells), f32(TILES, ROWS, 128)),
        in_specs=[SMEM, VMEM],
        out_specs=(VMEM, VMEM, VMEM),
        scratch_shapes=[
            pltpu.VMEM((4, ROWS, 128), jnp.float32),
            pltpu.VMEM((2, FIELDS, ROWS, 128), jnp.float32),
        ],
        cost_estimate=pl.CostEstimate(flops=8_000_000, bytes_accessed=8_000_000, transcendentals=0),
        compiler_params=PARAMS,
    )(plan, incoming)
    return pl.pallas_call(
        step_kernel,
        name="step",
        out_shape=f32(FIELDS, ROWS, MOST * BX),
        in_specs=[SMEM] + [VMEM] * 6,
        out_specs=HBM,
        scratch_shapes=[
            pltpu.VMEM((FIELDS, ROWS, MOST * BX), jnp.float32),
            pltpu.VMEM((4, ROWS, 128), jnp.float32),
            pltpu.SemaphoreType.DMA((PARTS,)),
        ],
        compiler_params=PARAMS,
    )(plan, cen, across, slope, sibling, first_rows, second_rows)


def solution(mesh):
    placed = (P(None, "sub", "slab"), P(None, "sub", "slab"), P(), P(), P())
    return jax.shard_map(
        body, mesh=mesh, in_specs=placed, out_specs=P(None, "sub", "slab"), check_vma=False
    )
```

```python
import jax
import jax.numpy as jnp
from jax import lax
from jax.experimental import pallas as pl
from jax.experimental.pallas import tpu as pltpu
from jax.sharding import PartitionSpec as P

BX = 64
BOX_DEV = 24
MOST = 48
NBOX = 1536
PPD = 48
NPOS = 3072
SLABS = 64
TILES = MOST // 2
QUARTER = MOST // 4
GU = 12
UU = 24
FIELDS = 4
ROWS = 16
BOX_ROWS = FIELDS * 8
MSG_ROWS = BOX_ROWS + 8

ANISOTROPY = 0.3
TIME_STEP = 0.1
COUPLING = 1.5
SOLUTE_ONE = 0.6
SOLUTE_TWO = -0.4
DIFF_HEAT = 2.0
DIFF_ONE = 0.5
DIFF_TWO = 0.25
LATENT = 0.5
REJECT_ONE = 0.5
REJECT_TWO = -0.3

SRC, FINE_L, FINE_R, OWN_L, OWN_R, SIB_L, SIB_R, MISC = range(8)


def lanes(shape=(8, 128)):
    return lax.broadcasted_iota(jnp.int32, shape, 1)


def pick(cond, a, b):
    return lax.select(cond, jnp.int32(a), jnp.int32(b))


def pack_kernel(
    owner_in, counts_in, pos_in, fine_in, coarse_in, out, starts, owner, counts, pos, fine, coarse, packed, sems
):
    copies = [
        pltpu.make_async_copy(a, b, sems.at[n])
        for n, (a, b) in enumerate(
            ((pos_in, pos), (owner_in, owner), (counts_in, counts), (fine_in, fine), (coarse_in, coarse))
        )
    ]
    for copy in copies:
        copy.start()
    for copy in copies:
        copy.wait()
    me = lax.axis_index("slab")
    lane = lanes()
    low = lane < 64

    for tile in range(BOX_DEV // 2):
        for f in range(FIELDS):
            top = fine[f, 0:8, tile * 128 : tile * 128 + 128]
            bottom = fine[f, 8:16, tile * 128 : tile * 128 + 128]
            packed[2 * tile, f * 8 : f * 8 + 8] = jnp.where(low, top, pltpu.roll(bottom, 64, 1))
            packed[2 * tile + 1, f * 8 : f * 8 + 8] = jnp.where(low, pltpu.roll(top, 64, 1), bottom)

    inner = lane & 31
    group = lane >> 5
    even = (lane & 1) == 0
    firsts = [jnp.zeros((8, 128), jnp.float32) for _ in range(2)]
    lasts = [jnp.zeros((8, 128), jnp.float32) for _ in range(2)]
    for f in range(FIELDS):
        first = jnp.zeros((8, 128), jnp.float32)
        last = jnp.zeros((8, 128), jnp.float32)
        for tile in range(12):
            x = coarse[f, :, tile * 128 : tile * 128 + 128]
            if tile:
                x = pltpu.roll(x, 2 * tile, 1)
            first = jnp.where(inner == 2 * tile, x, first)
            last = jnp.where(inner == (31 + 2 * tile) % 32, x, last)

        def moved(x, shift):
            shift = (f * 32 + shift) % 128
            return pltpu.roll(x, shift, 1) if shift else x

        here = group == f
        first_even = jnp.where(even, moved(first, 0), moved(first, -63))
        first_odd = jnp.where(even, moved(first, -32), moved(first, -95))
        last_even = jnp.where(even, moved(last, -125), moved(last, -62))
        last_odd = jnp.where(even, moved(last, -31), moved(last, -94))
        firsts = [jnp.where(here, a, b) for a, b in zip((first_even, first_odd), firsts)]
        lasts = [jnp.where(here, a, b) for a, b in zip((last_even, last_odd), lasts)]

    block = pick((me & 1) == 0, me + 1, (me + 31) & 63)
    base = block * PPD
    first_box = jnp.int32(0)
    for step in (1024, 512, 256, 128, 64, 32, 16, 8, 4, 2, 1):
        trial = first_box + step
        value = pos[jnp.minimum(trial, NBOX) - 1]
        first_box = pick((trial <= NBOX) & (value < base), trial, first_box)

    def mark(i, words):
        word0, word1 = words
        k = first_box + i
        at = pos[jnp.minimum(k, NBOX - 1)] - base
        good = (k < NBOX) & (at <= PPD)
        bit = jnp.left_shift(jnp.int32(1), at & 31)
        word0 = word0 | pick(good & (at < 32), bit, 0)
        word1 = word1 | pick(good & (at >= 32), bit, 0)
        return word0, word1

    word0, word1 = lax.fori_loop(0, PPD + 1, mark, (jnp.int32(0), jnp.int32(0)), unroll=49)
    for core in range(2):
        joint = 2 * inner + core
        words = jnp.where(joint < 32, word0, word1)
        fine_here = (lax.shift_right_logical(words, joint & 31) & 1) == 1
        edge = jnp.where(fine_here, lasts[core], firsts[core])
        for b in range(core, SLABS, 2):
            out[b, BOX_ROWS:MSG_ROWS] = edge

    def find(i, r):
        return r + pick(owner[i] == me, i, 0)

    residue = lax.fori_loop(0, SLABS, find, jnp.int32(0), unroll=64)

    def fill(b, start):
        starts[b] = start
        k = start - 1 + ((residue - (start - 1)) & 63)
        slot = jnp.clip(k >> 6, 0, BOX_DEV - 1)
        out[b, 0:BOX_ROWS] = packed[slot]
        return start + counts[b]

    lax.fori_loop(0, SLABS, fill, jnp.int32(0), unroll=64)


def plan_kernel(owner, counts, pos, starts, plan):
    me = lax.axis_index("slab")
    mine = me & 1
    start = starts[me]
    plan[MISC * 64] = start
    plan[MISC * 64 + 1] = counts[me]

    def source(i, carry):
        plan[SRC * 64 + i] = owner[(start + i - 2) & 63]
        return carry

    lax.fori_loop(0, MOST + 4, source, 0, unroll=4)

    def code(at, joint, wanted):
        block = (at * 43691) >> 21
        joint = joint + at - block * PPD
        device = pick((block & 1) == 1, block - 1, (block + 33) & 63)
        keep = wanted & ((joint & 1) == mine)
        return pick(keep, device * 32 + (joint >> 1), -1)

    def ghosts(first, left_row, right_row, flags):
        def one(s, carry):
            k = jnp.minimum(first + s, NBOX - 1)
            at = pos[k]
            before = pos[jnp.maximum(k - 1, 0)]
            after = pos[jnp.minimum(k + 1, NBOX - 1)]
            fine_l = before == at - 1
            fine_r = after == at + 1
            if flags:
                plan[FINE_L * 64 + s] = pick(fine_l, 1, 0)
                plan[FINE_R * 64 + s] = pick(fine_r, 1, 0)
            has_l = jnp.logical_not(fine_l) & (k > 0)
            has_r = jnp.logical_not(fine_r) & (k < NBOX - 1)
            plan[left_row * 64 + s] = code(jnp.maximum(at - 1, 0), 1, has_l)
            plan[right_row * 64 + s] = code(jnp.minimum(at + 1, NPOS - 1), 0, has_r)
            return carry

        lax.fori_loop(0, MOST, one, 0, unroll=2)

    ghosts(start, OWN_L, OWN_R, True)
    ghosts(starts[me ^ 1], SIB_L, SIB_R, False)


def gather_edges(plan, inc, left, right):
    lane = lanes()
    inner = lane & 31

    def one(m, carry):
        out = []
        for q, edges in enumerate(carry):
            for row, to in ((left, m), (right, m + QUARTER)):
                code = plan[row * 64 + q * QUARTER + m]
                x = inc[jnp.maximum(code, 0) >> 5, BOX_ROWS:MSG_ROWS]
                x = pltpu.roll(x, (to - (code & 31)) & 127, 1)
                edges = jnp.where((inner == to) & (code >= 0), x, edges)
            out.append(edges)
        return tuple(out)

    zero = jnp.zeros((8, 128), jnp.float32)
    return lax.fori_loop(0, QUARTER, one, (zero,) * 4, unroll=GU)


def edge_kernel(plan, inc, first_rows, second_rows, sibling):
    low = lanes((1, 128)) < 64
    odd = (lax.axis_index("sub") & 1) == 1

    def one(t, carry):
        a = plan[SRC * 64 + 2 + 2 * t]
        b = plan[SRC * 64 + 3 + 2 * t]
        for f in range(FIELDS):
            row = f * 8
            bottom = jnp.where(low, inc[a, row : row + 1], pltpu.roll(inc[b, row : row + 1], 64, 1))
            row = f * 8 + 7
            top = jnp.where(low, pltpu.roll(inc[a, row : row + 1], 64, 1), inc[b, row : row + 1])
            first_rows[t, f : f + 1] = jnp.where(odd, bottom, top)
            second_rows[t, f : f + 1] = jnp.where(odd, top, bottom)
        return carry

    lax.fori_loop(0, TILES, one, 0, unroll=24)
    for n, edges in enumerate(gather_edges(plan, inc, SIB_L, SIB_R)):
        sibling[n] = edges


def advance(center, across, sq_x, south_cells, north_cells):
    laplace = [a + s + n - 4.0 * c for c, a, s, n in zip(center, across, south_cells, north_cells)]
    phase = center[0]
    grad_y = 0.5 * (north_cells[0] - south_cells[0])
    sq_y = grad_y * grad_y
    spread_sum = sq_x + sq_y + 1.0
    anisotropy = 1.0 + ANISOTROPY * (sq_x * sq_x - 6.0 * sq_x * sq_y + sq_y * sq_y) / (
        spread_sum * spread_sum
    )
    couple = center[1] + SOLUTE_ONE * center[2] + SOLUTE_TWO * center[3]
    wall_term = 1.0 - phase * phase
    phase_step = TIME_STEP * (
        anisotropy * anisotropy * laplace[0]
        + phase
        - phase * phase * phase
        - COUPLING * wall_term * wall_term * couple
    )
    return (
        phase + phase_step,
        center[1] + TIME_STEP * DIFF_HEAT * laplace[1] + LATENT * phase_step,
        center[2] + TIME_STEP * DIFF_ONE * laplace[2] + REJECT_ONE * center[2] * phase_step,
        center[3] + TIME_STEP * DIFF_TWO * laplace[3] + REJECT_TWO * center[3] * phase_step,
    )


def whole_rows(coarse_rows, edges):
    row = lax.broadcasted_iota(jnp.int32, (8, 128), 0) >> 1
    for n, x in enumerate(coarse_rows):
        edges[n, 0:8] = jnp.take_along_axis(x, row, axis=0)
        edges[n, 8:16] = jnp.take_along_axis(x, 4 + row, axis=0)


def ghost_source():
    lane = lanes()
    return jnp.where(lane >= 64, 1, 0) + jnp.where((lane & 63) >= 32, QUARTER, 0)


def ghosts_of(edges, t, f, where_from):
    q = (2 * t * 43691) >> 19
    at = where_from + (2 * t - q * QUARTER + 32 * f)
    return jnp.concatenate([jnp.take_along_axis(edges[q, h : h + 8], at, axis=1) for h in (0, 8)], axis=0)


def middle_kernel(plan, inc, cen, across, slope, edges, outside):
    lane = lanes()
    low = lane < 64
    start = plan[MISC * 64]

    def unpack(a, b, put):
        for f in range(FIELDS):
            x = inc[a, f * 8 : f * 8 + 8]
            y = inc[b, f * 8 : f * 8 + 8]
            put(f, 0, jnp.where(low, x, pltpu.roll(y, 64, 1)))
            put(f, 8, jnp.where(low, pltpu.roll(x, 64, 1), y))

    def inside(t, carry):
        def put(f, row, x):
            cen[t, f, row : row + 8] = x

        unpack(plan[SRC * 64 + 2 + 2 * t], plan[SRC * 64 + 3 + 2 * t], put)
        return carry

    lax.fori_loop(0, TILES, inside, 0, unroll=UU)
    for n, s in enumerate((0, MOST + 2)):

        def put(f, row, x):
            outside[n, f, row : row + 8] = x

        unpack(plan[SRC * 64 + s], plan[SRC * 64 + s + 1], put)

    whole_rows(gather_edges(plan, inc, OWN_L, OWN_R), edges)
    lane = lanes((ROWS, 128))
    where_from = ghost_source()

    def one(t, before, after):
        s = 2 * t
        fl0, fl1 = plan[FINE_L * 64 + s] == 1, plan[FINE_L * 64 + s + 1] == 1
        fr0, fr1 = plan[FINE_R * 64 + s] == 1, plan[FINE_R * 64 + s + 1] == 1
        k = start + s
        ghost_w = ((lane == 0) & jnp.logical_not(fl0)) | ((lane == 64) & jnp.logical_not(fl1))
        ghost_e = ((lane == 63) & jnp.logical_not(fr0)) | ((lane == 127) & jnp.logical_not(fr1))
        border = (
            ((lane == 0) & (k == 0))
            | ((lane == 63) & (k == NBOX - 1))
            | ((lane == 127) & (k + 1 == NBOX - 1))
        )
        for f in range(FIELDS):
            c = cen[t, f]
            w = pltpu.roll(jnp.where(lane == 127, before[f], c), 1, 1)
            e = pltpu.roll(jnp.where(lane == 0, after[f], c), 127, 1)
            g = ghosts_of(edges, t, f, where_from)
            g = jnp.where(border, c, g)
            w = jnp.where(ghost_w, g, w)
            e = jnp.where(ghost_e, g, e)
            across[t, f] = w + e
            if f == 0:
                slope[t] = e - w

    def between(t, carry):
        one(t, cen.at[t - 1], cen.at[t + 1])
        return carry

    one(0, outside.at[0], cen.at[1])
    lax.fori_loop(1, TILES - 1, between, 0, unroll=22)
    one(TILES - 1, cen.at[TILES - 2], outside.at[1])


def step_kernel(plan, cen, across, slope, sibling, first_rows, second_rows, out, held, edges, sems):
    sub = lax.axis_index("sub")
    count = plan[MISC * 64 + 1]
    lane = lanes((ROWS, 128))
    row = lax.broadcasted_iota(jnp.int32, (ROWS, 128), 0)
    odd = (sub & 1) == 1
    at_bottom = sub == 0
    at_top = sub == lax.axis_size("sub") - 1
    right = (lane & 63) >= 32
    where_from = ghost_source()
    whole_rows([sibling[n] for n in range(4)], edges)

    def one(t, carry):
        live = jnp.where(lane < 64, 2 * t, 2 * t + 1) < count
        center, sides, south, north = [], [], [], []
        for f in range(FIELDS):
            c = cen[t, f]
            one_side, other_side = first_rows[t, f : f + 1], second_rows[t, f : f + 1]
            below = jnp.where(at_bottom, c[0:1], jnp.where(odd, one_side, other_side))
            above = jnp.where(at_top, c[15:16], jnp.where(odd, other_side, one_side))
            g = ghosts_of(edges, t, f, where_from)
            g = jnp.where(((lane + 1) & 63) < 2, g, 0.0)
            if f == 0:
                grad_x = 0.5 * (slope[t] + jnp.where(right, g, -g))
            center.append(c)
            sides.append(across[t, f] + g)
            south.append(jnp.where(row == 0, below, pltpu.roll(c, 1, 0)))
            north.append(jnp.where(row == ROWS - 1, above, pltpu.roll(c, ROWS - 1, 0)))
        stepped = advance(center, sides, grad_x * grad_x, south, north)
        at = pl.ds(pl.multiple_of(t * 128, 128), 128)
        for f in range(FIELDS):
            held[f, :, at] = jnp.where(live, stepped[f], 0.0)
        return carry

    copies = []
    for part in range(PARTS):
        each = TILES // PARTS
        lax.fori_loop(part * each, (part + 1) * each, one, 0, unroll=UNROLL)
        columns = pl.ds(part * each * 128, each * 128)
        copies.append(pltpu.make_async_copy(held.at[:, :, columns], out.at[:, :, columns], sems.at[part]))
        copies[-1].start()
    for copy in copies:
        copy.wait()


PARTS = 4
UNROLL = 6
SMEM = pl.BlockSpec(memory_space=pltpu.SMEM)
VMEM = pl.BlockSpec(memory_space=pltpu.VMEM)
HBM = pl.BlockSpec(memory_space=pltpu.HBM)
PARAMS = pltpu.CompilerParams(vmem_limit_bytes=32 * 1024 * 1024)


def f32(*shape):
    return jax.ShapeDtypeStruct(shape, jnp.float32)


def i32(*shape):
    return jax.ShapeDtypeStruct(shape, jnp.int32)


def body(fine_old, coarse, box_pos, old_owner, new_counts):
    outgoing, starts = pl.pallas_call(
        pack_kernel,
        name="pack",
        out_shape=(f32(SLABS, MSG_ROWS, 128), i32(SLABS)),
        in_specs=[HBM] * 5,
        out_specs=(VMEM, SMEM),
        scratch_shapes=[
            pltpu.SMEM((NBOX,), jnp.int32),
            pltpu.SMEM((SLABS,), jnp.int32),
            pltpu.SMEM((NBOX,), jnp.int32),
            pltpu.VMEM((FIELDS, ROWS, BOX_DEV * BX), jnp.float32),
            pltpu.VMEM((FIELDS, ROWS // 2, PPD * BX // 2), jnp.float32),
            pltpu.VMEM((BOX_DEV, BOX_ROWS, 128), jnp.float32),
            pltpu.SemaphoreType.DMA((5,)),
        ],
        compiler_params=pltpu.CompilerParams(vmem_limit_bytes=62914560),
    )(old_owner, new_counts, box_pos, fine_old, coarse)
    incoming = lax.all_to_all(outgoing, "slab", 0, 0, tiled=True)
    plan = pl.pallas_call(
        plan_kernel,
        name="plan",
        out_shape=i32(8 * 64),
        in_specs=[SMEM] * 4,
        out_specs=SMEM,
        compiler_params=PARAMS,
    )(old_owner, new_counts, box_pos, starts)
    first_rows, second_rows, sibling = pl.pallas_call(
        edge_kernel,
        name="edges",
        out_shape=(f32(TILES, FIELDS, 128), f32(TILES, FIELDS, 128), f32(4, 8, 128)),
        in_specs=[SMEM, VMEM],
        out_specs=(VMEM, VMEM, VMEM),
        compiler_params=PARAMS,
    )(plan, incoming)
    count = lax.axis_size("sub")
    pairs = [(i, i + 1) for i in range(count - 1)]
    pairs = [pairs[start::2] + [(b, a) for a, b in pairs[start::2]] for start in (0, 1)]
    first_rows = lax.ppermute(first_rows, "sub", pairs[0])
    second_rows = lax.ppermute(second_rows, "sub", pairs[1])
    sibling = lax.ppermute(sibling, "slab", [(i, i ^ 1) for i in range(SLABS)])
    cells = (TILES, FIELDS, ROWS, 128)
    cen, across, slope = pl.pallas_call(
        middle_kernel,
        name="middle",
        out_shape=(f32(*cells), f32(*cells), f32(TILES, ROWS, 128)),
        in_specs=[SMEM, VMEM],
        out_specs=(VMEM, VMEM, VMEM),
        scratch_shapes=[
            pltpu.VMEM((4, ROWS, 128), jnp.float32),
            pltpu.VMEM((2, FIELDS, ROWS, 128), jnp.float32),
        ],
        cost_estimate=pl.CostEstimate(flops=8_000_000, bytes_accessed=8_000_000, transcendentals=0),
        compiler_params=PARAMS,
    )(plan, incoming)
    return pl.pallas_call(
        step_kernel,
        name="step",
        out_shape=f32(FIELDS, ROWS, MOST * BX),
        in_specs=[SMEM] + [VMEM] * 6,
        out_specs=HBM,
        scratch_shapes=[
            pltpu.VMEM((FIELDS, ROWS, MOST * BX), jnp.float32),
            pltpu.VMEM((4, ROWS, 128), jnp.float32),
            pltpu.SemaphoreType.DMA((PARTS,)),
        ],
        compiler_params=PARAMS,
    )(plan, cen, across, slope, sibling, first_rows, second_rows)


def solution(mesh):
    placed = (P(None, "sub", "slab"), P(None, "sub", "slab"), P(), P(), P())
    return jax.shard_map(
        body, mesh=mesh, in_specs=placed, out_specs=P(None, "sub", "slab"), check_vma=False
    )
```

```python
import jax
import jax.numpy as jnp
from jax import lax
from jax.experimental import pallas as pl
from jax.experimental.pallas import tpu as pltpu
from jax.sharding import PartitionSpec as P

BX = 64
BOX_DEV = 24
MOST = 48
NBOX = 1536
PPD = 48
NPOS = 3072
SLABS = 64
TILES = MOST // 2
QUARTER = MOST // 4
GU = 12
UU = 24
FIELDS = 4
ROWS = 16
BOX_ROWS = FIELDS * 8
MSG_ROWS = BOX_ROWS + 8

ANISOTROPY = 0.3
TIME_STEP = 0.1
COUPLING = 1.5
SOLUTE_ONE = 0.6
SOLUTE_TWO = -0.4
DIFF_HEAT = 2.0
DIFF_ONE = 0.5
DIFF_TWO = 0.25
LATENT = 0.5
REJECT_ONE = 0.5
REJECT_TWO = -0.3

SRC, FINE_L, FINE_R, OWN_L, OWN_R, SIB_L, SIB_R, MISC = range(8)


def lanes(shape=(8, 128)):
    return lax.broadcasted_iota(jnp.int32, shape, 1)


def pick(cond, a, b):
    return lax.select(cond, jnp.int32(a), jnp.int32(b))


def pack_kernel(
    owner_in, counts_in, pos_in, fine_in, coarse_in, out, starts, owner, counts, pos, fine, coarse, packed, sems
):
    copies = [
        pltpu.make_async_copy(a, b, sems.at[n])
        for n, (a, b) in enumerate(
            ((pos_in, pos), (owner_in, owner), (counts_in, counts), (fine_in, fine), (coarse_in, coarse))
        )
    ]
    for copy in copies:
        copy.start()
    for copy in copies:
        copy.wait()
    me = lax.axis_index("slab")
    lane = lanes()
    low = lane < 64

    for tile in range(BOX_DEV // 2):
        for f in range(FIELDS):
            top = fine[f, 0:8, tile * 128 : tile * 128 + 128]
            bottom = fine[f, 8:16, tile * 128 : tile * 128 + 128]
            packed[2 * tile, f * 8 : f * 8 + 8] = jnp.where(low, top, pltpu.roll(bottom, 64, 1))
            packed[2 * tile + 1, f * 8 : f * 8 + 8] = jnp.where(low, pltpu.roll(top, 64, 1), bottom)

    inner = lane & 31
    group = lane >> 5
    even = (lane & 1) == 0
    firsts = [jnp.zeros((8, 128), jnp.float32) for _ in range(2)]
    lasts = [jnp.zeros((8, 128), jnp.float32) for _ in range(2)]
    for f in range(FIELDS):
        first = jnp.zeros((8, 128), jnp.float32)
        last = jnp.zeros((8, 128), jnp.float32)
        for tile in range(12):
            x = coarse[f, :, tile * 128 : tile * 128 + 128]
            if tile:
                x = pltpu.roll(x, 2 * tile, 1)
            first = jnp.where(inner == 2 * tile, x, first)
            last = jnp.where(inner == (31 + 2 * tile) % 32, x, last)

        def moved(x, shift):
            shift = (f * 32 + shift) % 128
            return pltpu.roll(x, shift, 1) if shift else x

        here = group == f
        first_even = jnp.where(even, moved(first, 0), moved(first, -63))
        first_odd = jnp.where(even, moved(first, -32), moved(first, -95))
        last_even = jnp.where(even, moved(last, -125), moved(last, -62))
        last_odd = jnp.where(even, moved(last, -31), moved(last, -94))
        firsts = [jnp.where(here, a, b) for a, b in zip((first_even, first_odd), firsts)]
        lasts = [jnp.where(here, a, b) for a, b in zip((last_even, last_odd), lasts)]

    block = pick((me & 1) == 0, me + 1, (me + 31) & 63)
    base = block * PPD
    first_box = jnp.int32(0)
    for step in (1024, 512, 256, 128, 64, 32, 16, 8, 4, 2, 1):
        trial = first_box + step
        value = pos[jnp.minimum(trial, NBOX) - 1]
        first_box = pick((trial <= NBOX) & (value < base), trial, first_box)

    def mark(i, words):
        word0, word1 = words
        k = first_box + i
        at = pos[jnp.minimum(k, NBOX - 1)] - base
        good = (k < NBOX) & (at <= PPD)
        bit = jnp.left_shift(jnp.int32(1), at & 31)
        word0 = word0 | pick(good & (at < 32), bit, 0)
        word1 = word1 | pick(good & (at >= 32), bit, 0)
        return word0, word1

    word0, word1 = lax.fori_loop(0, PPD + 1, mark, (jnp.int32(0), jnp.int32(0)), unroll=49)
    for core in range(2):
        joint = 2 * inner + core
        words = jnp.where(joint < 32, word0, word1)
        fine_here = (lax.shift_right_logical(words, joint & 31) & 1) == 1
        edge = jnp.where(fine_here, lasts[core], firsts[core])
        for b in range(core, SLABS, 2):
            out[b, BOX_ROWS:MSG_ROWS] = edge

    def find(i, r):
        return r + pick(owner[i] == me, i, 0)

    residue = lax.fori_loop(0, SLABS, find, jnp.int32(0), unroll=64)

    def fill(b, start):
        starts[b] = start
        k = start - 1 + ((residue - (start - 1)) & 63)
        slot = jnp.clip(k >> 6, 0, BOX_DEV - 1)
        out[b, 0:BOX_ROWS] = packed[slot]
        return start + counts[b]

    lax.fori_loop(0, SLABS, fill, jnp.int32(0), unroll=32)


def plan_kernel(owner, counts, pos, starts, plan):
    me = lax.axis_index("slab")
    mine = me & 1
    start = starts[me]
    plan[MISC * 64] = start
    plan[MISC * 64 + 1] = counts[me]

    def source(i, carry):
        plan[SRC * 64 + i] = owner[(start + i - 2) & 63]
        return carry

    lax.fori_loop(0, MOST + 4, source, 0, unroll=4)

    def code(at, joint, wanted):
        block = (at * 43691) >> 21
        joint = joint + at - block * PPD
        device = pick((block & 1) == 1, block - 1, (block + 33) & 63)
        keep = wanted & ((joint & 1) == mine)
        return pick(keep, device * 32 + (joint >> 1), -1)

    def ghosts(first, left_row, right_row, flags):
        def one(s, carry):
            k = jnp.minimum(first + s, NBOX - 1)
            at = pos[k]
            before = pos[jnp.maximum(k - 1, 0)]
            after = pos[jnp.minimum(k + 1, NBOX - 1)]
            fine_l = before == at - 1
            fine_r = after == at + 1
            if flags:
                plan[FINE_L * 64 + s] = pick(fine_l, 1, 0)
                plan[FINE_R * 64 + s] = pick(fine_r, 1, 0)
            has_l = jnp.logical_not(fine_l) & (k > 0)
            has_r = jnp.logical_not(fine_r) & (k < NBOX - 1)
            plan[left_row * 64 + s] = code(jnp.maximum(at - 1, 0), 1, has_l)
            plan[right_row * 64 + s] = code(jnp.minimum(at + 1, NPOS - 1), 0, has_r)
            return carry

        lax.fori_loop(0, MOST, one, 0, unroll=2)

    ghosts(start, OWN_L, OWN_R, True)
    ghosts(starts[me ^ 1], SIB_L, SIB_R, False)


def gather_edges(plan, inc, left, right):
    lane = lanes()
    inner = lane & 31

    def one(m, carry):
        out = []
        for q, edges in enumerate(carry):
            for row, to in ((left, m), (right, m + QUARTER)):
                code = plan[row * 64 + q * QUARTER + m]
                x = inc[jnp.maximum(code, 0) >> 5, BOX_ROWS:MSG_ROWS]
                x = pltpu.roll(x, (to - (code & 31)) & 127, 1)
                edges = jnp.where((inner == to) & (code >= 0), x, edges)
            out.append(edges)
        return tuple(out)

    zero = jnp.zeros((8, 128), jnp.float32)
    return lax.fori_loop(0, QUARTER, one, (zero,) * 4, unroll=GU)


def edge_kernel(plan, inc, low_rows, high_rows, sibling):
    low = lanes((FIELDS, 128)) < 64

    def one(t, carry):
        a = plan[SRC * 64 + 2 + 2 * t]
        b = plan[SRC * 64 + 3 + 2 * t]
        bottoms = [inc[s, pl.ds(0, FIELDS, stride=8)] for s in (a, b)]
        tops = [inc[s, pl.ds(7, FIELDS, stride=8)] for s in (a, b)]
        low_rows[t] = jnp.where(low, bottoms[0], pltpu.roll(bottoms[1], 64, 1))
        high_rows[t] = jnp.where(low, pltpu.roll(tops[0], 64, 1), tops[1])
        return carry

    lax.fori_loop(0, TILES, one, 0, unroll=24)
    for n, edges in enumerate(gather_edges(plan, inc, SIB_L, SIB_R)):
        sibling[n] = edges


def advance(center, across, sq_x, south_cells, north_cells):
    laplace = [a + s + n - 4.0 * c for c, a, s, n in zip(center, across, south_cells, north_cells)]
    phase = center[0]
    grad_y = 0.5 * (north_cells[0] - south_cells[0])
    sq_y = grad_y * grad_y
    spread_sum = sq_x + sq_y + 1.0
    anisotropy = 1.0 + ANISOTROPY * (sq_x * sq_x - 6.0 * sq_x * sq_y + sq_y * sq_y) / (
        spread_sum * spread_sum
    )
    couple = center[1] + SOLUTE_ONE * center[2] + SOLUTE_TWO * center[3]
    wall_term = 1.0 - phase * phase
    phase_step = TIME_STEP * (
        anisotropy * anisotropy * laplace[0]
        + phase
        - phase * phase * phase
        - COUPLING * wall_term * wall_term * couple
    )
    return (
        phase + phase_step,
        center[1] + TIME_STEP * DIFF_HEAT * laplace[1] + LATENT * phase_step,
        center[2] + TIME_STEP * DIFF_ONE * laplace[2] + REJECT_ONE * center[2] * phase_step,
        center[3] + TIME_STEP * DIFF_TWO * laplace[3] + REJECT_TWO * center[3] * phase_step,
    )


def whole_rows(coarse_rows, edges):
    row = lax.broadcasted_iota(jnp.int32, (8, 128), 0) >> 1
    for n, x in enumerate(coarse_rows):
        edges[n, 0:8] = jnp.take_along_axis(x, row, axis=0)
        edges[n, 8:16] = jnp.take_along_axis(x, 4 + row, axis=0)


def ghost_source():
    lane = lanes()
    return jnp.where(lane >= 64, 1, 0) + jnp.where((lane & 63) >= 32, QUARTER, 0)


def ghosts_of(edges, t, f, where_from):
    q = (2 * t * 43691) >> 19
    at = where_from + (2 * t - q * QUARTER + 32 * f)
    return jnp.concatenate([jnp.take_along_axis(edges[q, h : h + 8], at, axis=1) for h in (0, 8)], axis=0)


def middle_kernel(plan, inc, cen, across, slope, edges, outside):
    lane = lanes()
    low = lane < 64
    start = plan[MISC * 64]

    def unpack(a, b, put):
        for f in range(FIELDS):
            x = inc[a, f * 8 : f * 8 + 8]
            y = inc[b, f * 8 : f * 8 + 8]
            put(f, 0, jnp.where(low, x, pltpu.roll(y, 64, 1)))
            put(f, 8, jnp.where(low, pltpu.roll(x, 64, 1), y))

    def inside(t, carry):
        def put(f, row, x):
            cen[t, f, row : row + 8] = x

        unpack(plan[SRC * 64 + 2 + 2 * t], plan[SRC * 64 + 3 + 2 * t], put)
        return carry

    lax.fori_loop(0, TILES, inside, 0, unroll=UU)
    for n, s in enumerate((0, MOST + 2)):

        def put(f, row, x):
            outside[n, f, row : row + 8] = x

        unpack(plan[SRC * 64 + s], plan[SRC * 64 + s + 1], put)

    whole_rows(gather_edges(plan, inc, OWN_L, OWN_R), edges)
    lane = lanes((ROWS, 128))
    where_from = ghost_source()

    def one(t, before, after):
        s = 2 * t
        fl0, fl1 = plan[FINE_L * 64 + s] == 1, plan[FINE_L * 64 + s + 1] == 1
        fr0, fr1 = plan[FINE_R * 64 + s] == 1, plan[FINE_R * 64 + s + 1] == 1
        k = start + s
        ghost_w = ((lane == 0) & jnp.logical_not(fl0)) | ((lane == 64) & jnp.logical_not(fl1))
        ghost_e = ((lane == 63) & jnp.logical_not(fr0)) | ((lane == 127) & jnp.logical_not(fr1))
        border = (
            ((lane == 0) & (k == 0))
            | ((lane == 63) & (k == NBOX - 1))
            | ((lane == 127) & (k + 1 == NBOX - 1))
        )
        for f in range(FIELDS):
            c = cen[t, f]
            w = pltpu.roll(jnp.where(lane == 127, before[f], c), 1, 1)
            e = pltpu.roll(jnp.where(lane == 0, after[f], c), 127, 1)
            g = ghosts_of(edges, t, f, where_from)
            g = jnp.where(border, c, g)
            w = jnp.where(ghost_w, g, w)
            e = jnp.where(ghost_e, g, e)
            across[t, f] = w + e
            if f == 0:
                slope[t] = e - w

    def between(t, carry):
        one(t, cen.at[t - 1], cen.at[t + 1])
        return carry

    one(0, outside.at[0], cen.at[1])
    lax.fori_loop(1, TILES - 1, between, 0, unroll=22)
    one(TILES - 1, cen.at[TILES - 2], outside.at[1])


def step_kernel(plan, cen, across, slope, sibling, from_below, from_above, out, held, edges, sems):
    sub = lax.axis_index("sub")
    count = plan[MISC * 64 + 1]
    lane = lanes((ROWS, 128))
    row = lax.broadcasted_iota(jnp.int32, (ROWS, 128), 0)
    at_bottom = sub == 0
    at_top = sub == lax.axis_size("sub") - 1
    right = (lane & 63) >= 32
    where_from = ghost_source()
    whole_rows([sibling[n] for n in range(4)], edges)

    def one(t, carry):
        live = jnp.where(lane < 64, 2 * t, 2 * t + 1) < count
        center, sides, south, north = [], [], [], []
        for f in range(FIELDS):
            c = cen[t, f]
            below = jnp.where(at_bottom, c[0:1], from_below[t, f : f + 1])
            above = jnp.where(at_top, c[15:16], from_above[t, f : f + 1])
            g = ghosts_of(edges, t, f, where_from)
            g = jnp.where(((lane + 1) & 63) < 2, g, 0.0)
            if f == 0:
                grad_x = 0.5 * (slope[t] + jnp.where(right, g, -g))
            center.append(c)
            sides.append(across[t, f] + g)
            south.append(jnp.where(row == 0, below, pltpu.roll(c, 1, 0)))
            north.append(jnp.where(row == ROWS - 1, above, pltpu.roll(c, ROWS - 1, 0)))
        stepped = advance(center, sides, grad_x * grad_x, south, north)
        at = pl.ds(pl.multiple_of(t * 128, 128), 128)
        for f in range(FIELDS):
            held[f, :, at] = jnp.where(live, stepped[f], 0.0)
        return carry

    copies = []
    for part in range(PARTS):
        each = TILES // PARTS
        lax.fori_loop(part * each, (part + 1) * each, one, 0, unroll=UNROLL)
        columns = pl.ds(part * each * 128, each * 128)
        copies.append(pltpu.make_async_copy(held.at[:, :, columns], out.at[:, :, columns], sems.at[part]))
        copies[-1].start()
    for copy in copies:
        copy.wait()


PARTS = 4
UNROLL = 6
SMEM = pl.BlockSpec(memory_space=pltpu.SMEM)
VMEM = pl.BlockSpec(memory_space=pltpu.VMEM)
HBM = pl.BlockSpec(memory_space=pltpu.HBM)
PARAMS = pltpu.CompilerParams(vmem_limit_bytes=32 * 1024 * 1024)


def f32(*shape):
    return jax.ShapeDtypeStruct(shape, jnp.float32)


def i32(*shape):
    return jax.ShapeDtypeStruct(shape, jnp.int32)


def body(fine_old, coarse, box_pos, old_owner, new_counts):
    outgoing, starts = pl.pallas_call(
        pack_kernel,
        name="pack",
        out_shape=(f32(SLABS, MSG_ROWS, 128), i32(SLABS)),
        in_specs=[HBM] * 5,
        out_specs=(VMEM, SMEM),
        scratch_shapes=[
            pltpu.SMEM((NBOX,), jnp.int32),
            pltpu.SMEM((SLABS,), jnp.int32),
            pltpu.SMEM((NBOX,), jnp.int32),
            pltpu.VMEM((FIELDS, ROWS, BOX_DEV * BX), jnp.float32),
            pltpu.VMEM((FIELDS, ROWS // 2, PPD * BX // 2), jnp.float32),
            pltpu.VMEM((BOX_DEV, BOX_ROWS, 128), jnp.float32),
            pltpu.SemaphoreType.DMA((5,)),
        ],
        compiler_params=pltpu.CompilerParams(vmem_limit_bytes=62914560),
    )(old_owner, new_counts, box_pos, fine_old, coarse)
    incoming = lax.all_to_all(outgoing, "slab", 0, 0, tiled=True)
    plan = pl.pallas_call(
        plan_kernel,
        name="plan",
        out_shape=i32(8 * 64),
        in_specs=[SMEM] * 4,
        out_specs=SMEM,
        compiler_params=PARAMS,
    )(old_owner, new_counts, box_pos, starts)
    low_rows, high_rows, sibling = pl.pallas_call(
        edge_kernel,
        name="edges",
        out_shape=(f32(TILES, FIELDS, 128), f32(TILES, FIELDS, 128), f32(4, 8, 128)),
        in_specs=[SMEM, VMEM],
        out_specs=(VMEM, VMEM, VMEM),
        compiler_params=PARAMS,
    )(plan, incoming)
    count = lax.axis_size("sub")
    up = [(i, i + 1) for i in range(count - 1)]
    sibling = lax.ppermute(sibling, "slab", [(i, i ^ 1) for i in range(SLABS)])
    from_above = lax.ppermute(low_rows, "sub", [(b, a) for a, b in up])
    from_below = lax.ppermute(high_rows, "sub", up)
    cells = (TILES, FIELDS, ROWS, 128)
    cen, across, slope = pl.pallas_call(
        middle_kernel,
        name="middle",
        out_shape=(f32(*cells), f32(*cells), f32(TILES, ROWS, 128)),
        in_specs=[SMEM, VMEM],
        out_specs=(VMEM, VMEM, VMEM),
        scratch_shapes=[
            pltpu.VMEM((4, ROWS, 128), jnp.float32),
            pltpu.VMEM((2, FIELDS, ROWS, 128), jnp.float32),
        ],
        cost_estimate=pl.CostEstimate(flops=8_000_000, bytes_accessed=8_000_000, transcendentals=0),
        compiler_params=PARAMS,
    )(plan, incoming)
    return pl.pallas_call(
        step_kernel,
        name="step",
        out_shape=f32(FIELDS, ROWS, MOST * BX),
        in_specs=[SMEM] + [VMEM] * 6,
        out_specs=HBM,
        scratch_shapes=[
            pltpu.VMEM((FIELDS, ROWS, MOST * BX), jnp.float32),
            pltpu.VMEM((4, ROWS, 128), jnp.float32),
            pltpu.SemaphoreType.DMA((PARTS,)),
        ],
        compiler_params=PARAMS,
    )(plan, cen, across, slope, sibling, from_below, from_above)


def solution(mesh):
    placed = (P(None, "sub", "slab"), P(None, "sub", "slab"), P(), P(), P())
    return jax.shard_map(
        body, mesh=mesh, in_specs=placed, out_specs=P(None, "sub", "slab"), check_vma=False
    )
```

```python
import jax
import jax.numpy as jnp
from jax import lax
from jax.experimental import pallas as pl
from jax.experimental.pallas import tpu as pltpu
from jax.sharding import PartitionSpec as P

BX = 64
BOX_DEV = 24
MOST = 48
NBOX = 1536
PPD = 48
NPOS = 3072
SLABS = 64
TILES = MOST // 2
QUARTER = MOST // 4
GU = 12
UU = 24
FIELDS = 4
ROWS = 16
BOX_ROWS = FIELDS * 8
MSG_ROWS = BOX_ROWS + 8

ANISOTROPY = 0.3
TIME_STEP = 0.1
COUPLING = 1.5
SOLUTE_ONE = 0.6
SOLUTE_TWO = -0.4
DIFF_HEAT = 2.0
DIFF_ONE = 0.5
DIFF_TWO = 0.25
LATENT = 0.5
REJECT_ONE = 0.5
REJECT_TWO = -0.3

SRC, FINE_L, FINE_R, OWN_L, OWN_R, SIB_L, SIB_R, MISC = range(8)


def lanes(shape=(8, 128)):
    return lax.broadcasted_iota(jnp.int32, shape, 1)


def pick(cond, a, b):
    return lax.select(cond, jnp.int32(a), jnp.int32(b))


def pack_kernel(
    owner_in, counts_in, pos_in, fine_in, coarse_in, out, starts, owner, counts, pos, fine, coarse, packed, sems
):
    copies = [
        pltpu.make_async_copy(a, b, sems.at[n])
        for n, (a, b) in enumerate(
            ((pos_in, pos), (owner_in, owner), (counts_in, counts), (fine_in, fine), (coarse_in, coarse))
        )
    ]
    for copy in copies:
        copy.start()
    for copy in copies:
        copy.wait()
    me = lax.axis_index("slab")
    lane = lanes()
    low = lane < 64

    for tile in range(BOX_DEV // 2):
        for f in range(FIELDS):
            top = fine[f, 0:8, tile * 128 : tile * 128 + 128]
            bottom = fine[f, 8:16, tile * 128 : tile * 128 + 128]
            packed[2 * tile, f * 8 : f * 8 + 8] = jnp.where(low, top, pltpu.roll(bottom, 64, 1))
            packed[2 * tile + 1, f * 8 : f * 8 + 8] = jnp.where(low, pltpu.roll(top, 64, 1), bottom)

    inner = lane & 31
    group = lane >> 5
    even = (lane & 1) == 0
    firsts = [jnp.zeros((8, 128), jnp.float32) for _ in range(2)]
    lasts = [jnp.zeros((8, 128), jnp.float32) for _ in range(2)]
    for f in range(FIELDS):
        first = jnp.zeros((8, 128), jnp.float32)
        last = jnp.zeros((8, 128), jnp.float32)
        for tile in range(12):
            x = coarse[f, :, tile * 128 : tile * 128 + 128]
            if tile:
                x = pltpu.roll(x, 2 * tile, 1)
            first = jnp.where(inner == 2 * tile, x, first)
            last = jnp.where(inner == (31 + 2 * tile) % 32, x, last)

        def moved(x, shift):
            shift = (f * 32 + shift) % 128
            return pltpu.roll(x, shift, 1) if shift else x

        here = group == f
        first_even = jnp.where(even, moved(first, 0), moved(first, -63))
        first_odd = jnp.where(even, moved(first, -32), moved(first, -95))
        last_even = jnp.where(even, moved(last, -125), moved(last, -62))
        last_odd = jnp.where(even, moved(last, -31), moved(last, -94))
        firsts = [jnp.where(here, a, b) for a, b in zip((first_even, first_odd), firsts)]
        lasts = [jnp.where(here, a, b) for a, b in zip((last_even, last_odd), lasts)]

    block = pick((me & 1) == 0, me + 1, (me + 31) & 63)
    base = block * PPD
    first_box = jnp.int32(0)
    for step in (1024, 512, 256, 128, 64, 32, 16, 8, 4, 2, 1):
        trial = first_box + step
        value = pos[jnp.minimum(trial, NBOX) - 1]
        first_box = pick((trial <= NBOX) & (value < base), trial, first_box)

    def mark(i, words):
        word0, word1 = words
        k = first_box + i
        at = pos[jnp.minimum(k, NBOX - 1)] - base
        good = (k < NBOX) & (at <= PPD)
        bit = jnp.left_shift(jnp.int32(1), at & 31)
        word0 = word0 | pick(good & (at < 32), bit, 0)
        word1 = word1 | pick(good & (at >= 32), bit, 0)
        return word0, word1

    word0, word1 = lax.fori_loop(0, PPD + 1, mark, (jnp.int32(0), jnp.int32(0)), unroll=49)
    for core in range(2):
        joint = 2 * inner + core
        words = jnp.where(joint < 32, word0, word1)
        fine_here = (lax.shift_right_logical(words, joint & 31) & 1) == 1
        edge = jnp.where(fine_here, lasts[core], firsts[core])
        for b in range(core, SLABS, 2):
            out[b, BOX_ROWS:MSG_ROWS] = edge

    def find(i, r):
        return r + pick(owner[i] == me, i, 0)

    residue = lax.fori_loop(0, SLABS, find, jnp.int32(0), unroll=64)

    def fill(b, start):
        starts[b] = start
        k = start - 1 + ((residue - (start - 1)) & 63)
        slot = jnp.clip(k >> 6, 0, BOX_DEV - 1)
        out[b, 0:BOX_ROWS] = packed[slot]
        return start + counts[b]

    lax.fori_loop(0, SLABS, fill, jnp.int32(0), unroll=32)


def plan_kernel(owner, counts, pos, starts, plan):
    me = lax.axis_index("slab")
    mine = me & 1
    start = starts[me]
    plan[MISC * 64] = start
    plan[MISC * 64 + 1] = counts[me]

    def source(i, carry):
        plan[SRC * 64 + i] = owner[(start + i - 2) & 63]
        return carry

    lax.fori_loop(0, MOST + 4, source, 0, unroll=4)

    def code(at, joint, wanted):
        block = (at * 43691) >> 21
        joint = joint + at - block * PPD
        device = pick((block & 1) == 1, block - 1, (block + 33) & 63)
        keep = wanted & ((joint & 1) == mine)
        return pick(keep, device * 32 + (joint >> 1), -1)

    def ghosts(first, left_row, right_row, flags):
        def one(s, carry):
            k = jnp.minimum(first + s, NBOX - 1)
            at = pos[k]
            before = pos[jnp.maximum(k - 1, 0)]
            after = pos[jnp.minimum(k + 1, NBOX - 1)]
            fine_l = before == at - 1
            fine_r = after == at + 1
            if flags:
                plan[FINE_L * 64 + s] = pick(fine_l, 1, 0)
                plan[FINE_R * 64 + s] = pick(fine_r, 1, 0)
            has_l = jnp.logical_not(fine_l) & (k > 0)
            has_r = jnp.logical_not(fine_r) & (k < NBOX - 1)
            plan[left_row * 64 + s] = code(jnp.maximum(at - 1, 0), 1, has_l)
            plan[right_row * 64 + s] = code(jnp.minimum(at + 1, NPOS - 1), 0, has_r)
            return carry

        lax.fori_loop(0, MOST, one, 0, unroll=2)

    ghosts(start, OWN_L, OWN_R, True)
    ghosts(starts[me ^ 1], SIB_L, SIB_R, False)


def gather_edges(plan, inc, left, right):
    lane = lanes()
    inner = lane & 31

    def one(m, carry):
        out = []
        for q, edges in enumerate(carry):
            for row, to in ((left, m), (right, m + QUARTER)):
                code = plan[row * 64 + q * QUARTER + m]
                x = inc[jnp.maximum(code, 0) >> 5, BOX_ROWS:MSG_ROWS]
                x = pltpu.roll(x, (to - (code & 31)) & 127, 1)
                edges = jnp.where((inner == to) & (code >= 0), x, edges)
            out.append(edges)
        return tuple(out)

    zero = jnp.zeros((8, 128), jnp.float32)
    return lax.fori_loop(0, QUARTER, one, (zero,) * 4, unroll=GU)


def edge_kernel(plan, inc, low_rows, high_rows, sibling):
    low = lanes((FIELDS, 128)) < 64

    def one(t, carry):
        a = plan[SRC * 64 + 2 + 2 * t]
        b = plan[SRC * 64 + 3 + 2 * t]
        bottoms = [inc[s, pl.ds(0, FIELDS, stride=8)] for s in (a, b)]
        tops = [inc[s, pl.ds(7, FIELDS, stride=8)] for s in (a, b)]
        low_rows[t] = jnp.where(low, bottoms[0], pltpu.roll(bottoms[1], 64, 1))
        high_rows[t] = jnp.where(low, pltpu.roll(tops[0], 64, 1), tops[1])
        return carry

    lax.fori_loop(0, TILES, one, 0, unroll=24)
    for n, edges in enumerate(gather_edges(plan, inc, SIB_L, SIB_R)):
        sibling[n] = edges


def advance(center, across, sq_x, south_cells, north_cells):
    laplace = [a + s + n - 4.0 * c for c, a, s, n in zip(center, across, south_cells, north_cells)]
    phase = center[0]
    grad_y = 0.5 * (north_cells[0] - south_cells[0])
    sq_y = grad_y * grad_y
    spread_sum = sq_x + sq_y + 1.0
    anisotropy = 1.0 + ANISOTROPY * (sq_x * sq_x - 6.0 * sq_x * sq_y + sq_y * sq_y) / (
        spread_sum * spread_sum
    )
    couple = center[1] + SOLUTE_ONE * center[2] + SOLUTE_TWO * center[3]
    wall_term = 1.0 - phase * phase
    phase_step = TIME_STEP * (
        anisotropy * anisotropy * laplace[0]
        + phase
        - phase * phase * phase
        - COUPLING * wall_term * wall_term * couple
    )
    return (
        phase + phase_step,
        center[1] + TIME_STEP * DIFF_HEAT * laplace[1] + LATENT * phase_step,
        center[2] + TIME_STEP * DIFF_ONE * laplace[2] + REJECT_ONE * center[2] * phase_step,
        center[3] + TIME_STEP * DIFF_TWO * laplace[3] + REJECT_TWO * center[3] * phase_step,
    )


def whole_rows(coarse_rows, edges):
    row = lax.broadcasted_iota(jnp.int32, (8, 128), 0) >> 1
    for n, x in enumerate(coarse_rows):
        edges[n, 0:8] = jnp.take_along_axis(x, row, axis=0)
        edges[n, 8:16] = jnp.take_along_axis(x, 4 + row, axis=0)


def ghost_source():
    lane = lanes()
    return jnp.where(lane >= 64, 1, 0) + jnp.where((lane & 63) >= 32, QUARTER, 0)


def ghosts_of(edges, t, f, where_from):
    q = (2 * t * 43691) >> 19
    at = where_from + (2 * t - q * QUARTER + 32 * f)
    return jnp.concatenate([jnp.take_along_axis(edges[q, h : h + 8], at, axis=1) for h in (0, 8)], axis=0)


def middle_kernel(plan, inc, cen, across, slope, edges, outside):
    lane = lanes()
    low = lane < 64
    start = plan[MISC * 64]

    def unpack(a, b, put):
        for f in range(FIELDS):
            x = inc[a, f * 8 : f * 8 + 8]
            y = inc[b, f * 8 : f * 8 + 8]
            put(f, 0, jnp.where(low, x, pltpu.roll(y, 64, 1)))
            put(f, 8, jnp.where(low, pltpu.roll(x, 64, 1), y))

    def inside(t, carry):
        def put(f, row, x):
            cen[t, f, row : row + 8] = x

        unpack(plan[SRC * 64 + 2 + 2 * t], plan[SRC * 64 + 3 + 2 * t], put)
        return carry

    lax.fori_loop(0, TILES, inside, 0, unroll=UU)
    for n, s in enumerate((0, MOST + 2)):

        def put(f, row, x):
            outside[n, f, row : row + 8] = x

        unpack(plan[SRC * 64 + s], plan[SRC * 64 + s + 1], put)

    whole_rows(gather_edges(plan, inc, OWN_L, OWN_R), edges)
    lane = lanes((ROWS, 128))
    where_from = ghost_source()

    def one(t, before, after):
        s = 2 * t
        fl0, fl1 = plan[FINE_L * 64 + s] == 1, plan[FINE_L * 64 + s + 1] == 1
        fr0, fr1 = plan[FINE_R * 64 + s] == 1, plan[FINE_R * 64 + s + 1] == 1
        k = start + s
        ghost_w = ((lane == 0) & jnp.logical_not(fl0)) | ((lane == 64) & jnp.logical_not(fl1))
        ghost_e = ((lane == 63) & jnp.logical_not(fr0)) | ((lane == 127) & jnp.logical_not(fr1))
        border = (
            ((lane == 0) & (k == 0))
            | ((lane == 63) & (k == NBOX - 1))
            | ((lane == 127) & (k + 1 == NBOX - 1))
        )
        for f in range(FIELDS):
            c = cen[t, f]
            w = pltpu.roll(jnp.where(lane == 127, before[f], c), 1, 1)
            e = pltpu.roll(jnp.where(lane == 0, after[f], c), 127, 1)
            g = ghosts_of(edges, t, f, where_from)
            g = jnp.where(border, c, g)
            w = jnp.where(ghost_w, g, w)
            e = jnp.where(ghost_e, g, e)
            across[t, f] = w + e
            if f == 0:
                slope[t] = e - w

    def between(t, carry):
        one(t, cen.at[t - 1], cen.at[t + 1])
        return carry

    one(0, outside.at[0], cen.at[1])
    lax.fori_loop(1, TILES - 1, between, 0, unroll=22)
    one(TILES - 1, cen.at[TILES - 2], outside.at[1])


def step_kernel(plan, cen, across, slope, sibling, from_above, from_below, out, held, edges, sems):
    sub = lax.axis_index("sub")
    count = plan[MISC * 64 + 1]
    lane = lanes((ROWS, 128))
    row = lax.broadcasted_iota(jnp.int32, (ROWS, 128), 0)
    at_bottom = sub == 0
    at_top = sub == lax.axis_size("sub") - 1
    right = (lane & 63) >= 32
    where_from = ghost_source()
    whole_rows([sibling[n] for n in range(4)], edges)

    def one(t, carry):
        live = jnp.where(lane < 64, 2 * t, 2 * t + 1) < count
        center, sides, south, north = [], [], [], []
        for f in range(FIELDS):
            c = cen[t, f]
            below = jnp.where(at_bottom, c[0:1], from_below[t, f : f + 1])
            above = jnp.where(at_top, c[15:16], from_above[t, f : f + 1])
            g = ghosts_of(edges, t, f, where_from)
            g = jnp.where(((lane + 1) & 63) < 2, g, 0.0)
            if f == 0:
                grad_x = 0.5 * (slope[t] + jnp.where(right, g, -g))
            center.append(c)
            sides.append(across[t, f] + g)
            south.append(jnp.where(row == 0, below, pltpu.roll(c, 1, 0)))
            north.append(jnp.where(row == ROWS - 1, above, pltpu.roll(c, ROWS - 1, 0)))
        stepped = advance(center, sides, grad_x * grad_x, south, north)
        at = pl.ds(pl.multiple_of(t * 128, 128), 128)
        for f in range(FIELDS):
            held[f, :, at] = jnp.where(live, stepped[f], 0.0)
        return carry

    copies = []
    for part in range(PARTS):
        each = TILES // PARTS
        lax.fori_loop(part * each, (part + 1) * each, one, 0, unroll=UNROLL)
        columns = pl.ds(part * each * 128, each * 128)
        copies.append(pltpu.make_async_copy(held.at[:, :, columns], out.at[:, :, columns], sems.at[part]))
        copies[-1].start()
    for copy in copies:
        copy.wait()


PARTS = 4
UNROLL = 6
SMEM = pl.BlockSpec(memory_space=pltpu.SMEM)
VMEM = pl.BlockSpec(memory_space=pltpu.VMEM)
HBM = pl.BlockSpec(memory_space=pltpu.HBM)
PARAMS = pltpu.CompilerParams(vmem_limit_bytes=32 * 1024 * 1024)


def f32(*shape):
    return jax.ShapeDtypeStruct(shape, jnp.float32)


def i32(*shape):
    return jax.ShapeDtypeStruct(shape, jnp.int32)


def body(fine_old, coarse, box_pos, old_owner, new_counts):
    outgoing, starts = pl.pallas_call(
        pack_kernel,
        name="pack",
        out_shape=(f32(SLABS, MSG_ROWS, 128), i32(SLABS)),
        in_specs=[HBM] * 5,
        out_specs=(VMEM, SMEM),
        scratch_shapes=[
            pltpu.SMEM((NBOX,), jnp.int32),
            pltpu.SMEM((SLABS,), jnp.int32),
            pltpu.SMEM((NBOX,), jnp.int32),
            pltpu.VMEM((FIELDS, ROWS, BOX_DEV * BX), jnp.float32),
            pltpu.VMEM((FIELDS, ROWS // 2, PPD * BX // 2), jnp.float32),
            pltpu.VMEM((BOX_DEV, BOX_ROWS, 128), jnp.float32),
            pltpu.SemaphoreType.DMA((5,)),
        ],
        compiler_params=pltpu.CompilerParams(vmem_limit_bytes=62914560),
    )(old_owner, new_counts, box_pos, fine_old, coarse)
    incoming = lax.all_to_all(outgoing, "slab", 0, 0, tiled=True)
    plan = pl.pallas_call(
        plan_kernel,
        name="plan",
        out_shape=i32(8 * 64),
        in_specs=[SMEM] * 4,
        out_specs=SMEM,
        compiler_params=PARAMS,
    )(old_owner, new_counts, box_pos, starts)
    low_rows, high_rows, sibling = pl.pallas_call(
        edge_kernel,
        name="edges",
        out_shape=(f32(TILES, FIELDS, 128), f32(TILES, FIELDS, 128), f32(4, 8, 128)),
        in_specs=[SMEM, VMEM],
        out_specs=(VMEM, VMEM, VMEM),
        compiler_params=PARAMS,
    )(plan, incoming)
    count = lax.axis_size("sub")
    up = [(i, i + 1) for i in range(count - 1)]
    sibling = lax.ppermute(sibling, "slab", [(i, i ^ 1) for i in range(SLABS)])
    from_above = lax.ppermute(low_rows, "sub", [(b, a) for a, b in up])
    from_below = lax.ppermute(high_rows, "sub", up)
    cells = (TILES, FIELDS, ROWS, 128)
    cen, across, slope = pl.pallas_call(
        middle_kernel,
        name="middle",
        out_shape=(f32(*cells), f32(*cells), f32(TILES, ROWS, 128)),
        in_specs=[SMEM, VMEM],
        out_specs=(VMEM, VMEM, VMEM),
        scratch_shapes=[
            pltpu.VMEM((4, ROWS, 128), jnp.float32),
            pltpu.VMEM((2, FIELDS, ROWS, 128), jnp.float32),
        ],
        cost_estimate=pl.CostEstimate(flops=8_000_000, bytes_accessed=8_000_000, transcendentals=0),
        compiler_params=PARAMS,
    )(plan, incoming)
    return pl.pallas_call(
        step_kernel,
        name="step",
        out_shape=f32(FIELDS, ROWS, MOST * BX),
        in_specs=[SMEM] + [VMEM] * 6,
        out_specs=HBM,
        scratch_shapes=[
            pltpu.VMEM((FIELDS, ROWS, MOST * BX), jnp.float32),
            pltpu.VMEM((4, ROWS, 128), jnp.float32),
            pltpu.SemaphoreType.DMA((PARTS,)),
        ],
        compiler_params=PARAMS,
    )(plan, cen, across, slope, sibling, from_above, from_below)


def solution(mesh):
    placed = (P(None, "sub", "slab"), P(None, "sub", "slab"), P(), P(), P())
    return jax.shard_map(
        body, mesh=mesh, in_specs=placed, out_specs=P(None, "sub", "slab"), check_vma=False
    )
```

```python
import jax
import jax.numpy as jnp
from jax import lax
from jax.experimental import pallas as pl
from jax.experimental.pallas import tpu as pltpu
from jax.sharding import PartitionSpec as P

BX = 64
BOX_DEV = 24
MOST = 48
NBOX = 1536
PPD = 48
NPOS = 3072
SLABS = 64
TILES = MOST // 2
QUARTER = MOST // 4
GU = 12
UU = 24
FIELDS = 4
ROWS = 16
BOX_ROWS = FIELDS * 8
MSG_ROWS = BOX_ROWS + 8

ANISOTROPY = 0.3
TIME_STEP = 0.1
COUPLING = 1.5
SOLUTE_ONE = 0.6
SOLUTE_TWO = -0.4
DIFF_HEAT = 2.0
DIFF_ONE = 0.5
DIFF_TWO = 0.25
LATENT = 0.5
REJECT_ONE = 0.5
REJECT_TWO = -0.3

SRC, FINE_L, FINE_R, OWN_L, OWN_R, SIB_L, SIB_R, MISC = range(8)


def lanes(shape=(8, 128)):
    return lax.broadcasted_iota(jnp.int32, shape, 1)


def pick(cond, a, b):
    return lax.select(cond, jnp.int32(a), jnp.int32(b))


def pack_kernel(
    owner_in, counts_in, pos_in, fine_in, coarse_in, out, starts, owner, counts, pos, fine, coarse, packed, sems
):
    copies = [
        pltpu.make_async_copy(a, b, sems.at[n])
        for n, (a, b) in enumerate(
            ((pos_in, pos), (owner_in, owner), (counts_in, counts), (fine_in, fine), (coarse_in, coarse))
        )
    ]
    for copy in copies:
        copy.start()
    for copy in copies:
        copy.wait()
    me = lax.axis_index("slab")
    lane = lanes()
    low = lane < 64

    for tile in range(BOX_DEV // 2):
        for f in range(FIELDS):
            top = fine[f, 0:8, tile * 128 : tile * 128 + 128]
            bottom = fine[f, 8:16, tile * 128 : tile * 128 + 128]
            packed[2 * tile, f * 8 : f * 8 + 8] = jnp.where(low, top, pltpu.roll(bottom, 64, 1))
            packed[2 * tile + 1, f * 8 : f * 8 + 8] = jnp.where(low, pltpu.roll(top, 64, 1), bottom)

    inner = lane & 31
    group = lane >> 5
    even = (lane & 1) == 0
    firsts = [jnp.zeros((8, 128), jnp.float32) for _ in range(2)]
    lasts = [jnp.zeros((8, 128), jnp.float32) for _ in range(2)]
    for f in range(FIELDS):
        first = jnp.zeros((8, 128), jnp.float32)
        last = jnp.zeros((8, 128), jnp.float32)
        for tile in range(12):
            x = coarse[f, :, tile * 128 : tile * 128 + 128]
            if tile:
                x = pltpu.roll(x, 2 * tile, 1)
            first = jnp.where(inner == 2 * tile, x, first)
            last = jnp.where(inner == (31 + 2 * tile) % 32, x, last)

        def moved(x, shift):
            shift = (f * 32 + shift) % 128
            return pltpu.roll(x, shift, 1) if shift else x

        here = group == f
        first_even = jnp.where(even, moved(first, 0), moved(first, -63))
        first_odd = jnp.where(even, moved(first, -32), moved(first, -95))
        last_even = jnp.where(even, moved(last, -125), moved(last, -62))
        last_odd = jnp.where(even, moved(last, -31), moved(last, -94))
        firsts = [jnp.where(here, a, b) for a, b in zip((first_even, first_odd), firsts)]
        lasts = [jnp.where(here, a, b) for a, b in zip((last_even, last_odd), lasts)]

    block = pick((me & 1) == 0, me + 1, (me + 31) & 63)
    base = block * PPD
    first_box = jnp.int32(0)
    for step in (1024, 512, 256, 128, 64, 32, 16, 8, 4, 2, 1):
        trial = first_box + step
        value = pos[jnp.minimum(trial, NBOX) - 1]
        first_box = pick((trial <= NBOX) & (value < base), trial, first_box)

    def mark(i, words):
        word0, word1 = words
        k = first_box + i
        at = pos[jnp.minimum(k, NBOX - 1)] - base
        good = (k < NBOX) & (at <= PPD)
        bit = jnp.left_shift(jnp.int32(1), at & 31)
        word0 = word0 | pick(good & (at < 32), bit, 0)
        word1 = word1 | pick(good & (at >= 32), bit, 0)
        return word0, word1

    word0, word1 = lax.fori_loop(0, PPD + 1, mark, (jnp.int32(0), jnp.int32(0)), unroll=49)
    for core in range(2):
        joint = 2 * inner + core
        words = jnp.where(joint < 32, word0, word1)
        fine_here = (lax.shift_right_logical(words, joint & 31) & 1) == 1
        edge = jnp.where(fine_here, lasts[core], firsts[core])
        for b in range(core, SLABS, 2):
            out[b, BOX_ROWS:MSG_ROWS] = edge

    def find(i, r):
        return r + pick(owner[i] == me, i, 0)

    residue = lax.fori_loop(0, SLABS, find, jnp.int32(0), unroll=64)

    def fill(b, start):
        starts[b] = start
        k = start - 1 + ((residue - (start - 1)) & 63)
        slot = jnp.clip(k >> 6, 0, BOX_DEV - 1)
        out[b, 0:BOX_ROWS] = packed[slot]
        return start + counts[b]

    lax.fori_loop(0, SLABS, fill, jnp.int32(0), unroll=32)


def plan_kernel(owner, counts, pos, starts, plan):
    me = lax.axis_index("slab")
    mine = me & 1
    start = starts[me]
    plan[MISC * 64] = start
    plan[MISC * 64 + 1] = counts[me]

    def source(i, carry):
        plan[SRC * 64 + i] = owner[(start + i - 2) & 63]
        return carry

    lax.fori_loop(0, MOST + 4, source, 0, unroll=4)

    def code(at, joint, wanted):
        block = (at * 43691) >> 21
        joint = joint + at - block * PPD
        device = pick((block & 1) == 1, block - 1, (block + 33) & 63)
        keep = wanted & ((joint & 1) == mine)
        return pick(keep, device * 32 + (joint >> 1), -1)

    def ghosts(first, left_row, right_row, flags):
        def one(s, carry):
            k = jnp.minimum(first + s, NBOX - 1)
            at = pos[k]
            before = pos[jnp.maximum(k - 1, 0)]
            after = pos[jnp.minimum(k + 1, NBOX - 1)]
            fine_l = before == at - 1
            fine_r = after == at + 1
            if flags:
                plan[FINE_L * 64 + s] = pick(fine_l, 1, 0)
                plan[FINE_R * 64 + s] = pick(fine_r, 1, 0)
            has_l = jnp.logical_not(fine_l) & (k > 0)
            has_r = jnp.logical_not(fine_r) & (k < NBOX - 1)
            plan[left_row * 64 + s] = code(jnp.maximum(at - 1, 0), 1, has_l)
            plan[right_row * 64 + s] = code(jnp.minimum(at + 1, NPOS - 1), 0, has_r)
            return carry

        lax.fori_loop(0, MOST, one, 0, unroll=2)

    ghosts(start, OWN_L, OWN_R, True)
    ghosts(starts[me ^ 1], SIB_L, SIB_R, False)


def gather_edges(plan, inc, left, right):
    lane = lanes()
    inner = lane & 31

    def one(m, carry):
        out = []
        for q, edges in enumerate(carry):
            for row, to in ((left, m), (right, m + QUARTER)):
                code = plan[row * 64 + q * QUARTER + m]
                x = inc[jnp.maximum(code, 0) >> 5, BOX_ROWS:MSG_ROWS]
                x = pltpu.roll(x, (to - (code & 31)) & 127, 1)
                edges = jnp.where((inner == to) & (code >= 0), x, edges)
            out.append(edges)
        return tuple(out)

    zero = jnp.zeros((8, 128), jnp.float32)
    return lax.fori_loop(0, QUARTER, one, (zero,) * 4, unroll=GU)


def edge_kernel(plan, inc, low_rows, high_rows, sibling):
    low = lanes((FIELDS, 128)) < 64

    def one(t, carry):
        a = plan[SRC * 64 + 2 + 2 * t]
        b = plan[SRC * 64 + 3 + 2 * t]
        bottoms = [inc[s, pl.ds(0, FIELDS, stride=8)] for s in (a, b)]
        tops = [inc[s, pl.ds(7, FIELDS, stride=8)] for s in (a, b)]
        low_rows[t] = jnp.where(low, bottoms[0], pltpu.roll(bottoms[1], 64, 1))
        high_rows[t] = jnp.where(low, pltpu.roll(tops[0], 64, 1), tops[1])
        return carry

    lax.fori_loop(0, TILES, one, 0, unroll=24)
    for n, edges in enumerate(gather_edges(plan, inc, SIB_L, SIB_R)):
        sibling[n] = edges


def advance(center, across, sq_x, south_cells, north_cells):
    laplace = [a + s + n - 4.0 * c for c, a, s, n in zip(center, across, south_cells, north_cells)]
    phase = center[0]
    grad_y = 0.5 * (north_cells[0] - south_cells[0])
    sq_y = grad_y * grad_y
    spread_sum = sq_x + sq_y + 1.0
    anisotropy = 1.0 + ANISOTROPY * (sq_x * sq_x - 6.0 * sq_x * sq_y + sq_y * sq_y) / (
        spread_sum * spread_sum
    )
    couple = center[1] + SOLUTE_ONE * center[2] + SOLUTE_TWO * center[3]
    wall_term = 1.0 - phase * phase
    phase_step = TIME_STEP * (
        anisotropy * anisotropy * laplace[0]
        + phase
        - phase * phase * phase
        - COUPLING * wall_term * wall_term * couple
    )
    return (
        phase + phase_step,
        center[1] + TIME_STEP * DIFF_HEAT * laplace[1] + LATENT * phase_step,
        center[2] + TIME_STEP * DIFF_ONE * laplace[2] + REJECT_ONE * center[2] * phase_step,
        center[3] + TIME_STEP * DIFF_TWO * laplace[3] + REJECT_TWO * center[3] * phase_step,
    )


def whole_rows(coarse_rows, edges):
    row = lax.broadcasted_iota(jnp.int32, (8, 128), 0) >> 1
    for n, x in enumerate(coarse_rows):
        edges[n, 0:8] = jnp.take_along_axis(x, row, axis=0)
        edges[n, 8:16] = jnp.take_along_axis(x, 4 + row, axis=0)


def ghost_source():
    lane = lanes()
    return jnp.where(lane >= 64, 1, 0) + jnp.where((lane & 63) >= 32, QUARTER, 0)


def ghosts_of(edges, t, f, where_from):
    q = (2 * t * 43691) >> 19
    at = where_from + (2 * t - q * QUARTER + 32 * f)
    return jnp.concatenate([jnp.take_along_axis(edges[q, h : h + 8], at, axis=1) for h in (0, 8)], axis=0)


def middle_kernel(plan, inc, cen, across, slope, alive, edges, outside):
    lane = lanes()
    low = lane < 64
    start = plan[MISC * 64]

    def unpack(a, b, put):
        for f in range(FIELDS):
            x = inc[a, f * 8 : f * 8 + 8]
            y = inc[b, f * 8 : f * 8 + 8]
            put(f, 0, jnp.where(low, x, pltpu.roll(y, 64, 1)))
            put(f, 8, jnp.where(low, pltpu.roll(x, 64, 1), y))

    def inside(t, carry):
        def put(f, row, x):
            cen[t, f, row : row + 8] = x

        unpack(plan[SRC * 64 + 2 + 2 * t], plan[SRC * 64 + 3 + 2 * t], put)
        return carry

    lax.fori_loop(0, TILES, inside, 0, unroll=UU)
    for n, s in enumerate((0, MOST + 2)):

        def put(f, row, x):
            outside[n, f, row : row + 8] = x

        unpack(plan[SRC * 64 + s], plan[SRC * 64 + s + 1], put)

    whole_rows(gather_edges(plan, inc, OWN_L, OWN_R), edges)
    lane = lanes((ROWS, 128))
    where_from = ghost_source()
    count = plan[MISC * 64 + 1]
    slot = lax.broadcasted_iota(jnp.int32, (TILES, 128), 0) * 2 + (lanes((TILES, 128)) >> 6)
    alive[...] = jnp.where(slot < count, 1.0, 0.0)

    def one(t, before, after):
        s = 2 * t
        fl0, fl1 = plan[FINE_L * 64 + s] == 1, plan[FINE_L * 64 + s + 1] == 1
        fr0, fr1 = plan[FINE_R * 64 + s] == 1, plan[FINE_R * 64 + s + 1] == 1
        k = start + s
        ghost_w = ((lane == 0) & jnp.logical_not(fl0)) | ((lane == 64) & jnp.logical_not(fl1))
        ghost_e = ((lane == 63) & jnp.logical_not(fr0)) | ((lane == 127) & jnp.logical_not(fr1))
        border = (
            ((lane == 0) & (k == 0))
            | ((lane == 63) & (k == NBOX - 1))
            | ((lane == 127) & (k + 1 == NBOX - 1))
        )
        for f in range(FIELDS):
            c = cen[t, f]
            w = pltpu.roll(jnp.where(lane == 127, before[f], c), 1, 1)
            e = pltpu.roll(jnp.where(lane == 0, after[f], c), 127, 1)
            g = ghosts_of(edges, t, f, where_from)
            g = jnp.where(border, c, g)
            w = jnp.where(ghost_w, g, w)
            e = jnp.where(ghost_e, g, e)
            across[t, f] = w + e
            if f == 0:
                slope[t] = e - w

    def between(t, carry):
        one(t, cen.at[t - 1], cen.at[t + 1])
        return carry

    one(0, outside.at[0], cen.at[1])
    lax.fori_loop(1, TILES - 1, between, 0, unroll=22)
    one(TILES - 1, cen.at[TILES - 2], outside.at[1])


def step_kernel(cen, across, slope, alive, sibling, from_below, from_above, out, held, edges, sems):
    sub = lax.axis_index("sub")
    lane = lanes((ROWS, 128))
    row = lax.broadcasted_iota(jnp.int32, (ROWS, 128), 0)
    at_bottom = sub == 0
    at_top = sub == lax.axis_size("sub") - 1
    right = (lane & 63) >= 32
    where_from = ghost_source()
    whole_rows([sibling[n] for n in range(4)], edges)

    def one(t, carry):
        live = jnp.broadcast_to(alive[pl.ds(t, 1)], (ROWS, 128)) == 1.0
        center, sides, south, north = [], [], [], []
        for f in range(FIELDS):
            c = cen[t, f]
            below = jnp.where(at_bottom, c[0:1], from_below[t, f : f + 1])
            above = jnp.where(at_top, c[15:16], from_above[t, f : f + 1])
            g = ghosts_of(edges, t, f, where_from)
            g = jnp.where(((lane + 1) & 63) < 2, g, 0.0)
            if f == 0:
                grad_x = 0.5 * (slope[t] + jnp.where(right, g, -g))
            center.append(c)
            sides.append(across[t, f] + g)
            south.append(jnp.where(row == 0, below, pltpu.roll(c, 1, 0)))
            north.append(jnp.where(row == ROWS - 1, above, pltpu.roll(c, ROWS - 1, 0)))
        stepped = advance(center, sides, grad_x * grad_x, south, north)
        at = pl.ds(pl.multiple_of(t * 128, 128), 128)
        for f in range(FIELDS):
            held[f, :, at] = jnp.where(live, stepped[f], 0.0)
        return carry

    copies = []
    for part in range(PARTS):
        each = TILES // PARTS
        lax.fori_loop(part * each, (part + 1) * each, one, 0, unroll=UNROLL)
        columns = pl.ds(part * each * 128, each * 128)
        copies.append(pltpu.make_async_copy(held.at[:, :, columns], out.at[:, :, columns], sems.at[part]))
        copies[-1].start()
    for copy in copies:
        copy.wait()


PARTS = 4
UNROLL = 6
SMEM = pl.BlockSpec(memory_space=pltpu.SMEM)
VMEM = pl.BlockSpec(memory_space=pltpu.VMEM)
HBM = pl.BlockSpec(memory_space=pltpu.HBM)
PARAMS = pltpu.CompilerParams(vmem_limit_bytes=32 * 1024 * 1024)


def f32(*shape):
    return jax.ShapeDtypeStruct(shape, jnp.float32)


def i32(*shape):
    return jax.ShapeDtypeStruct(shape, jnp.int32)


def body(fine_old, coarse, box_pos, old_owner, new_counts):
    outgoing, starts = pl.pallas_call(
        pack_kernel,
        name="pack",
        out_shape=(f32(SLABS, MSG_ROWS, 128), i32(SLABS)),
        in_specs=[HBM] * 5,
        out_specs=(VMEM, SMEM),
        scratch_shapes=[
            pltpu.SMEM((NBOX,), jnp.int32),
            pltpu.SMEM((SLABS,), jnp.int32),
            pltpu.SMEM((NBOX,), jnp.int32),
            pltpu.VMEM((FIELDS, ROWS, BOX_DEV * BX), jnp.float32),
            pltpu.VMEM((FIELDS, ROWS // 2, PPD * BX // 2), jnp.float32),
            pltpu.VMEM((BOX_DEV, BOX_ROWS, 128), jnp.float32),
            pltpu.SemaphoreType.DMA((5,)),
        ],
        compiler_params=pltpu.CompilerParams(vmem_limit_bytes=62914560),
    )(old_owner, new_counts, box_pos, fine_old, coarse)
    incoming = lax.all_to_all(outgoing, "slab", 0, 0, tiled=True)
    plan = pl.pallas_call(
        plan_kernel,
        name="plan",
        out_shape=i32(8 * 64),
        in_specs=[SMEM] * 4,
        out_specs=SMEM,
        compiler_params=PARAMS,
    )(old_owner, new_counts, box_pos, starts)
    low_rows, high_rows, sibling = pl.pallas_call(
        edge_kernel,
        name="edges",
        out_shape=(f32(TILES, FIELDS, 128), f32(TILES, FIELDS, 128), f32(4, 8, 128)),
        in_specs=[SMEM, VMEM],
        out_specs=(VMEM, VMEM, VMEM),
        compiler_params=PARAMS,
    )(plan, incoming)
    count = lax.axis_size("sub")
    up = [(i, i + 1) for i in range(count - 1)]
    sibling = lax.ppermute(sibling, "slab", [(i, i ^ 1) for i in range(SLABS)])
    from_above = lax.ppermute(low_rows, "sub", [(b, a) for a, b in up])
    from_below = lax.ppermute(high_rows, "sub", up)
    cells = (TILES, FIELDS, ROWS, 128)
    cen, across, slope, alive = pl.pallas_call(
        middle_kernel,
        name="middle",
        out_shape=(f32(*cells), f32(*cells), f32(TILES, ROWS, 128), f32(TILES, 128)),
        in_specs=[SMEM, VMEM],
        out_specs=(VMEM, VMEM, VMEM, VMEM),
        scratch_shapes=[
            pltpu.VMEM((4, ROWS, 128), jnp.float32),
            pltpu.VMEM((2, FIELDS, ROWS, 128), jnp.float32),
        ],
        cost_estimate=pl.CostEstimate(flops=8_000_000, bytes_accessed=8_000_000, transcendentals=0),
        compiler_params=PARAMS,
    )(plan, incoming)
    return pl.pallas_call(
        step_kernel,
        name="step",
        out_shape=f32(FIELDS, ROWS, MOST * BX),
        in_specs=[VMEM] * 7,
        out_specs=HBM,
        scratch_shapes=[
            pltpu.VMEM((FIELDS, ROWS, MOST * BX), jnp.float32),
            pltpu.VMEM((4, ROWS, 128), jnp.float32),
            pltpu.SemaphoreType.DMA((PARTS,)),
        ],
        compiler_params=PARAMS,
    )(cen, across, slope, alive, sibling, from_below, from_above)


def solution(mesh):
    placed = (P(None, "sub", "slab"), P(None, "sub", "slab"), P(), P(), P())
    return jax.shard_map(
        body, mesh=mesh, in_specs=placed, out_specs=P(None, "sub", "slab"), check_vma=False
    )
```

```python
import jax
import jax.numpy as jnp
from jax import lax
from jax.experimental import pallas as pl
from jax.experimental.pallas import tpu as pltpu
from jax.sharding import PartitionSpec as P

BX = 64
BOX_DEV = 24
MOST = 48
NBOX = 1536
PPD = 48
NPOS = 3072
SLABS = 64
TILES = MOST // 2
QUARTER = MOST // 4
GU = 12
UU = 24
FIELDS = 4
ROWS = 16
BOX_ROWS = FIELDS * 8
MSG_ROWS = BOX_ROWS + 8

ANISOTROPY = 0.3
TIME_STEP = 0.1
COUPLING = 1.5
SOLUTE_ONE = 0.6
SOLUTE_TWO = -0.4
DIFF_HEAT = 2.0
DIFF_ONE = 0.5
DIFF_TWO = 0.25
LATENT = 0.5
REJECT_ONE = 0.5
REJECT_TWO = -0.3

SRC, FINE_L, FINE_R, OWN_L, OWN_R, SIB_L, SIB_R, MISC = range(8)


def lanes(shape=(8, 128)):
    return lax.broadcasted_iota(jnp.int32, shape, 1)


def pick(cond, a, b):
    return lax.select(cond, jnp.int32(a), jnp.int32(b))


def pack_kernel(
    owner_in, counts_in, pos_in, fine_in, coarse_in, out, starts, owner, counts, pos, fine, coarse, packed, sems
):
    copies = [
        pltpu.make_async_copy(a, b, sems.at[n])
        for n, (a, b) in enumerate(
            ((pos_in, pos), (owner_in, owner), (counts_in, counts), (fine_in, fine), (coarse_in, coarse))
        )
    ]
    for copy in copies:
        copy.start()
    for copy in copies:
        copy.wait()
    me = lax.axis_index("slab")
    lane = lanes()
    low = lane < 64

    for tile in range(BOX_DEV // 2):
        for f in range(FIELDS):
            top = fine[f, 0:8, tile * 128 : tile * 128 + 128]
            bottom = fine[f, 8:16, tile * 128 : tile * 128 + 128]
            packed[2 * tile, f * 8 : f * 8 + 8] = jnp.where(low, top, pltpu.roll(bottom, 64, 1))
            packed[2 * tile + 1, f * 8 : f * 8 + 8] = jnp.where(low, pltpu.roll(top, 64, 1), bottom)

    inner = lane & 31
    group = lane >> 5
    even = (lane & 1) == 0
    firsts = [jnp.zeros((8, 128), jnp.float32) for _ in range(2)]
    lasts = [jnp.zeros((8, 128), jnp.float32) for _ in range(2)]
    for f in range(FIELDS):
        first = jnp.zeros((8, 128), jnp.float32)
        last = jnp.zeros((8, 128), jnp.float32)
        for tile in range(12):
            x = coarse[f, :, tile * 128 : tile * 128 + 128]
            if tile:
                x = pltpu.roll(x, 2 * tile, 1)
            first = jnp.where(inner == 2 * tile, x, first)
            last = jnp.where(inner == (31 + 2 * tile) % 32, x, last)

        def moved(x, shift):
            shift = (f * 32 + shift) % 128
            return pltpu.roll(x, shift, 1) if shift else x

        here = group == f
        first_even = jnp.where(even, moved(first, 0), moved(first, -63))
        first_odd = jnp.where(even, moved(first, -32), moved(first, -95))
        last_even = jnp.where(even, moved(last, -125), moved(last, -62))
        last_odd = jnp.where(even, moved(last, -31), moved(last, -94))
        firsts = [jnp.where(here, a, b) for a, b in zip((first_even, first_odd), firsts)]
        lasts = [jnp.where(here, a, b) for a, b in zip((last_even, last_odd), lasts)]

    block = pick((me & 1) == 0, me + 1, (me + 31) & 63)
    base = block * PPD
    first_box = jnp.int32(0)
    for step in (1024, 512, 256, 128, 64, 32, 16, 8, 4, 2, 1):
        trial = first_box + step
        value = pos[jnp.minimum(trial, NBOX) - 1]
        first_box = pick((trial <= NBOX) & (value < base), trial, first_box)

    def mark(i, words):
        word0, word1 = words
        at = pos[jnp.minimum(first_box + i, NBOX - 1)] - base
        bit = jnp.left_shift(jnp.int32(1), at & 31)
        word = at >> 5
        word0 = word0 | pick(word == 0, bit, 0)
        word1 = word1 | pick(word == 1, bit, 0)
        return word0, word1

    word0, word1 = lax.fori_loop(0, PPD + 1, mark, (jnp.int32(0), jnp.int32(0)), unroll=49)
    for core in range(2):
        joint = 2 * inner + core
        words = jnp.where(joint < 32, word0, word1)
        fine_here = (lax.shift_right_logical(words, joint & 31) & 1) == 1
        edge = jnp.where(fine_here, lasts[core], firsts[core])
        for b in range(core, SLABS, 2):
            out[b, BOX_ROWS:MSG_ROWS] = edge

    def find(i, r):
        return r + pick(owner[i] == me, i, 0)

    residue = lax.fori_loop(0, SLABS, find, jnp.int32(0), unroll=64)

    def fill(b, start):
        starts[b] = start
        k = start - 1 + ((residue - (start - 1)) & 63)
        slot = jnp.clip(k >> 6, 0, BOX_DEV - 1)
        out[b, 0:BOX_ROWS] = packed[slot]
        return start + counts[b]

    lax.fori_loop(0, SLABS, fill, jnp.int32(0), unroll=32)


def plan_kernel(owner, counts, pos, starts, plan):
    me = lax.axis_index("slab")
    mine = me & 1
    start = starts[me]
    plan[MISC * 64] = start
    plan[MISC * 64 + 1] = counts[me]

    def source(i, carry):
        plan[SRC * 64 + i] = owner[(start + i - 2) & 63]
        return carry

    lax.fori_loop(0, MOST + 4, source, 0, unroll=4)

    def code(at, joint, wanted):
        block = (at * 43691) >> 21
        joint = joint + at - block * PPD
        device = pick((block & 1) == 1, block - 1, (block + 33) & 63)
        keep = wanted & ((joint & 1) == mine)
        return pick(keep, device * 32 + (joint >> 1), -1)

    def ghosts(first, left_row, right_row, flags):
        def one(s, carry):
            k = jnp.minimum(first + s, NBOX - 1)
            at = pos[k]
            before = pos[jnp.maximum(k - 1, 0)]
            after = pos[jnp.minimum(k + 1, NBOX - 1)]
            fine_l = before == at - 1
            fine_r = after == at + 1
            if flags:
                plan[FINE_L * 64 + s] = pick(fine_l, 1, 0)
                plan[FINE_R * 64 + s] = pick(fine_r, 1, 0)
            has_l = jnp.logical_not(fine_l) & (k > 0)
            has_r = jnp.logical_not(fine_r) & (k < NBOX - 1)
            plan[left_row * 64 + s] = code(jnp.maximum(at - 1, 0), 1, has_l)
            plan[right_row * 64 + s] = code(jnp.minimum(at + 1, NPOS - 1), 0, has_r)
            return carry

        lax.fori_loop(0, MOST, one, 0, unroll=2)

    ghosts(start, OWN_L, OWN_R, True)
    ghosts(starts[me ^ 1], SIB_L, SIB_R, False)


def gather_edges(plan, inc, left, right):
    lane = lanes()
    inner = lane & 31

    def one(m, carry):
        out = []
        for q, edges in enumerate(carry):
            for row, to in ((left, m), (right, m + QUARTER)):
                code = plan[row * 64 + q * QUARTER + m]
                x = inc[jnp.maximum(code, 0) >> 5, BOX_ROWS:MSG_ROWS]
                x = pltpu.roll(x, (to - (code & 31)) & 127, 1)
                edges = jnp.where((inner == to) & (code >= 0), x, edges)
            out.append(edges)
        return tuple(out)

    zero = jnp.zeros((8, 128), jnp.float32)
    return lax.fori_loop(0, QUARTER, one, (zero,) * 4, unroll=GU)


def edge_kernel(plan, inc, low_rows, high_rows):
    low = lanes((FIELDS, 128)) < 64

    def one(t, carry):
        a = plan[SRC * 64 + 2 + 2 * t]
        b = plan[SRC * 64 + 3 + 2 * t]
        bottoms = [inc[s, pl.ds(0, FIELDS, stride=8)] for s in (a, b)]
        tops = [inc[s, pl.ds(7, FIELDS, stride=8)] for s in (a, b)]
        low_rows[t] = jnp.where(low, bottoms[0], pltpu.roll(bottoms[1], 64, 1))
        high_rows[t] = jnp.where(low, pltpu.roll(tops[0], 64, 1), tops[1])
        return carry

    lax.fori_loop(0, TILES, one, 0, unroll=24)


def sibling_kernel(plan, inc, sibling):
    for n, edges in enumerate(gather_edges(plan, inc, SIB_L, SIB_R)):
        sibling[n] = edges


def advance(center, across, sq_x, south_cells, north_cells):
    laplace = [a + s + n - 4.0 * c for c, a, s, n in zip(center, across, south_cells, north_cells)]
    phase = center[0]
    grad_y = 0.5 * (north_cells[0] - south_cells[0])
    sq_y = grad_y * grad_y
    spread_sum = sq_x + sq_y + 1.0
    anisotropy = 1.0 + ANISOTROPY * (sq_x * sq_x - 6.0 * sq_x * sq_y + sq_y * sq_y) / (
        spread_sum * spread_sum
    )
    couple = center[1] + SOLUTE_ONE * center[2] + SOLUTE_TWO * center[3]
    wall_term = 1.0 - phase * phase
    phase_step = TIME_STEP * (
        anisotropy * anisotropy * laplace[0]
        + phase
        - phase * phase * phase
        - COUPLING * wall_term * wall_term * couple
    )
    return (
        phase + phase_step,
        center[1] + TIME_STEP * DIFF_HEAT * laplace[1] + LATENT * phase_step,
        center[2] + TIME_STEP * DIFF_ONE * laplace[2] + REJECT_ONE * center[2] * phase_step,
        center[3] + TIME_STEP * DIFF_TWO * laplace[3] + REJECT_TWO * center[3] * phase_step,
    )


def whole_rows(coarse_rows, edges):
    row = lax.broadcasted_iota(jnp.int32, (8, 128), 0) >> 1
    for n, x in enumerate(coarse_rows):
        edges[n, 0:8] = jnp.take_along_axis(x, row, axis=0)
        edges[n, 8:16] = jnp.take_along_axis(x, 4 + row, axis=0)


def ghost_source():
    lane = lanes()
    return jnp.where(lane >= 64, 1, 0) + jnp.where((lane & 63) >= 32, QUARTER, 0)


def ghosts_of(edges, t, f, where_from):
    q = (2 * t * 43691) >> 19
    at = where_from + (2 * t - q * QUARTER + 32 * f)
    return jnp.concatenate([jnp.take_along_axis(edges[q, h : h + 8], at, axis=1) for h in (0, 8)], axis=0)


def middle_kernel(plan, inc, cen, across, slope, alive, edges, outside):
    lane = lanes()
    low = lane < 64
    start = plan[MISC * 64]

    def unpack(a, b, put):
        for f in range(FIELDS):
            x = inc[a, f * 8 : f * 8 + 8]
            y = inc[b, f * 8 : f * 8 + 8]
            put(f, 0, jnp.where(low, x, pltpu.roll(y, 64, 1)))
            put(f, 8, jnp.where(low, pltpu.roll(x, 64, 1), y))

    def inside(t, carry):
        def put(f, row, x):
            cen[t, f, row : row + 8] = x

        unpack(plan[SRC * 64 + 2 + 2 * t], plan[SRC * 64 + 3 + 2 * t], put)
        return carry

    lax.fori_loop(0, TILES, inside, 0, unroll=UU)
    for n, s in enumerate((0, MOST + 2)):

        def put(f, row, x):
            outside[n, f, row : row + 8] = x

        unpack(plan[SRC * 64 + s], plan[SRC * 64 + s + 1], put)

    whole_rows(gather_edges(plan, inc, OWN_L, OWN_R), edges)
    lane = lanes((ROWS, 128))
    where_from = ghost_source()
    count = plan[MISC * 64 + 1]
    slot = lax.broadcasted_iota(jnp.int32, (TILES, 128), 0) * 2 + (lanes((TILES, 128)) >> 6)
    alive[...] = jnp.where(slot < count, 1.0, 0.0)

    def one(t, before, after):
        s = 2 * t
        fl0, fl1 = plan[FINE_L * 64 + s] == 1, plan[FINE_L * 64 + s + 1] == 1
        fr0, fr1 = plan[FINE_R * 64 + s] == 1, plan[FINE_R * 64 + s + 1] == 1
        k = start + s
        ghost_w = ((lane == 0) & jnp.logical_not(fl0)) | ((lane == 64) & jnp.logical_not(fl1))
        ghost_e = ((lane == 63) & jnp.logical_not(fr0)) | ((lane == 127) & jnp.logical_not(fr1))
        border = (
            ((lane == 0) & (k == 0))
            | ((lane == 63) & (k == NBOX - 1))
            | ((lane == 127) & (k + 1 == NBOX - 1))
        )
        for f in range(FIELDS):
            c = cen[t, f]
            w = pltpu.roll(jnp.where(lane == 127, before[f], c), 1, 1)
            e = pltpu.roll(jnp.where(lane == 0, after[f], c), 127, 1)
            g = ghosts_of(edges, t, f, where_from)
            g = jnp.where(border, c, g)
            w = jnp.where(ghost_w, g, w)
            e = jnp.where(ghost_e, g, e)
            across[t, f] = w + e
            if f == 0:
                slope[t] = e - w

    def between(t, carry):
        one(t, cen.at[t - 1], cen.at[t + 1])
        return carry

    one(0, outside.at[0], cen.at[1])
    lax.fori_loop(1, TILES - 1, between, 0, unroll=22)
    one(TILES - 1, cen.at[TILES - 2], outside.at[1])


def step_kernel(cen, across, slope, alive, sibling, from_below, from_above, out, held, edges, sems):
    sub = lax.axis_index("sub")
    lane = lanes((ROWS, 128))
    row = lax.broadcasted_iota(jnp.int32, (ROWS, 128), 0)
    at_bottom = sub == 0
    at_top = sub == lax.axis_size("sub") - 1
    right = (lane & 63) >= 32
    where_from = ghost_source()
    whole_rows([sibling[n] for n in range(4)], edges)

    def one(t, carry):
        live = jnp.broadcast_to(alive[pl.ds(t, 1)], (ROWS, 128)) == 1.0
        center, sides, south, north = [], [], [], []
        for f in range(FIELDS):
            c = cen[t, f]
            below = jnp.where(at_bottom, c[0:1], from_below[t, f : f + 1])
            above = jnp.where(at_top, c[15:16], from_above[t, f : f + 1])
            g = ghosts_of(edges, t, f, where_from)
            g = jnp.where(((lane + 1) & 63) < 2, g, 0.0)
            if f == 0:
                grad_x = 0.5 * (slope[t] + jnp.where(right, g, -g))
            center.append(c)
            sides.append(across[t, f] + g)
            south.append(jnp.where(row == 0, below, pltpu.roll(c, 1, 0)))
            north.append(jnp.where(row == ROWS - 1, above, pltpu.roll(c, ROWS - 1, 0)))
        stepped = advance(center, sides, grad_x * grad_x, south, north)
        at = pl.ds(pl.multiple_of(t * 128, 128), 128)
        for f in range(FIELDS):
            held[f, :, at] = jnp.where(live, stepped[f], 0.0)
        return carry

    copies = []
    for part in range(PARTS):
        each = TILES // PARTS
        lax.fori_loop(part * each, (part + 1) * each, one, 0, unroll=UNROLL)
        columns = pl.ds(part * each * 128, each * 128)
        copies.append(pltpu.make_async_copy(held.at[:, :, columns], out.at[:, :, columns], sems.at[part]))
        copies[-1].start()
    for copy in copies:
        copy.wait()


PARTS = 4
UNROLL = 6
SMEM = pl.BlockSpec(memory_space=pltpu.SMEM)
VMEM = pl.BlockSpec(memory_space=pltpu.VMEM)
HBM = pl.BlockSpec(memory_space=pltpu.HBM)
PARAMS = pltpu.CompilerParams(vmem_limit_bytes=32 * 1024 * 1024)


def f32(*shape):
    return jax.ShapeDtypeStruct(shape, jnp.float32)


def i32(*shape):
    return jax.ShapeDtypeStruct(shape, jnp.int32)


def body(fine_old, coarse, box_pos, old_owner, new_counts):
    outgoing, starts = pl.pallas_call(
        pack_kernel,
        name="pack",
        out_shape=(f32(SLABS, MSG_ROWS, 128), i32(SLABS)),
        in_specs=[HBM] * 5,
        out_specs=(VMEM, SMEM),
        scratch_shapes=[
            pltpu.SMEM((NBOX,), jnp.int32),
            pltpu.SMEM((SLABS,), jnp.int32),
            pltpu.SMEM((NBOX,), jnp.int32),
            pltpu.VMEM((FIELDS, ROWS, BOX_DEV * BX), jnp.float32),
            pltpu.VMEM((FIELDS, ROWS // 2, PPD * BX // 2), jnp.float32),
            pltpu.VMEM((BOX_DEV, BOX_ROWS, 128), jnp.float32),
            pltpu.SemaphoreType.DMA((5,)),
        ],
        compiler_params=pltpu.CompilerParams(vmem_limit_bytes=62914560),
    )(old_owner, new_counts, box_pos, fine_old, coarse)
    incoming = lax.all_to_all(outgoing, "slab", 0, 0, tiled=True)
    plan = pl.pallas_call(
        plan_kernel,
        name="plan",
        out_shape=i32(8 * 64),
        in_specs=[SMEM] * 4,
        out_specs=SMEM,
        compiler_params=PARAMS,
    )(old_owner, new_counts, box_pos, starts)
    low_rows, high_rows = pl.pallas_call(
        edge_kernel,
        name="edges",
        out_shape=(f32(TILES, FIELDS, 128), f32(TILES, FIELDS, 128)),
        in_specs=[VMEM, VMEM],
        out_specs=(VMEM, VMEM),
        compiler_params=PARAMS,
    )(plan, incoming)
    sibling = pl.pallas_call(
        sibling_kernel,
        name="sibling",
        out_shape=f32(4, 8, 128),
        in_specs=[VMEM, VMEM],
        out_specs=VMEM,
        compiler_params=PARAMS,
    )(plan, incoming)
    count = lax.axis_size("sub")
    up = [(i, i + 1) for i in range(count - 1)]
    sibling = lax.ppermute(sibling, "slab", [(i, i ^ 1) for i in range(SLABS)])
    from_above = lax.ppermute(low_rows, "sub", [(b, a) for a, b in up])
    from_below = lax.ppermute(high_rows, "sub", up)
    cells = (TILES, FIELDS, ROWS, 128)
    cen, across, slope, alive = pl.pallas_call(
        middle_kernel,
        name="middle",
        out_shape=(f32(*cells), f32(*cells), f32(TILES, ROWS, 128), f32(TILES, 128)),
        in_specs=[SMEM, VMEM],
        out_specs=(VMEM, VMEM, VMEM, VMEM),
        scratch_shapes=[
            pltpu.VMEM((4, ROWS, 128), jnp.float32),
            pltpu.VMEM((2, FIELDS, ROWS, 128), jnp.float32),
        ],
        cost_estimate=pl.CostEstimate(flops=8_000_000, bytes_accessed=8_000_000, transcendentals=0),
        compiler_params=PARAMS,
    )(plan, incoming)
    return pl.pallas_call(
        step_kernel,
        name="step",
        out_shape=f32(FIELDS, ROWS, MOST * BX),
        in_specs=[VMEM] * 7,
        out_specs=HBM,
        scratch_shapes=[
            pltpu.VMEM((FIELDS, ROWS, MOST * BX), jnp.float32),
            pltpu.VMEM((4, ROWS, 128), jnp.float32),
            pltpu.SemaphoreType.DMA((PARTS,)),
        ],
        compiler_params=PARAMS,
    )(cen, across, slope, alive, sibling, from_below, from_above)


def solution(mesh):
    placed = (P(None, "sub", "slab"), P(None, "sub", "slab"), P(), P(), P())
    return jax.shard_map(
        body, mesh=mesh, in_specs=placed, out_specs=P(None, "sub", "slab"), check_vma=False
    )
```

```python
import jax
import jax.numpy as jnp
from jax import lax
from jax.experimental import pallas as pl
from jax.experimental.pallas import tpu as pltpu
from jax.sharding import PartitionSpec as P

BX = 64
BOX_DEV = 24
MOST = 48
NBOX = 1536
PPD = 48
NPOS = 3072
SLABS = 64
TILES = MOST // 2
QUARTER = MOST // 4
GU = 12
UU = 24
FIELDS = 4
ROWS = 16
BOX_ROWS = FIELDS * 8
MSG_ROWS = BOX_ROWS + 8

ANISOTROPY = 0.3
TIME_STEP = 0.1
COUPLING = 1.5
SOLUTE_ONE = 0.6
SOLUTE_TWO = -0.4
DIFF_HEAT = 2.0
DIFF_ONE = 0.5
DIFF_TWO = 0.25
LATENT = 0.5
REJECT_ONE = 0.5
REJECT_TWO = -0.3

SRC, FINE_L, FINE_R, OWN_L, OWN_R, SIB_L, SIB_R, MISC = range(8)


def lanes(shape=(8, 128)):
    return lax.broadcasted_iota(jnp.int32, shape, 1)


def pick(cond, a, b):
    return lax.select(cond, jnp.int32(a), jnp.int32(b))


def pack_kernel(
    owner_in, counts_in, pos_in, fine_in, coarse_in, out, owner, counts, pos, fine, coarse, packed, sems
):
    copies = [
        pltpu.make_async_copy(a, b, sems.at[n])
        for n, (a, b) in enumerate(
            ((pos_in, pos), (owner_in, owner), (counts_in, counts), (fine_in, fine), (coarse_in, coarse))
        )
    ]
    for copy in copies:
        copy.start()
    for copy in copies:
        copy.wait()
    me = lax.axis_index("slab")
    lane = lanes()
    low = lane < 64

    for tile in range(BOX_DEV // 2):
        for f in range(FIELDS):
            top = fine[f, 0:8, tile * 128 : tile * 128 + 128]
            bottom = fine[f, 8:16, tile * 128 : tile * 128 + 128]
            packed[2 * tile, f * 8 : f * 8 + 8] = jnp.where(low, top, pltpu.roll(bottom, 64, 1))
            packed[2 * tile + 1, f * 8 : f * 8 + 8] = jnp.where(low, pltpu.roll(top, 64, 1), bottom)

    inner = lane & 31
    group = lane >> 5
    even = (lane & 1) == 0
    firsts = [jnp.zeros((8, 128), jnp.float32) for _ in range(2)]
    lasts = [jnp.zeros((8, 128), jnp.float32) for _ in range(2)]
    for f in range(FIELDS):
        first = jnp.zeros((8, 128), jnp.float32)
        last = jnp.zeros((8, 128), jnp.float32)
        for tile in range(12):
            x = coarse[f, :, tile * 128 : tile * 128 + 128]
            if tile:
                x = pltpu.roll(x, 2 * tile, 1)
            first = jnp.where(inner == 2 * tile, x, first)
            last = jnp.where(inner == (31 + 2 * tile) % 32, x, last)

        def moved(x, shift):
            shift = (f * 32 + shift) % 128
            return pltpu.roll(x, shift, 1) if shift else x

        here = group == f
        first_even = jnp.where(even, moved(first, 0), moved(first, -63))
        first_odd = jnp.where(even, moved(first, -32), moved(first, -95))
        last_even = jnp.where(even, moved(last, -125), moved(last, -62))
        last_odd = jnp.where(even, moved(last, -31), moved(last, -94))
        firsts = [jnp.where(here, a, b) for a, b in zip((first_even, first_odd), firsts)]
        lasts = [jnp.where(here, a, b) for a, b in zip((last_even, last_odd), lasts)]

    block = pick((me & 1) == 0, me + 1, (me + 31) & 63)
    base = block * PPD
    first_box = jnp.int32(0)
    for step in (1024, 512, 256, 128, 64, 32, 16, 8, 4, 2, 1):
        trial = first_box + step
        value = pos[jnp.minimum(trial, NBOX) - 1]
        first_box = pick((trial <= NBOX) & (value < base), trial, first_box)

    def mark(i, words):
        word0, word1 = words
        at = pos[jnp.minimum(first_box + i, NBOX - 1)] - base
        bit = jnp.left_shift(jnp.int32(1), at & 31)
        word = at >> 5
        word0 = word0 | pick(word == 0, bit, 0)
        word1 = word1 | pick(word == 1, bit, 0)
        return word0, word1

    word0, word1 = lax.fori_loop(0, PPD + 1, mark, (jnp.int32(0), jnp.int32(0)), unroll=49)
    for core in range(2):
        joint = 2 * inner + core
        words = jnp.where(joint < 32, word0, word1)
        fine_here = (lax.shift_right_logical(words, joint & 31) & 1) == 1
        edge = jnp.where(fine_here, lasts[core], firsts[core])
        for b in range(core, SLABS, 2):
            out[b, BOX_ROWS:MSG_ROWS] = edge

    def find(i, r):
        return r + pick(owner[i] == me, i, 0)

    residue = lax.fori_loop(0, SLABS, find, jnp.int32(0), unroll=64)

    def fill(b, start):
        k = start - 1 + ((residue - (start - 1)) & 63)
        slot = jnp.clip(k >> 6, 0, BOX_DEV - 1)
        out[b, 0:BOX_ROWS] = packed[slot]
        return start + counts[b]

    lax.fori_loop(0, SLABS, fill, jnp.int32(0), unroll=32)


def plan_kernel(owner, counts, pos, plan):
    me = lax.axis_index("slab")
    mine = me & 1

    def total(b, sums):
        start, other = sums
        n = counts[b]
        return start + pick(b < me, n, 0), other + pick(b < (me ^ 1), n, 0)

    start, other = lax.fori_loop(0, SLABS, total, (jnp.int32(0), jnp.int32(0)), unroll=16)
    plan[MISC * 64] = start
    plan[MISC * 64 + 1] = counts[me]

    def source(i, carry):
        plan[SRC * 64 + i] = owner[(start + i - 2) & 63]
        return carry

    lax.fori_loop(0, MOST + 4, source, 0, unroll=4)

    def code(at, joint, wanted):
        block = (at * 43691) >> 21
        joint = joint + at - block * PPD
        device = pick((block & 1) == 1, block - 1, (block + 33) & 63)
        keep = wanted & ((joint & 1) == mine)
        return pick(keep, device * 32 + (joint >> 1), -1)

    def ghosts(first, left_row, right_row, flags):
        def one(s, carry):
            k = jnp.minimum(first + s, NBOX - 1)
            at = pos[k]
            before = pos[jnp.maximum(k - 1, 0)]
            after = pos[jnp.minimum(k + 1, NBOX - 1)]
            fine_l = before == at - 1
            fine_r = after == at + 1
            if flags:
                plan[FINE_L * 64 + s] = pick(fine_l, 1, 0)
                plan[FINE_R * 64 + s] = pick(fine_r, 1, 0)
            has_l = jnp.logical_not(fine_l) & (k > 0)
            has_r = jnp.logical_not(fine_r) & (k < NBOX - 1)
            plan[left_row * 64 + s] = code(jnp.maximum(at - 1, 0), 1, has_l)
            plan[right_row * 64 + s] = code(jnp.minimum(at + 1, NPOS - 1), 0, has_r)
            return carry

        lax.fori_loop(0, MOST, one, 0, unroll=2)

    ghosts(start, OWN_L, OWN_R, True)
    ghosts(other, SIB_L, SIB_R, False)


def gather_edges(plan, inc, left, right):
    lane = lanes()
    inner = lane & 31

    def one(m, carry):
        out = []
        for q, edges in enumerate(carry):
            for row, to in ((left, m), (right, m + QUARTER)):
                code = plan[row * 64 + q * QUARTER + m]
                x = inc[jnp.maximum(code, 0) >> 5, BOX_ROWS:MSG_ROWS]
                x = pltpu.roll(x, (to - (code & 31)) & 127, 1)
                edges = jnp.where((inner == to) & (code >= 0), x, edges)
            out.append(edges)
        return tuple(out)

    zero = jnp.zeros((8, 128), jnp.float32)
    return lax.fori_loop(0, QUARTER, one, (zero,) * 4, unroll=GU)


def edge_kernel(plan, inc, low_rows, high_rows):
    low = lanes((FIELDS, 128)) < 64

    def one(t, carry):
        a = plan[SRC * 64 + 2 + 2 * t]
        b = plan[SRC * 64 + 3 + 2 * t]
        bottoms = [inc[s, pl.ds(0, FIELDS, stride=8)] for s in (a, b)]
        tops = [inc[s, pl.ds(7, FIELDS, stride=8)] for s in (a, b)]
        low_rows[t] = jnp.where(low, bottoms[0], pltpu.roll(bottoms[1], 64, 1))
        high_rows[t] = jnp.where(low, pltpu.roll(tops[0], 64, 1), tops[1])
        return carry

    lax.fori_loop(0, TILES, one, 0, unroll=24)


def sibling_kernel(plan, inc, sibling):
    for n, edges in enumerate(gather_edges(plan, inc, SIB_L, SIB_R)):
        sibling[n] = edges


def advance(center, across, sq_x, south_cells, north_cells):
    laplace = [a + s + n - 4.0 * c for c, a, s, n in zip(center, across, south_cells, north_cells)]
    phase = center[0]
    grad_y = 0.5 * (north_cells[0] - south_cells[0])
    sq_y = grad_y * grad_y
    spread_sum = sq_x + sq_y + 1.0
    anisotropy = 1.0 + ANISOTROPY * (sq_x * sq_x - 6.0 * sq_x * sq_y + sq_y * sq_y) / (
        spread_sum * spread_sum
    )
    couple = center[1] + SOLUTE_ONE * center[2] + SOLUTE_TWO * center[3]
    wall_term = 1.0 - phase * phase
    phase_step = TIME_STEP * (
        anisotropy * anisotropy * laplace[0]
        + phase
        - phase * phase * phase
        - COUPLING * wall_term * wall_term * couple
    )
    return (
        phase + phase_step,
        center[1] + TIME_STEP * DIFF_HEAT * laplace[1] + LATENT * phase_step,
        center[2] + TIME_STEP * DIFF_ONE * laplace[2] + REJECT_ONE * center[2] * phase_step,
        center[3] + TIME_STEP * DIFF_TWO * laplace[3] + REJECT_TWO * center[3] * phase_step,
    )


def whole_rows(coarse_rows, edges):
    row = lax.broadcasted_iota(jnp.int32, (8, 128), 0) >> 1
    for n, x in enumerate(coarse_rows):
        edges[n, 0:8] = jnp.take_along_axis(x, row, axis=0)
        edges[n, 8:16] = jnp.take_along_axis(x, 4 + row, axis=0)


def ghost_source():
    lane = lanes()
    return jnp.where(lane >= 64, 1, 0) + jnp.where((lane & 63) >= 32, QUARTER, 0)


def ghosts_of(edges, t, f, where_from):
    q = (2 * t * 43691) >> 19
    at = where_from + (2 * t - q * QUARTER + 32 * f)
    return jnp.concatenate([jnp.take_along_axis(edges[q, h : h + 8], at, axis=1) for h in (0, 8)], axis=0)


def middle_kernel(plan, inc, cen, across, slope, alive, edges, outside):
    lane = lanes()
    low = lane < 64
    start = plan[MISC * 64]

    def unpack(a, b, put):
        for f in range(FIELDS):
            x = inc[a, f * 8 : f * 8 + 8]
            y = inc[b, f * 8 : f * 8 + 8]
            put(f, 0, jnp.where(low, x, pltpu.roll(y, 64, 1)))
            put(f, 8, jnp.where(low, pltpu.roll(x, 64, 1), y))

    def inside(t, carry):
        def put(f, row, x):
            cen[t, f, row : row + 8] = x

        unpack(plan[SRC * 64 + 2 + 2 * t], plan[SRC * 64 + 3 + 2 * t], put)
        return carry

    lax.fori_loop(0, TILES, inside, 0, unroll=UU)
    for n, s in enumerate((0, MOST + 2)):

        def put(f, row, x):
            outside[n, f, row : row + 8] = x

        unpack(plan[SRC * 64 + s], plan[SRC * 64 + s + 1], put)

    whole_rows(gather_edges(plan, inc, OWN_L, OWN_R), edges)
    lane = lanes((ROWS, 128))
    where_from = ghost_source()
    count = plan[MISC * 64 + 1]
    slot = lax.broadcasted_iota(jnp.int32, (TILES, 128), 0) * 2 + (lanes((TILES, 128)) >> 6)
    alive[...] = jnp.where(slot < count, 1.0, 0.0)

    def one(t, before, after):
        s = 2 * t
        fl0, fl1 = plan[FINE_L * 64 + s] == 1, plan[FINE_L * 64 + s + 1] == 1
        fr0, fr1 = plan[FINE_R * 64 + s] == 1, plan[FINE_R * 64 + s + 1] == 1
        k = start + s
        ghost_w = ((lane == 0) & jnp.logical_not(fl0)) | ((lane == 64) & jnp.logical_not(fl1))
        ghost_e = ((lane == 63) & jnp.logical_not(fr0)) | ((lane == 127) & jnp.logical_not(fr1))
        border = (
            ((lane == 0) & (k == 0))
            | ((lane == 63) & (k == NBOX - 1))
            | ((lane == 127) & (k + 1 == NBOX - 1))
        )
        for f in range(FIELDS):
            c = cen[t, f]
            w = pltpu.roll(jnp.where(lane == 127, before[f], c), 1, 1)
            e = pltpu.roll(jnp.where(lane == 0, after[f], c), 127, 1)
            g = ghosts_of(edges, t, f, where_from)
            g = jnp.where(border, c, g)
            w = jnp.where(ghost_w, g, w)
            e = jnp.where(ghost_e, g, e)
            across[t, f] = w + e
            if f == 0:
                slope[t] = e - w

    def between(t, carry):
        one(t, cen.at[t - 1], cen.at[t + 1])
        return carry

    one(0, outside.at[0], cen.at[1])
    lax.fori_loop(1, TILES - 1, between, 0, unroll=22)
    one(TILES - 1, cen.at[TILES - 2], outside.at[1])


def step_kernel(cen, across, slope, alive, sibling, from_below, from_above, out, held, edges, sems):
    sub = lax.axis_index("sub")
    lane = lanes((ROWS, 128))
    row = lax.broadcasted_iota(jnp.int32, (ROWS, 128), 0)
    at_bottom = sub == 0
    at_top = sub == lax.axis_size("sub") - 1
    right = (lane & 63) >= 32
    where_from = ghost_source()
    whole_rows([sibling[n] for n in range(4)], edges)

    def one(t, carry):
        live = jnp.broadcast_to(alive[pl.ds(t, 1)], (ROWS, 128)) == 1.0
        center, sides, south, north = [], [], [], []
        for f in range(FIELDS):
            c = cen[t, f]
            below = jnp.where(at_bottom, c[0:1], from_below[t, f : f + 1])
            above = jnp.where(at_top, c[15:16], from_above[t, f : f + 1])
            g = ghosts_of(edges, t, f, where_from)
            g = jnp.where(((lane + 1) & 63) < 2, g, 0.0)
            if f == 0:
                grad_x = 0.5 * (slope[t] + jnp.where(right, g, -g))
            center.append(c)
            sides.append(across[t, f] + g)
            south.append(jnp.where(row == 0, below, pltpu.roll(c, 1, 0)))
            north.append(jnp.where(row == ROWS - 1, above, pltpu.roll(c, ROWS - 1, 0)))
        stepped = advance(center, sides, grad_x * grad_x, south, north)
        at = pl.ds(pl.multiple_of(t * 128, 128), 128)
        for f in range(FIELDS):
            held[f, :, at] = jnp.where(live, stepped[f], 0.0)
        return carry

    copies = []
    for part in range(PARTS):
        each = TILES // PARTS
        lax.fori_loop(part * each, (part + 1) * each, one, 0, unroll=UNROLL)
        columns = pl.ds(part * each * 128, each * 128)
        copies.append(pltpu.make_async_copy(held.at[:, :, columns], out.at[:, :, columns], sems.at[part]))
        copies[-1].start()
    for copy in copies:
        copy.wait()


PARTS = 4
UNROLL = 6
SMEM = pl.BlockSpec(memory_space=pltpu.SMEM)
VMEM = pl.BlockSpec(memory_space=pltpu.VMEM)
HBM = pl.BlockSpec(memory_space=pltpu.HBM)
PARAMS = pltpu.CompilerParams(vmem_limit_bytes=32 * 1024 * 1024)


def f32(*shape):
    return jax.ShapeDtypeStruct(shape, jnp.float32)


def i32(*shape):
    return jax.ShapeDtypeStruct(shape, jnp.int32)


def body(fine_old, coarse, box_pos, old_owner, new_counts):
    outgoing = pl.pallas_call(
        pack_kernel,
        name="pack",
        out_shape=f32(SLABS, MSG_ROWS, 128),
        in_specs=[HBM] * 5,
        out_specs=VMEM,
        scratch_shapes=[
            pltpu.SMEM((NBOX,), jnp.int32),
            pltpu.SMEM((SLABS,), jnp.int32),
            pltpu.SMEM((NBOX,), jnp.int32),
            pltpu.VMEM((FIELDS, ROWS, BOX_DEV * BX), jnp.float32),
            pltpu.VMEM((FIELDS, ROWS // 2, PPD * BX // 2), jnp.float32),
            pltpu.VMEM((BOX_DEV, BOX_ROWS, 128), jnp.float32),
            pltpu.SemaphoreType.DMA((5,)),
        ],
        compiler_params=pltpu.CompilerParams(vmem_limit_bytes=62914560),
    )(old_owner, new_counts, box_pos, fine_old, coarse)
    incoming = lax.all_to_all(outgoing, "slab", 0, 0, tiled=True)
    plan = pl.pallas_call(
        plan_kernel,
        name="plan",
        out_shape=i32(8 * 64),
        in_specs=[SMEM] * 3,
        out_specs=SMEM,
        compiler_params=PARAMS,
    )(old_owner, new_counts, box_pos)
    low_rows, high_rows = pl.pallas_call(
        edge_kernel,
        name="edges",
        out_shape=(f32(TILES, FIELDS, 128), f32(TILES, FIELDS, 128)),
        in_specs=[VMEM, VMEM],
        out_specs=(VMEM, VMEM),
        compiler_params=PARAMS,
    )(plan, incoming)
    sibling = pl.pallas_call(
        sibling_kernel,
        name="sibling",
        out_shape=f32(4, 8, 128),
        in_specs=[VMEM, VMEM],
        out_specs=VMEM,
        compiler_params=PARAMS,
    )(plan, incoming)
    count = lax.axis_size("sub")
    up = [(i, i + 1) for i in range(count - 1)]
    sibling = lax.ppermute(sibling, "slab", [(i, i ^ 1) for i in range(SLABS)])
    from_above = lax.ppermute(low_rows, "sub", [(b, a) for a, b in up])
    from_below = lax.ppermute(high_rows, "sub", up)
    cells = (TILES, FIELDS, ROWS, 128)
    cen, across, slope, alive = pl.pallas_call(
        middle_kernel,
        name="middle",
        out_shape=(f32(*cells), f32(*cells), f32(TILES, ROWS, 128), f32(TILES, 128)),
        in_specs=[SMEM, VMEM],
        out_specs=(VMEM, VMEM, VMEM, VMEM),
        scratch_shapes=[
            pltpu.VMEM((4, ROWS, 128), jnp.float32),
            pltpu.VMEM((2, FIELDS, ROWS, 128), jnp.float32),
        ],
        cost_estimate=pl.CostEstimate(flops=8_000_000, bytes_accessed=8_000_000, transcendentals=0),
        compiler_params=PARAMS,
    )(plan, incoming)
    return pl.pallas_call(
        step_kernel,
        name="step",
        out_shape=f32(FIELDS, ROWS, MOST * BX),
        in_specs=[VMEM] * 7,
        out_specs=HBM,
        scratch_shapes=[
            pltpu.VMEM((FIELDS, ROWS, MOST * BX), jnp.float32),
            pltpu.VMEM((4, ROWS, 128), jnp.float32),
            pltpu.SemaphoreType.DMA((PARTS,)),
        ],
        compiler_params=PARAMS,
    )(cen, across, slope, alive, sibling, from_below, from_above)


def solution(mesh):
    placed = (P(None, "sub", "slab"), P(None, "sub", "slab"), P(), P(), P())
    return jax.shard_map(
        body, mesh=mesh, in_specs=placed, out_specs=P(None, "sub", "slab"), check_vma=False
    )
```
